32 devices in a mesh: dp: 8 (over z, x), seq: 4 (over y, core).
Axes of the slice: x: 2, y: 2, z: 4, core: 2. Of those that a mesh axis runs over, the one named last changes fastest.
Arguments:
- short_tokens: bfloat16 [192, 128, 768], P(('dp', 'seq')), may hold values from -6 to 6
- long_tokens: bfloat16 [8, 512, 768], P('dp', 'seq'), may hold values from -6 to 6
- short_cotangent: bfloat16 [192, 128, 768], P(('dp', 'seq')), may hold values from -6 to 6
- long_cotangent: bfloat16 [8, 512, 768], P('dp', 'seq'), may hold values from -6 to 6
- qkv_weight: bfloat16 [2, 768, 2304], P(None, ('dp', 'seq')), may hold values from -0.21875 to 0.21875
- out_weight: bfloat16 [2, 768, 768], P(None, ('dp', 'seq')), may hold values from -3.5 to 3.5
- up_weight: bfloat16 [2, 768, 3072], P(None, ('dp', 'seq')), may hold values from -0.21875 to 0.21875
- down_weight: bfloat16 [2, 3072, 768], P(None, ('dp', 'seq')), may hold values from -0.109375 to 0.109375
- vectors: bfloat16 [2, 768, 8], P(None, ('dp', 'seq')), may hold values from -1.25 to 1.65, as said below
- up_bias: bfloat16 [2, 3072], P(None, ('dp', 'seq')), may hold values from -1.796875 to 1.796875
- mask_logit: float32 [2, 12, 4, 4], replicated, may hold values from -5 to 5
- short_noise: float32 [2, 192, 12], P(None, ('dp', 'seq')), may hold values from -5 to 5
- gate_noise: float32 [2, 8, 12, 4, 4], P(None, 'dp'), may hold values from -5 to 5
- block_mask: int32 [8, 4, 4], P('dp'), may hold values 0 or 1
- block_order: int32 [8, 4], P('dp'), may hold values from 0 to 3, each once within a row
Outputs:
- short_output: bfloat16 [192, 128, 768], P(('dp', 'seq'))
- long_output: bfloat16 [8, 512, 768], P('dp', 'seq')
- short_grad: bfloat16 [192, 128, 768], P(('dp', 'seq'))
- long_grad: bfloat16 [8, 512, 768], P('dp', 'seq')
- qkv_grad: float32 [2, 768, 2304], P(None, ('dp', 'seq'))
- out_grad: float32 [2, 768, 768], P(None, ('dp', 'seq'))
- up_grad: float32 [2, 768, 3072], P(None, ('dp', 'seq'))
- down_grad: float32 [2, 3072, 768], P(None, ('dp', 'seq'))
- vectors_grad: float32 [2, 768, 8], P(None, ('dp', 'seq'))
- up_bias_grad: float32 [2, 3072], P(None, ('dp', 'seq'))
- mask_logit_grad: float32 [2, 12, 4, 4], replicated
The draws below stay inside these ranges and needn't reach their ends.
Inputs may be any that keep to these rules, and one draw needn't show every extreme that they name: `block_mask`: 1 where true query block i of that split sequence may attend true key block j. `block_order`: each row is a permutation of the 4 block numbers. `vectors`: columns 3 and 6 are gains near one, the others biases near zero.
All inputs are finite; a program needn't handle non-finite values.
Results may differ from the reference program's by a relative error of at most 0.024.
Values may be sent and summed in bfloat16 or wider, within the bound.
No kernel may reach another device: no remote copies, remote signals or barrier semaphores. Data moves between devices by JAX's collectives and lax.ppermute only.
A program may use at most 256 MiB of HBM per device.

```python
import jax
import jax.numpy as jnp
from jax import lax

D = 768
HEADS = 12
HEAD = 64
FF = 3072
BLK = 128
LAYERS = 2
SHORT_DEV = 6
KB = 4
LONG_LEN = 512
SHORTS = 192
LONGS = 8
N_DP = 8
N_SEQ = 4


def draw_vectors(key, part):
    key = jax.random.fold_in(key, 5)
    base = jnp.clip(jax.random.normal(key, (LAYERS, D, 8), jnp.float32), -4.0, 4.0)
    column = jnp.arange(8)
    is_gain = (column == 3) | (column == 6)
    return jnp.where(is_gain[None, None, :], 1.0 + 0.15 * base, 0.3 * base).astype(jnp.bfloat16)


def place_ends(values, rng, smallest, largest):
    longest = values.shape.index(max(values.shape))
    spots = []
    for shift in (0, 1):
        where = [jax.random.randint(jax.random.fold_in(rng, axis), (), 0, length) for axis, length in enumerate(values.shape)]
        where[longest] = (where[longest] + shift) % values.shape[longest]
        spots.append(tuple(where))
    return values.at[spots[0]].set(smallest).at[spots[1]].set(largest)


def levels(stream_key, shape, pieces, least, high):
    loudness = 1.0
    for dim, blocks in pieces:
        heights = jax.random.uniform(jax.random.fold_in(jax.random.fold_in(stream_key, 6), dim), (blocks,), jnp.float32, least / len(pieces), high / len(pieces))
        loudness = loudness * jnp.repeat(jnp.exp(heights), shape[dim] // blocks).reshape((-1,) + (1,) * (len(shape) - 1 - dim))
    return loudness


def scatter_about(rng, shape, scale, most, split=(), kind=jnp.bfloat16):
    values = jax.random.normal(rng, shape, jnp.float32) * scale
    if len(split) > 0:
        values = levels(rng, shape, split, -0.22, 0.18) * values
    return jnp.clip(values, min=-most, max=most).astype(kind)


def setup_inputs(seed: int = 0) -> dict:
    splits = jax.random.split(jax.random.key(seed), 16)
    return {
        "short_tokens": scatter_about(splits[0], (SHORTS, BLK, D), 1.0, 6.0, ((0, 32),)),
        "long_tokens": scatter_about(splits[1], (LONGS, LONG_LEN, D), 1.0, 6.0, ((0, 8), (1, 4))),
        "short_cotangent": scatter_about(splits[2], (SHORTS, BLK, D), 1.0, 6.0, ((0, 32),)),
        "long_cotangent": scatter_about(splits[3], (LONGS, LONG_LEN, D), 1.0, 6.0, ((0, 8), (1, 4))),
        "qkv_weight": scatter_about(splits[4], (LAYERS, D, 3 * D), D ** -0.5, 0.21875, ((1, 32),)),
        "out_weight": scatter_about(splits[5], (LAYERS, D, D), (max(D // 256, 1)) ** -0.5, 3.5, ((1, 32),)),
        "up_weight": scatter_about(splits[6], (LAYERS, D, FF), D ** -0.5, 0.21875, ((1, 32),)),
        "down_weight": scatter_about(splits[7], (LAYERS, FF, D), FF ** -0.5, 0.109375, ((1, 32),)),
        "vectors": draw_vectors(jax.random.fold_in(splits[15], 71), 0),
        "up_bias": scatter_about(splits[9], (LAYERS, FF), 0.3, 1.796875, ((1, 32),)),
        "mask_logit": scatter_about(splits[10], (LAYERS, HEADS, KB, KB), 1.0, 5.0, (), jnp.float32),
        "short_noise": scatter_about(splits[11], (LAYERS, SHORTS, HEADS), 1.0, 5.0, ((1, 32),), jnp.float32),
        "gate_noise": scatter_about(splits[12], (LAYERS, LONGS, HEADS, KB, KB), 1.0, 5.0, ((1, 8),), jnp.float32),
        "block_mask": place_ends((jax.random.randint(splits[13], (LONGS, KB, KB), 0, 3) < 2).astype(jnp.int32), jax.random.fold_in(splits[13], 1), 0, 1),
        "block_order": jax.vmap(lambda own: jax.random.permutation(own, KB))(jax.random.split(splits[14], LONGS)).reshape((LONGS, KB)).astype(jnp.int32),
    }


@jax.custom_vjp
def low(v):
    return lax.optimization_barrier(v.astype(jnp.bfloat16)).astype(jnp.float32)

@jax.custom_vjp
def low_back(v):
    return v

def low_keep(v):
    return (low(v), None)

def low_pass(kept, grad):
    return (grad,)

def back_keep(v):
    return (v, None)

def back_low(kept, grad):
    return (low(grad),)
low.defvjp(low_keep, low_pass)
low_back.defvjp(back_keep, back_low)

def product(spec, left, right):
    return jnp.einsum(spec, left, right, precision=lax.Precision.HIGHEST)

def layer_norm(rows, gain, shift):
    center = rows - lax.optimization_barrier(jnp.mean(rows, axis=-1, keepdims=True))
    spread = lax.optimization_barrier(jnp.mean(center * center, axis=-1, keepdims=True))
    return center * lax.rsqrt(spread + 1e-05) * gain + shift

def project(rows, w_qkv, bias):
    return low(low_back(product('gtd,de->gte', low(rows), w_qkv) + bias))

def attend(qkv, allowed, gating):
    groups, length, triple = qkv.shape
    width = triple // 3
    where_block = jnp.arange(length) // BLK
    query = qkv[..., :width].reshape(groups, length, HEADS, HEAD)
    keys = qkv[..., width:2 * width].reshape(groups, length, HEADS, HEAD)
    values = qkv[..., 2 * width:].reshape(groups, length, HEADS, HEAD)
    scores = low_back(product('gqhe,gkhe->ghqk', query, keys) * 0.125)
    full = allowed[:, where_block][:, :, where_block]
    scores = jnp.where(full[:, None], scores, -1e+30)
    row_max = lax.optimization_barrier(jnp.max(scores, axis=-1, keepdims=True))
    raised = jnp.exp(scores - row_max)
    prob = raised / lax.optimization_barrier(jnp.sum(raised, axis=-1, keepdims=True))
    gate_full = gating[:, :, where_block][:, :, :, where_block]
    weighted = low(prob * gate_full)
    mixed = product('ghqk,gkhe->gqhe', weighted, values).reshape(groups, length, width)
    return low(low_back(mixed))

def finish(rows, mixed, w_out, w_up, w_down, vec, up_b):
    attended = low_back(product('gtd,de->gte', mixed, w_out) + vec[:, 2])
    hidden = layer_norm(rows + attended, vec[:, 3], vec[:, 4])
    upper = low_back(product('gtd,df->gtf', low(hidden), w_up) + up_b)
    active = low(jax.nn.gelu(upper, approximate=False))
    branch = low_back(product('gtf,fd->gtd', active, w_down) + vec[:, 5])
    return layer_norm(hidden + branch, vec[:, 6], vec[:, 7])

def one_layer(short_x, long_x, weights, logit, short_n, long_n, pattern, order):
    w_qkv, w_out, w_up, w_down, vec, up_b = weights
    width = short_x.shape[-1]
    zero = jnp.zeros((width,), jnp.float32)
    bias = jnp.concatenate([vec[:, 0], zero, vec[:, 1]])
    short_qkv = project(short_x, w_qkv, bias)
    long_qkv = project(long_x, w_qkv, bias)
    count = short_x.shape[0]
    short_allowed = jnp.ones((count, 1, 1), dtype=bool)
    short_gate = jax.nn.sigmoid(logit[:, 0, 0][None] + short_n)[:, :, None, None]
    placed = order[0]
    diagonal = jnp.eye(KB, dtype=bool)
    long_allowed = ((pattern[0][placed][:, placed] > 0) | diagonal)[None]
    long_gate = jax.nn.sigmoid(logit[:, placed][:, :, placed] + long_n[0][:, placed][:, :, placed])[None]
    short_mixed = attend(short_qkv, short_allowed, short_gate)
    long_mixed = attend(long_qkv, long_allowed, long_gate)
    return (finish(short_x, short_mixed, w_out, w_up, w_down, vec, up_b), finish(long_x, long_mixed, w_out, w_up, w_down, vec, up_b))

def forward(params, short_x, long_x, short_n, long_n, pattern, order):
    w_qkv, w_out, w_up, w_down, vec, up_b, logit = params
    for layer in range(LAYERS):
        weights = (w_qkv[layer], w_out[layer], w_up[layer], w_down[layer], vec[layer], up_b[layer])
        short_x, long_x = one_layer(short_x, long_x, weights, logit[layer], short_n[layer], long_n[layer], pattern, order)
    return (short_x, long_x)

def reference(short_tokens, long_tokens, short_cotangent, long_cotangent, qkv_weight, out_weight, up_weight, down_weight, vectors, up_bias, mask_logit, short_noise, gate_noise, block_mask, block_order):
    params = (qkv_weight.astype(jnp.float32), out_weight.astype(jnp.float32), up_weight.astype(jnp.float32), down_weight.astype(jnp.float32), vectors.astype(jnp.float32), up_bias.astype(jnp.float32), mask_logit.astype(jnp.float32))
    per_group = N_SEQ * SHORT_DEV
    long_len = BLK * N_SEQ
    short_in = short_tokens.astype(jnp.float32).reshape(N_DP, per_group, BLK, D)
    long_in = long_tokens.astype(jnp.float32).reshape(N_DP, 1, long_len, D)
    short_dy = short_cotangent.astype(jnp.float32).reshape(N_DP, per_group, BLK, D)
    long_dy = long_cotangent.astype(jnp.float32).reshape(N_DP, 1, long_len, D)
    short_n = short_noise.reshape(LAYERS, N_DP, per_group, HEADS).transpose(1, 0, 2, 3)
    long_n = gate_noise.reshape(LAYERS, N_DP, 1, HEADS, KB, KB).transpose(1, 0, 2, 3, 4, 5)
    pattern = block_mask.reshape(N_DP, 1, KB, KB)
    order = block_order.reshape(N_DP, 1, KB)

    def step(totals, item):
        xs, xl, dys, dyl, noise_s, noise_l, pattern_g, order_g = item

        def local_forward(p, short_x, long_x):
            return forward(p, short_x, long_x, noise_s, noise_l, pattern_g, order_g)
        outputs, pull = jax.vjp(local_forward, params, xs, xl)
        param_grads, dxs, dxl = pull((dys, dyl))
        totals = tuple((a + b for a, b in zip(totals, param_grads)))
        return (totals, (outputs[0].astype(jnp.bfloat16), outputs[1].astype(jnp.bfloat16), dxs.astype(jnp.bfloat16), dxl.astype(jnp.bfloat16)))
    start = tuple((jnp.zeros_like(p) for p in params))
    totals, (ys, yl, gs, gl) = lax.scan(step, start, (short_in, long_in, short_dy, long_dy, short_n, long_n, pattern, order))
    short_shape = (N_DP * per_group, BLK, D)
    long_shape = (N_DP, long_len, D)
    return (ys.reshape(short_shape), yl.reshape(long_shape), gs.reshape(short_shape), gl.reshape(long_shape), totals[0], totals[1], totals[2], totals[3], totals[4], totals[5], totals[6])
```

```python
import functools

import jax
import jax.numpy as jnp
from jax import lax
from jax.experimental import pallas as pl
from jax.experimental.pallas import tpu as pltpu
from jax.sharding import PartitionSpec as P

HEADS = 12
HEAD = 64
BLOCK = 128
AXES = ("dp", "seq")
BF16 = jnp.bfloat16
F32 = jnp.float32
VMEM = pl.BlockSpec(memory_space=pltpu.VMEM)
SMEM = pl.BlockSpec(memory_space=pltpu.SMEM)
ANY = pl.BlockSpec(memory_space=pl.ANY)
SMALL = 128
ROOT_HALF = 0.7071067811865476
ROOT_TWO_PI_INV = 0.3989422804014327


def sds(shape, dtype):
    return jax.ShapeDtypeStruct(shape, dtype)


def params(mib=60):
    return pltpu.CompilerParams(vmem_limit_bytes=mib * 2**20)


def cost(us):
    return pl.CostEstimate(flops=0, bytes_accessed=int(us * 3.3e6), transcendentals=0)


def dot(left, right):
    return jnp.dot(left, right, preferred_element_type=F32)


def dot_rt(left, right):
    return lax.dot_general(left, right, (((1,), (1,)), ((), ())), preferred_element_type=F32)


def dot_lt(left, right):
    return lax.dot_general(left, right, (((0,), (0,)), ((), ())), preferred_element_type=F32)


class Plan:
    def __init__(self, mesh, width):
        dp, seq = mesh.shape["dp"], mesh.shape["seq"]
        self.dp, self.seq, self.devices = dp, seq, dp * seq
        depth = dp // 2
        chips = depth * 4
        self.staged = (
            seq == 4
            and dp % 2 == 0
            and depth & (depth - 1) == 0
            and width % chips == 0
            and (width // chips) % 16 == 0
        )
        self.depth, self.chips = depth, chips
        self.block = width // chips if self.staged else 0
        if self.staged:
            self.z_perms = [self.flip(z=step) for step in range(1, depth)]
            self.first = self.flip_by_core((0, 1), (1, 0))
            self.second = self.flip_by_core((1, 0), (0, 1))
            self.cores = self.flip(core=1)

    def flip(self, z=0, x=0, y=0, core=0):
        pairs = []
        for dev in range(self.devices):
            pairs.append((dev, dev ^ (z * 8 + x * 4 + y * 2 + core)))
        return pairs

    def flip_by_core(self, even, odd):
        pairs = []
        for dev in range(self.devices):
            x, y = even if dev % 2 == 0 else odd
            pairs.append((dev, dev ^ (x * 4 + y * 2)))
        return pairs

    def tables(self):
        if not self.staged:
            return None
        me = lax.axis_index("dp") * 4 + lax.axis_index("seq")
        core = me % 2
        chip = me // 2
        slot = jnp.arange(self.chips, dtype=jnp.int32)
        steps, a, b = slot % self.depth, (slot // self.depth) % 2, slot // (2 * self.depth)
        y_first = steps * 4 + b * 2 + a
        x_first = steps * 4 + a * 2 + b
        own = jnp.where(core == 0, y_first, x_first)
        other = jnp.where(core == 0, x_first, y_first)
        away = slot ^ chip
        z, x, y = away // 4, (away // 2) % 2, away % 2
        y_slot = (x * 2 + y) * self.depth + z
        x_slot = (y * 2 + x) * self.depth + z
        own_slot = jnp.where(core == 0, y_slot, x_slot)
        other_slot = jnp.where(core == 0, x_slot, y_slot)
        return jnp.concatenate(
            [own ^ chip, other ^ chip, own_slot, other_slot, jnp.full((8,), core, jnp.int32)]
        ).astype(jnp.int32)


def send(value, pairs):
    return lax.ppermute(value, AXES, pairs)


def after(value, *earlier):
    return lax.optimization_barrier((value, *earlier))[0]


class Gather:
    def __init__(self, plan, halves, core, *earlier):
        self.plan = plan
        mine = lax.dynamic_index_in_dim(halves, core, 0, keepdims=False)
        away = lax.dynamic_index_in_dim(halves, 1 - core, 0, keepdims=False)
        got = send(away, plan.cores)
        base = jnp.where(core == 0, jnp.concatenate([mine, got]), jnp.concatenate([got, mine]))
        self.base = after(base, *earlier)

    def line(self):
        self.along = jnp.stack([self.base] + [send(self.base, pairs) for pairs in self.plan.z_perms])

    def first(self, *earlier):
        self.along = after(self.along, *earlier)
        self.near = jnp.concatenate([self.along, send(self.along, self.plan.first)])

    def second(self, *earlier):
        self.near = after(self.near, *earlier)
        self.far = send(self.near, self.plan.second)

    def finish(self):
        cores = self.plan.cores
        return (self.near, self.far, send(self.near, cores), send(self.far, cores))


class Reduce:
    def __init__(self, plan, own, other):
        self.plan, self.own = plan, own
        self.part = plan.chips // 2
        self.quarter = self.part // 2
        self.pending = send(other, plan.cores)

    def wait(self, *values):
        if isinstance(self.pending, list):
            self.pending = [after(value, *values) for value in self.pending]
        else:
            self.pending = after(self.pending, *values)

    def second(self, *earlier):
        part = self.part
        self.got = self.pending
        away = self.own[part:].astype(F32) + self.got[part:].astype(F32)
        self.operand = after(away.astype(BF16), *earlier) if earlier else away.astype(BF16)
        self.pending = send(self.operand, self.plan.second)

    def first(self):
        part, quarter = self.part, self.quarter
        self.got_b = self.pending
        near = self.own[quarter:part].astype(F32) + self.got[quarter:part].astype(F32)
        near = near + self.got_b[quarter:].astype(F32)
        self.operand = near.astype(BF16)
        self.pending = send(self.operand, self.plan.first)

    def line(self):
        quarter = self.quarter
        line = self.own[:quarter].astype(F32) + self.got[:quarter].astype(F32)
        line = line + self.got_b[:quarter].astype(F32) + self.pending.astype(F32)
        self.operand = low = line.astype(BF16)
        self.total = line[0]
        self.pending = [send(low[step + 1], pairs) for step, pairs in enumerate(self.plan.z_perms)]

    def finish(self):
        total = self.total
        for value in self.pending:
            total = total + value.astype(F32)
        return total


class Butterfly:
    def __init__(self, plan, value):
        self.plan, self.value, self.bit, self.pending = plan, value, 1, None

    def step(self, *earlier):
        if self.pending is not None:
            self.value = self.value + after(self.pending, *earlier)
        self.pending = None
        if self.bit < self.plan.devices:
            pairs = [(dev, dev ^ self.bit) for dev in range(self.plan.devices)]
            self.pending = send(self.value, pairs)
            self.bit *= 2

    def finish(self):
        while self.pending is not None:
            self.step()
        return self.value


def load_blocks(table, pieces, target, sems, start=0):
    copies = []
    if len(pieces) == 1:
        source = pieces[0].at[:, start : start + target.shape[1]]
        copies.append(pltpu.make_async_copy(source, target, sems.at[0]))
    else:
        count, rows, cols = pieces[0].shape
        core = table[4 * 2 * count]
        for place, piece in enumerate(pieces):
            half = core if place < 2 else 1 - core
            lanes = pl.ds(pl.multiple_of(half * cols, 128), cols)
            for index in range(count):
                chip = table[place * count + index]
                copies.append(
                    pltpu.make_async_copy(
                        piece.at[index],
                        target.at[pl.ds(pl.multiple_of(chip * rows, 16), rows), lanes],
                        sems.at[place * count + index],
                    )
                )
    for copy in copies:
        copy.start()
    return copies


def wait_all(copies):
    for copy in copies:
        copy.wait()


def project_kernel(count, half, start, table, rows_short, rows_long, bias, *rest):
    pieces, (out_short, out_query, out_kv, weight, sems) = rest[:count], rest[count:]
    wait_all(load_blocks(table, pieces, weight, sems, start))
    width = out_query.shape[1]
    stride = weight.shape[1] // 2
    tile = 384
    for part in range(2):
        for step in range(half // tile):
            start = part * half + step * tile
            lanes = slice(part * stride + step * tile, part * stride + (step + 1) * tile)
            place = slice(start, start + tile)
            block = weight[:, lanes]
            low = (dot(rows_long[...], block) + bias[:, place]).astype(BF16)
            if start < width:
                out_query[:, place] = low
            else:
                out_kv[:, start - width : start - width + tile] = low
            out_short[:, place] = (dot(rows_short[...], block) + bias[:, place]).astype(BF16)


def project(table, rows_short, rows_long, bias, pieces, half, start):
    short, width = rows_short.shape
    count = short + rows_long.shape[0]
    return pl.pallas_call(
        functools.partial(project_kernel, len(pieces), half, start),
        out_shape=[
            sds((short, 2 * half), BF16),
            sds((count - short, width), BF16),
            sds((count - short, 2 * half - width), BF16),
        ],
        in_specs=[SMEM, VMEM, VMEM, VMEM] + [ANY] * len(pieces),
        out_specs=[VMEM] * 3,
        scratch_shapes=[
            pltpu.VMEM(natural_shape(pieces, 2 * half), BF16),
            pltpu.SemaphoreType.DMA((32,)),
        ],
        compiler_params=params(),
        cost_estimate=cost(10),
        name="project",
    )(table, rows_short, rows_long, bias, *pieces)


def head_masks():
    lane = lax.broadcasted_iota(jnp.int32, (BLOCK, BLOCK), 1)
    low = jnp.where(lane < HEAD, 1.0, 0.0).astype(BF16)
    high = jnp.where(lane < HEAD, 0.0, 1.0).astype(BF16)
    return low, high


def spread(pair, low, high):
    return jnp.concatenate([pair * low, pair * high], axis=0)


def short_forward_kernel(qkv, gate, mixed, raised, inverse):
    low, high = head_masks()
    ones = jnp.concatenate([low, high], axis=0)
    width = mixed.shape[1]
    for pair in range(HEADS // 2):
        lanes = slice(pair * 128, pair * 128 + 128)
        query = qkv[:, lanes] * 0.125
        keys = spread(qkv[:, width + pair * 128 : width + pair * 128 + 128], low, high)
        values = spread(qkv[:, 2 * width + pair * 128 : 2 * width + pair * 128 + 128], low, high)
        scores = dot_rt(query, keys)
        left, right = scores[:, :BLOCK], scores[:, BLOCK:]
        left = jnp.exp(left - jnp.max(left, axis=1, keepdims=True))
        right = jnp.exp(right - jnp.max(right, axis=1, keepdims=True))
        prob = jnp.concatenate([left, right], axis=1).astype(BF16)
        both = dot(prob, jnp.concatenate([values, ones], axis=1))
        inv = 1.0 / both[:, BLOCK:]
        raised[0, pair] = prob
        inverse[:, lanes] = inv
        mixed[:, lanes] = (both[:, :BLOCK] * inv * gate[0, :, lanes]).astype(BF16)


def short_forward(qkv, gate):
    rows = qkv.shape[0]
    width = qkv.shape[1] // 3
    count = rows // BLOCK
    pairs = HEADS // 2
    return pl.pallas_call(
        short_forward_kernel,
        grid=(count,),
        out_shape=[
            sds((rows, width), BF16),
            sds((count, pairs, BLOCK, 2 * BLOCK), BF16),
            sds((rows, width), F32),
        ],
        in_specs=[
            pl.BlockSpec((BLOCK, 3 * width), lambda i: (i, 0)),
            pl.BlockSpec((1, 1, width), lambda i: (i, 0, 0)),
        ],
        out_specs=[
            pl.BlockSpec((BLOCK, width), lambda i: (i, 0)),
            pl.BlockSpec((1, pairs, BLOCK, 2 * BLOCK), lambda i: (i, 0, 0, 0)),
            pl.BlockSpec((BLOCK, width), lambda i: (i, 0)),
        ],
        compiler_params=params(),
        cost_estimate=cost(7),
        name="short_forward",
    )(qkv, gate)


def long_forward_kernel(blocks, opened, queries, gate, *rest):
    sources, (mixed, raised, inverse, parts) = rest[:blocks], rest[blocks:]
    low, high = head_masks()
    ones = jnp.concatenate([low, high], axis=0)
    width = mixed.shape[1]
    for pair in range(HEADS // 2):
        lanes = slice(pair * 128, pair * 128 + 128)
        query = queries[:, lanes] * 0.125
        scores, values = [], []
        for index in range(blocks):
            source = sources[index]
            keys = spread(source[:, lanes], low, high)
            values.append(spread(source[:, width + pair * 128 : width + pair * 128 + 128], low, high))
            score = dot_rt(query, keys)
            scores.append(jnp.where(opened[index] > 0, score, -1e30))
        top = functools.reduce(jnp.maximum, scores)
        top_left = jnp.max(top[:, :BLOCK], axis=1, keepdims=True)
        top_right = jnp.max(top[:, BLOCK:], axis=1, keepdims=True)
        both = []
        for index in range(blocks):
            left = jnp.exp(scores[index][:, :BLOCK] - top_left)
            right = jnp.exp(scores[index][:, BLOCK:] - top_right)
            prob = jnp.concatenate([left, right], axis=1).astype(BF16)
            raised[pair, index] = prob
            both.append(dot(prob, jnp.concatenate([values[index], ones], axis=1)))
        inv = 1.0 / sum(value[:, BLOCK:] for value in both)
        inverse[:, lanes] = inv
        total = 0.0
        for index in range(blocks):
            part = both[index][:, :BLOCK] * inv
            parts[index, :, lanes] = part.astype(BF16)
            total = total + part * gate[index : index + 1, lanes]
        mixed[:, lanes] = total.astype(BF16)


def long_forward(opened, queries, gate, sources):
    rows, width = queries.shape
    blocks = len(sources)
    return pl.pallas_call(
        functools.partial(long_forward_kernel, blocks),
        out_shape=[
            sds((rows, width), BF16),
            sds((HEADS // 2, blocks, BLOCK, 2 * BLOCK), BF16),
            sds((rows, width), F32),
            sds((blocks, rows, width), BF16),
        ],
        in_specs=[SMEM, VMEM, VMEM] + [VMEM] * blocks,
        out_specs=[VMEM] * 4,
        compiler_params=params(),
        cost_estimate=cost(5.3),
        name="long_forward",
    )(opened, queries, gate, *sources)


def norm_rows(rows, gain, shift):
    inverse = 1.0 / rows.shape[1]
    center = rows - jnp.sum(rows, axis=1, keepdims=True) * inverse
    spread_ = jnp.sum(center * center, axis=1, keepdims=True) * inverse
    scale = lax.rsqrt(spread_ + 1e-05)
    unit = center * scale
    return unit, scale, unit * gain + shift


def mlp_forward_kernel(
    counts,
    columns,
    table,
    rows_short,
    rows_long,
    mixed_short,
    mixed_long,
    vec,
    up_bias,
    *rest,
):
    count_a, count_b = counts
    out_cols, up_cols = columns
    pieces_a, pieces_b = rest[:count_a], rest[count_a : count_a + count_b]
    (
        y_short,
        y_long,
        y_low_short,
        y_low_long,
        hid_low,
        unit1,
        scale1,
        unit2,
        scale2,
        act_out,
        slope_out,
        weight_a,
        weight_b,
        hidden,
        act,
        slope,
        sem_a,
        sem_b,
        sem_o,
    ) = rest[count_a + count_b :]
    loads_a, loads_b = load_mlp(table, pieces_a, pieces_b, weight_a, weight_b, sem_a, sem_b)
    short = rows_short.shape[0]
    total = hidden.shape[0]
    wait_all(loads_a)
    spans = [(rows_short, mixed_short, low, low + 384, low) for low in range(0, short, 384)]
    spans.append((rows_long, mixed_long, 0, rows_long.shape[0], short))
    for rows, mixed, low, high, base in spans:
        here = slice(base, base + high - low)
        joined = [dot(mixed[low:high, :], weight_a[:, start : start + count]) for start, count in out_cols]
        summed = rows[low:high, :].astype(F32) + jnp.concatenate(joined, axis=1) + vec[2:3, :]
        unit, scale, hid = norm_rows(summed, vec[3:4, :], vec[4:5, :])
        unit1[here, :] = unit.astype(BF16)
        scale1[here, :] = scale
        hidden[here, :] = hid
        hid_low[here, :] = hid.astype(BF16)
    tile = 512
    base = 0
    for start, count in up_cols:

        @pl.loop(0, count // tile)
        def _(step, start=start, base=base):
            lanes = pl.ds(pl.multiple_of(start + step * tile, 128), tile)
            place = pl.ds(pl.multiple_of(base + step * tile, 128), tile)
            upper = dot(hid_low[...], weight_a[:, lanes]) + up_bias[:, place]
            below = 0.5 + 0.5 * lax.erf(upper * ROOT_HALF)
            act[:, place] = (upper * below).astype(BF16)
            bell = ROOT_TWO_PI_INV * jnp.exp(-0.5 * upper * upper)
            slope[:, place] = (below + upper * bell).astype(BF16)
            index = base // tile + step
            pltpu.make_async_copy(act.at[:, place], act_out.at[:, place], sem_o.at[0, index]).start()
            pltpu.make_async_copy(slope.at[:, place], slope_out.at[:, place], sem_o.at[1, index]).start()

        base += count

    wait_all(loads_b)
    for step in range(hidden.shape[1] // 256):
        lanes = slice(step * 256, step * 256 + 256)
        hidden[:, lanes] = hidden[:, lanes] + dot(act[...], weight_b[:, lanes]) + vec[5:6, lanes]

    def finish(here, there, y_wide, y_low):
        unit, scale, y = norm_rows(hidden[here, :], vec[6:7, :], vec[7:8, :])
        unit2[here, :] = unit.astype(BF16)
        scale2[here, :] = scale
        y_wide[there, :] = y
        y_low[there, :] = y.astype(BF16)

    @pl.loop(0, short // BLOCK)
    def _(step):
        here = pl.ds(pl.multiple_of(step * BLOCK, BLOCK), BLOCK)
        finish(here, here, y_short, y_low_short)

    finish(slice(short, total), slice(0, total - short), y_long, y_low_long)

    @pl.loop(0, base // tile)
    def _(index):
        place = pl.ds(pl.multiple_of(index * tile, 128), tile)
        pltpu.make_async_copy(act.at[:, place], act_out.at[:, place], sem_o.at[0, index]).wait()
        pltpu.make_async_copy(slope.at[:, place], slope_out.at[:, place], sem_o.at[1, index]).wait()


def load_mlp(table, pieces_a, pieces_b, weight_a, weight_b, sem_a, sem_b):
    width = weight_b.shape[1]
    if len(pieces_a) == 1:
        (source,) = pieces_a
        edge = weight_a.shape[1]
        loads_a = [pltpu.make_async_copy(source.at[:, :edge], weight_a, sem_a.at[0])]
        loads_a[0].start()
    else:
        (source,) = pieces_b
        edge = 0
        loads_a = load_blocks(table, pieces_a, weight_a, sem_a)
    loads_b = []
    for group in range(weight_b.shape[0] // width):
        lanes = slice(edge + group * width, edge + (group + 1) * width)
        copy = pltpu.make_async_copy(
            source.at[:, lanes], weight_b.at[group * width : (group + 1) * width, :], sem_b.at[group]
        )
        copy.start()
        loads_b.append(copy)
    return loads_a, loads_b


def mlp_columns(staged, width, inner):
    if not staged:
        return [(0, width)], [(width, inner)]
    half, half_up = width // 2, inner // 2
    stride = half + half_up
    return [(0, half), (stride, half)], [(half, half_up), (stride + half, half_up)]


def natural_shape(pieces, cols):
    if len(pieces) == 1:
        return (pieces[0].shape[0], cols)
    return (2 * pieces[0].shape[0] * pieces[0].shape[1], 2 * pieces[0].shape[2])


def mlp_forward(table, rows_short, rows_long, mixed_short, mixed_long, vec, up_bias, pieces_a, pieces_b):
    rows = rows_short.shape[0] + rows_long.shape[0]
    width = rows_short.shape[1]
    inner = up_bias.shape[1]
    return pl.pallas_call(
        functools.partial(
            mlp_forward_kernel,
            (len(pieces_a), len(pieces_b)),
            mlp_columns(len(pieces_a) > 1, width, inner),
        ),
        out_shape=[
            sds(rows_short.shape, F32),
            sds(rows_long.shape, F32),
            sds(rows_short.shape, BF16),
            sds(rows_long.shape, BF16),
            sds((rows, width), BF16),
            sds((rows, width), BF16),
            sds((rows, 1), F32),
            sds((rows, width), BF16),
            sds((rows, 1), F32),
            sds((rows, inner), BF16),
            sds((rows, inner), BF16),
        ],
        in_specs=[SMEM] + [VMEM] * 6 + [ANY] * (len(pieces_a) + len(pieces_b)),
        out_specs=[VMEM] * 9 + [ANY, ANY],
        scratch_shapes=[
            pltpu.VMEM((width, width + inner), BF16),
            pltpu.VMEM((inner, width), BF16),
            pltpu.VMEM((rows, width), F32),
            pltpu.VMEM((rows, inner), BF16),
            pltpu.VMEM((rows, inner), BF16),
            pltpu.SemaphoreType.DMA((32,)),
            pltpu.SemaphoreType.DMA((32,)),
            pltpu.SemaphoreType.DMA((2, inner // 512)),
        ],
        compiler_params=params(),
        cost_estimate=cost(28),
        name="mlp_forward",
    )(table, rows_short, rows_long, mixed_short, mixed_long, vec, up_bias, *pieces_a, *pieces_b)


def norm_back(grad, unit, scale, gain):
    inverse = 1.0 / grad.shape[1]
    pulled = grad * gain
    mean = jnp.sum(pulled, axis=1, keepdims=True) * inverse
    along = jnp.sum(pulled * unit, axis=1, keepdims=True) * inverse
    return scale * (pulled - mean - unit * along)


def mlp_backward_kernel(counts, columns, table, grad_short, grad_long, unit2, scale2, unit1, scale1, vec, slope_in, *rest):
    count_a, count_b = counts
    out_cols, up_cols = columns
    pieces_a, pieces_b = rest[:count_a], rest[count_a : count_a + count_b]
    (
        d_first,
        d_out,
        d_att,
        d_mixed_short,
        d_mixed_long,
        sums,
        sums_up,
        d_up_out,
        weight_a,
        weight_b,
        second,
        slope,
        d_up,
        sem_a,
        sem_b,
        sem_o,
    ) = rest[count_a + count_b :]
    total, width = second.shape
    slope_load = pltpu.make_async_copy(slope_in, slope, sem_o.at[1, 0])
    slope_load.start()
    loads_a, loads_b = load_mlp(table, pieces_a, pieces_b, weight_a, weight_b, sem_a, sem_b)
    sums[...] = jnp.zeros_like(sums)

    def begin(here, grad):
        dy = grad.astype(F32)
        unit = unit2[here, :].astype(F32)
        dr = norm_back(dy, unit, scale2[here, :], vec[6:7, :])
        second[here, :] = dr
        low = dr.astype(BF16)
        d_out[here, :] = low
        sums[5:6, :] += jnp.sum(low.astype(F32), axis=0, keepdims=True)
        sums[6:7, :] += jnp.sum(dy * unit, axis=0, keepdims=True)
        sums[7:8, :] += jnp.sum(dy, axis=0, keepdims=True)

    short = grad_short.shape[0]

    @pl.loop(0, short // BLOCK)
    def _(step):
        here = pl.ds(pl.multiple_of(step * BLOCK, BLOCK), BLOCK)
        begin(here, grad_short[here, :])

    begin(slice(short, total), grad_long[...])
    wait_all(loads_b)
    slope_load.wait()
    tile = 512
    steps = slope.shape[1] // tile

    @pl.loop(0, steps)
    def _(step):
        place = pl.ds(pl.multiple_of(step * tile, 128), tile)
        low = (dot_rt(d_out[...], weight_b[place, :]) * slope[:, place].astype(F32)).astype(BF16)
        d_up[:, place] = low
        sums_up[:, place] = jnp.sum(low.astype(F32), axis=0, keepdims=True)
        pltpu.make_async_copy(d_up.at[:, place], d_up_out.at[:, place], sem_o.at[0, step]).start()

    wait_all(loads_a)
    for step in range(width // 256):
        lanes = slice(step * 256, step * 256 + 256)
        full = second[:, lanes]
        base = 0
        for start, count in up_cols:
            full = full + dot_rt(d_up[:, base : base + count], weight_a[lanes, start : start + count])
            base += count
        second[:, lanes] = full

    @pl.loop(0, total // BLOCK)
    def _(step):
        here = pl.ds(pl.multiple_of(step * BLOCK, BLOCK), BLOCK)
        dh = second[here, :]
        unit = unit1[here, :].astype(F32)
        dr = norm_back(dh, unit, scale1[here, :], vec[3:4, :])
        d_first[here, :] = dr
        low = dr.astype(BF16)
        d_att[here, :] = low
        sums[2:3, :] += jnp.sum(low.astype(F32), axis=0, keepdims=True)
        sums[3:4, :] += jnp.sum(dh * unit, axis=0, keepdims=True)
        sums[4:5, :] += jnp.sum(dh, axis=0, keepdims=True)

    for step in range(width // 256):
        lanes = slice(step * 256, step * 256 + 256)
        full = 0.0
        base = 0
        for start, count in out_cols:
            full = full + dot_rt(d_att[:, base : base + count], weight_a[lanes, start : start + count])
            base += count
        d_mixed_short[:, lanes] = full[:short].astype(BF16)
        d_mixed_long[:, lanes] = full[short:].astype(BF16)

    @pl.loop(0, steps)
    def _(step):
        place = pl.ds(pl.multiple_of(step * tile, 128), tile)
        pltpu.make_async_copy(d_up.at[:, place], d_up_out.at[:, place], sem_o.at[0, step]).wait()


def mlp_backward(table, grad, unit2, scale2, unit1, scale1, vec, slope, pieces_a, pieces_b):
    rows, width = unit2.shape
    short = grad[0].shape[0]
    inner = slope.shape[1]
    return pl.pallas_call(
        functools.partial(
            mlp_backward_kernel,
            (len(pieces_a), len(pieces_b)),
            mlp_columns(len(pieces_a) > 1, width, inner),
        ),
        out_shape=[
            sds((rows, width), F32),
            sds((rows, width), BF16),
            sds((rows, width), BF16),
            sds((short, width), BF16),
            sds((rows - short, width), BF16),
            sds((8, width), F32),
            sds((1, inner), F32),
            sds((rows, inner), BF16),
        ],
        in_specs=[SMEM] + [VMEM] * 7 + [ANY] * (1 + len(pieces_a) + len(pieces_b)),
        out_specs=[VMEM] * 7 + [ANY],
        scratch_shapes=[
            pltpu.VMEM((width, width + inner), BF16),
            pltpu.VMEM((inner, width), BF16),
            pltpu.VMEM((rows, width), F32),
            pltpu.VMEM((rows, inner), BF16),
            pltpu.VMEM((rows, inner), BF16),
            pltpu.SemaphoreType.DMA((32,)),
            pltpu.SemaphoreType.DMA((32,)),
            pltpu.SemaphoreType.DMA((2, inner // 512)),
        ],
        compiler_params=params(),
        cost_estimate=cost(28),
        name="mlp_backward",
    )(table, *grad, unit2, scale2, unit1, scale1, vec, slope, *pieces_a, *pieces_b)


def weight_grads_kernel(block, table, act_in, d_out, hid_low, d_up_in, mixed_short, mixed_long, d_att, own, other, act, d_up, mixed, buffer, sem_i, sem_o):
    chips = buffer.shape[1]
    inner = act.shape[1]
    width = d_out.shape[1]
    half_up, half = inner // 2, width // 2
    groups = inner // width
    tile = 512
    loads = []
    for step in range(inner // width):
        place = slice(step * width, step * width + width)
        loads.append(pltpu.make_async_copy(act_in.at[:, place], act.at[:, place], sem_i.at[0, step]))
        loads[-1].start()
    ups = []
    for step in range(inner // tile):
        place = slice(step * tile, step * tile + tile)
        ups.append(pltpu.make_async_copy(d_up_in.at[:, place], d_up.at[:, place], sem_i.at[1, step]))
        ups[-1].start()
    short = mixed_short.shape[0]
    mixed[:short, :] = mixed_short[...]
    mixed[short:, :] = mixed_long[...]
    core = table[4 * chips]

    def slot_of(far, chip):
        return table[2 * chips + far * chips + chip]

    outs = []
    for step in range(groups):
        loads[step].wait()
        result = dot_lt(act[:, step * width : (step + 1) * width], d_out[...]).astype(BF16)
        for part in range(2):
            far = jnp.bitwise_xor(core, part)
            for chip in range(chips):
                buffer[far, slot_of(far, chip), :, step * half : (step + 1) * half] = result[
                    chip * block : (chip + 1) * block, part * half : (part + 1) * half
                ]

    def flush(lanes, index):
        for far, target in enumerate((own, other)):
            copy = pltpu.make_async_copy(buffer.at[far, :, :, lanes], target.at[:, :, lanes], sem_o.at[far, index])
            copy.start()
            outs.append(copy)

    flush(slice(0, groups * half), 0)
    base = groups * half
    for step in range(inner // tile):
        ups[step].wait()
        result = dot_lt(hid_low[...], d_up[:, step * tile : (step + 1) * tile]).astype(BF16)
        part, place = divmod(step * tile, half_up)
        far = jnp.bitwise_xor(core, part)
        for chip in range(chips):
            buffer[far, slot_of(far, chip), :, base + place : base + place + tile] = result[
                chip * block : (chip + 1) * block, :
            ]
    flush(slice(base, base + half_up), 1)
    base += half_up
    result = dot_lt(mixed[...], d_att[...]).astype(BF16)
    for part in range(2):
        far = jnp.bitwise_xor(core, part)
        for chip in range(chips):
            buffer[far, slot_of(far, chip), :, base : base + half] = result[
                chip * block : (chip + 1) * block, part * half : (part + 1) * half
            ]
    flush(slice(base, base + half), 2)
    wait_all(outs)


def weight_grads(table, chips, act, d_out, hid_low, d_up, mixed_short, mixed_long, d_att):
    rows, inner = act.shape
    width = d_out.shape[1]
    block = width // chips
    cols = (inner * width // (block * chips) + inner + width) // 2
    return pl.pallas_call(
        functools.partial(weight_grads_kernel, block),
        out_shape=[sds((chips, block, cols), BF16)] * 2,
        in_specs=[SMEM, ANY, VMEM, VMEM, ANY, VMEM, VMEM, VMEM],
        out_specs=[ANY, ANY],
        scratch_shapes=[
            pltpu.VMEM((rows, inner), BF16),
            pltpu.VMEM((rows, inner), BF16),
            pltpu.VMEM((rows, width), BF16),
            pltpu.VMEM((2, chips, block, cols), BF16),
            pltpu.SemaphoreType.DMA((2, 8)),
            pltpu.SemaphoreType.DMA((2, 3)),
        ],
        compiler_params=params(),
        cost_estimate=cost(20),
        name="weight_grads",
    )(table, act, d_out, hid_low, d_up, mixed_short, mixed_long, d_att)


def packed_grads_kernel(act_in, d_out, hid_low, d_up_in, mixed_short, mixed_long, d_att, out, act, d_up, mixed, buffer, sem_i, sem_o):
    inner = act.shape[1]
    width = d_out.shape[1]
    tile = 512
    loads, ups, outs = [], [], []
    for step in range(inner // width):
        place = slice(step * width, step * width + width)
        loads.append(pltpu.make_async_copy(act_in.at[:, place], act.at[:, place], sem_i.at[0, step]))
        loads[-1].start()
    for step in range(inner // tile):
        place = slice(step * tile, step * tile + tile)
        ups.append(pltpu.make_async_copy(d_up_in.at[:, place], d_up.at[:, place], sem_i.at[1, step]))
        ups[-1].start()
    short = mixed_short.shape[0]
    mixed[:short, :] = mixed_short[...]
    mixed[short:, :] = mixed_long[...]

    def flush(start, stop):
        index = len(outs)
        copy = pltpu.make_async_copy(buffer.at[:, start:stop], out.at[:, start:stop], sem_o.at[index])
        copy.start()
        outs.append(copy)

    for step in range(inner // width):
        loads[step].wait()
        place = slice(step * width, step * width + width)
        buffer[:, place] = dot_lt(act[:, place], d_out[...]).astype(BF16)
    flush(0, inner)
    for step in range(inner // tile):
        ups[step].wait()
        place = slice(step * tile, step * tile + tile)
        buffer[:, inner + step * tile : inner + (step + 1) * tile] = dot_lt(hid_low[...], d_up[:, place]).astype(BF16)
    flush(inner, 2 * inner)
    buffer[:, 2 * inner :] = dot_lt(mixed[...], d_att[...]).astype(BF16)
    flush(2 * inner, 2 * inner + width)
    wait_all(outs)


def packed_grads(act, d_out, hid_low, d_up, mixed_short, mixed_long, d_att):
    rows, inner = act.shape
    width = d_out.shape[1]
    return pl.pallas_call(
        packed_grads_kernel,
        out_shape=sds((width, 2 * inner + width), BF16),
        in_specs=[ANY, VMEM, VMEM, ANY, VMEM, VMEM, VMEM],
        out_specs=ANY,
        scratch_shapes=[
            pltpu.VMEM((rows, inner), BF16),
            pltpu.VMEM((rows, inner), BF16),
            pltpu.VMEM((rows, width), BF16),
            pltpu.VMEM((width, 2 * inner + width), BF16),
            pltpu.SemaphoreType.DMA((2, 8)),
            pltpu.SemaphoreType.DMA((3,)),
        ],
        compiler_params=params(),
        cost_estimate=cost(20),
        name="packed_grads",
    )(act, d_out, hid_low, d_up, mixed_short, mixed_long, d_att)


def short_backward_kernel(qkv, mixed, d_mixed, raised, inverse, gate, d_qkv, gate_sum):
    low, high = head_masks()
    ones = jnp.concatenate([low, high], axis=0)
    width = mixed.shape[1]
    for pair in range(HEADS // 2):
        lanes = slice(pair * 128, pair * 128 + 128)
        query = qkv[:, lanes] * 0.125
        keys = spread(qkv[:, width + pair * 128 : width + pair * 128 + 128], low, high)
        values = spread(qkv[:, 2 * width + pair * 128 : 2 * width + pair * 128 + 128], low, high)
        grad = d_mixed[:, lanes].astype(F32)
        out = mixed[:, lanes].astype(F32)
        scaled = grad * inverse[:, lanes]
        gate_sum[0, :, lanes] = jnp.sum(grad * out, axis=0, keepdims=True)
        pulled = (scaled * gate[0, :, lanes]).astype(BF16)
        inner = (scaled * out).astype(BF16)
        prob = raised[0, pair]
        bent = dot_rt(jnp.concatenate([pulled, inner], axis=1), jnp.concatenate([values, -ones], axis=1))
        score = (prob.astype(F32) * bent).astype(BF16)
        d_qkv[:, lanes] = (dot(score, keys) * 0.125).astype(BF16)
        turned = dot_lt(query, score)
        turned = jnp.concatenate([turned[:HEAD, :BLOCK], turned[HEAD:, BLOCK:]], axis=0)
        d_qkv[:, width + pair * 128 : width + pair * 128 + 128] = turned.T.astype(BF16)
        turned = dot_lt(pulled, prob)
        turned = jnp.concatenate([turned[:HEAD, :BLOCK], turned[HEAD:, BLOCK:]], axis=0)
        d_qkv[:, 2 * width + pair * 128 : 2 * width + pair * 128 + 128] = turned.T.astype(BF16)


def short_backward(qkv, mixed, d_mixed, raised, inverse, gate):
    rows, width = mixed.shape
    count = rows // BLOCK
    pairs = HEADS // 2
    narrow = pl.BlockSpec((BLOCK, width), lambda i: (i, 0))
    wide = pl.BlockSpec((BLOCK, 3 * width), lambda i: (i, 0))
    vector = pl.BlockSpec((1, 1, width), lambda i: (i, 0, 0))
    return pl.pallas_call(
        short_backward_kernel,
        grid=(count,),
        out_shape=[sds((rows, 3 * width), BF16), sds((count, 1, width), F32)],
        in_specs=[
            wide,
            narrow,
            narrow,
            pl.BlockSpec((1, pairs, BLOCK, 2 * BLOCK), lambda i: (i, 0, 0, 0)),
            narrow,
            vector,
        ],
        out_specs=[wide, vector],
        compiler_params=params(),
        cost_estimate=cost(11.6),
        name="short_backward",
    )(qkv, mixed, d_mixed, raised, inverse, gate)


def long_backward_kernel(blocks, queries, mixed, d_mixed, raised, inverse, parts, gate, *rest):
    sources, (d_query, d_own, d_near, d_core, gate_sum) = rest[:blocks], rest[blocks:]
    low, high = head_masks()
    ones = jnp.concatenate([low, high], axis=0)
    width = mixed.shape[1]
    for pair in range(HEADS // 2):
        lanes = slice(pair * 128, pair * 128 + 128)
        query = queries[:, lanes] * 0.125
        grad = d_mixed[:, lanes].astype(F32)
        out = mixed[:, lanes].astype(F32)
        scaled = grad * inverse[:, lanes]
        inner = (scaled * out).astype(BF16)
        total = 0.0
        for index in range(blocks):
            source = sources[index]
            keys = spread(source[:, lanes], low, high)
            values = spread(source[:, width + pair * 128 : width + pair * 128 + 128], low, high)
            strength = gate[index : index + 1, lanes]
            pulled = (scaled * strength).astype(BF16)
            prob = raised[pair, index]
            bent = dot_rt(jnp.concatenate([pulled, inner], axis=1), jnp.concatenate([values, -ones], axis=1))
            score = (prob.astype(F32) * bent).astype(BF16)
            total = total + dot(score, keys)
            gate_sum[index : index + 1, lanes] = strength * jnp.sum(
                grad * parts[index, :, lanes].astype(F32), axis=0, keepdims=True
            )
            target = (d_own, d_core.at[0], d_near, d_core.at[1])[index]
            turned = dot_lt(query, score)
            turned = jnp.concatenate([turned[:HEAD, :BLOCK], turned[HEAD:, BLOCK:]], axis=0)
            target[:, lanes] = turned.T.astype(BF16)
            turned = dot_lt(pulled, prob)
            turned = jnp.concatenate([turned[:HEAD, :BLOCK], turned[HEAD:, BLOCK:]], axis=0)
            target[:, width + pair * 128 : width + pair * 128 + 128] = turned.T.astype(BF16)
        d_query[:, lanes] = (total * 0.125).astype(BF16)


def long_backward(queries, mixed, d_mixed, raised, inverse, parts, gate, sources):
    rows, width = mixed.shape
    blocks = len(sources)
    return pl.pallas_call(
        functools.partial(long_backward_kernel, blocks),
        out_shape=[
            sds((rows, width), BF16),
            sds((rows, 2 * width), BF16),
            sds((rows, 2 * width), BF16),
            sds((2, rows, 2 * width), BF16),
            sds((blocks, width), F32),
        ],
        in_specs=[VMEM] * (7 + blocks),
        out_specs=[VMEM] * 5,
        compiler_params=params(),
        cost_estimate=cost(8.7),
        name="long_backward",
    )(queries, mixed, d_mixed, raised, inverse, parts, gate, *sources)


def qkv_grads_kernel(block, table, rows_short, rows_long, d_short, d_query, d_kv, own, other, columns, rows, grad, buffer, sems):
    chips = buffer.shape[1]
    short, width = rows_short.shape
    half = grad.shape[1] // 2
    rows[:short, :] = rows_short[...]
    rows[short:, :] = rows_long[...]
    grad[:short, :] = d_short[...]
    grad[short:, :width] = d_query[...]
    grad[short:, width:] = d_kv[...]
    core = table[4 * chips]
    tile = 384
    copies = []
    for part in range(2):
        far = jnp.bitwise_xor(core, part)
        for step in range(half // tile):
            lanes = slice(part * half + step * tile, part * half + (step + 1) * tile)
            block_grad = grad[:, lanes]
            columns[:, lanes] = jnp.sum(block_grad.astype(F32), axis=0, keepdims=True)
            result = dot_lt(rows[...], block_grad).astype(BF16)
            for chip in range(chips):
                slot = table[2 * chips + far * chips + chip]
                buffer[far, slot, :, step * tile : (step + 1) * tile] = result[chip * block : (chip + 1) * block, :]
    for far, target in enumerate((other, own)):
        copy = pltpu.make_async_copy(buffer.at[1 - far], target, sems.at[far])
        copy.start()
        copies.append(copy)
    wait_all(copies)


def qkv_grads(table, chips, rows_short, rows_long, d_short, d_query, d_kv):
    short, width = rows_short.shape
    rows = short + rows_long.shape[0]
    block = width // chips
    half = 3 * width // 2
    return pl.pallas_call(
        functools.partial(qkv_grads_kernel, block),
        out_shape=[sds((chips, block, half), BF16)] * 2 + [sds((1, 3 * width), F32)],
        in_specs=[SMEM] + [VMEM] * 5,
        out_specs=[ANY, ANY, VMEM],
        scratch_shapes=[
            pltpu.VMEM((rows, width), BF16),
            pltpu.VMEM((rows, 3 * width), BF16),
            pltpu.VMEM((2, chips, block, half), BF16),
            pltpu.SemaphoreType.DMA((2,)),
        ],
        compiler_params=params(),
        cost_estimate=cost(10.3),
        name="qkv_grads",
    )(table, rows_short, rows_long, d_short, d_query, d_kv)


def input_grad_kernel(count, half, start, table, d_short, d_query, d_kv, d_first, *rest):
    pieces, (out_short, out_long, weight, grad, sems) = rest[:count], rest[count:]
    loads = load_blocks(table, pieces, weight, sems, start)
    short = d_short.shape[0]
    width = out_short.shape[1]
    grad[:short, :] = d_short[...]
    grad[short:, :width] = d_query[...]
    grad[short:, width:] = d_kv[...]
    wait_all(loads)
    stride = weight.shape[1] // 2
    for step in range(width // 256):
        lanes = slice(step * 256, step * 256 + 256)
        total = dot_rt(grad[:, :half], weight[lanes, :half])
        total = total + dot_rt(grad[:, half:], weight[lanes, stride : stride + half])
        total = (total + d_first[:, lanes]).astype(out_short.dtype)
        out_short[:, lanes] = total[:short]
        out_long[:, lanes] = total[short:]


def input_grad(table, d_short, d_query, d_kv, d_first, pieces, half, start, dtype):
    rows, width = d_first.shape
    short = d_short.shape[0]
    return pl.pallas_call(
        functools.partial(input_grad_kernel, len(pieces), half, start),
        out_shape=[sds((short, width), dtype), sds((rows - short, width), dtype)],
        in_specs=[SMEM] + [VMEM] * 4 + [ANY] * len(pieces),
        out_specs=[VMEM] * 2,
        scratch_shapes=[
            pltpu.VMEM(natural_shape(pieces, 2 * half), BF16),
            pltpu.VMEM((rows, 2 * half), BF16),
            pltpu.SemaphoreType.DMA((32,)),
        ],
        compiler_params=params(),
        cost_estimate=cost(10.6),
        name="input_grad",
    )(table, d_short, d_query, d_kv, d_first, *pieces)


def halves_of(array):
    half = array.shape[1] // 2
    return array[:, :half], array[:, half:]


def on_device(
    plan,
    short_tokens,
    long_tokens,
    short_cotangent,
    long_cotangent,
    qkv_weight,
    out_weight,
    up_weight,
    down_weight,
    vectors,
    up_bias,
    mask_logit,
    short_noise,
    gate_noise,
    block_mask,
    block_order,
):
    shorts, block_rows, width = short_tokens.shape
    blocks = lax.axis_size("seq")
    place = lax.axis_index("seq")
    device = lax.axis_index("dp") * plan.seq + place
    layers = qkv_weight.shape[0]
    inner = up_weight.shape[2]
    own_rows = qkv_weight.shape[1]
    short_rows = shorts * block_rows
    half_qkv, half = 3 * width // 2, width // 2
    half_up = inner // 2
    core = place % 2
    table = plan.tables()
    chips = plan.chips if plan.staged else 16
    if table is None:
        natural = jnp.arange(chips, dtype=jnp.int32)
        table = jnp.concatenate([natural] * 4 + [jnp.zeros((8,), jnp.int32)])

    weights = []
    per_row = inner // width

    def whole(array):
        return lax.all_gather(array, AXES, axis=0, tiled=True)

    small = [
        jnp.concatenate(
            [
                vectors[layer],
                up_bias[layer].reshape(per_row, own_rows).T,
                jnp.zeros((own_rows, SMALL - 8 - per_row), BF16),
            ],
            axis=1,
        )
        for layer in range(layers)
    ]

    def up_of(layer):
        up = up_weight[layer].reshape(own_rows, plan.devices, per_row, own_rows)
        return up.transpose(0, 2, 1, 3).reshape(own_rows, inner)

    def down_of(layer):
        down = down_weight[layer].reshape(per_row, own_rows, width).transpose(1, 0, 2)
        return down.reshape(own_rows, inner)

    def packed(layer):
        return [out_weight[layer], up_of(layer), down_of(layer)]

    def with_next(layer):
        return [qkv_weight[layer + 1]] if layer + 1 < layers else []

    first = jnp.concatenate(packed(0) + [qkv_weight[0]] + with_next(0) + [jnp.concatenate(small, axis=1)], axis=1)
    weights = [whole(first)]
    for layer in range(1, layers):
        rows = jnp.concatenate(packed(layer) + with_next(layer), axis=1)
        weights.append(whole(after(rows, weights[-1])))
    mlp_cols = 2 * inner + width
    tail = weights[0][:, weights[0].shape[1] - layers * SMALL :].astype(F32)
    ordered = tail.reshape(width, layers, SMALL).transpose(1, 2, 0)

    def qkv_of(layer):
        if layer == 0:
            return (weights[0],), mlp_cols
        return (weights[layer - 1],), mlp_cols + (3 * width if layer == 1 else 0)

    vecs = [ordered[layer, :8] for layer in range(layers)]
    up_biases = []
    for layer in range(layers):
        up_biases.append(ordered[layer, 8 : 8 + per_row].reshape(1, inner))

    block_ids = jnp.arange(blocks, dtype=jnp.int32)
    near_ids = block_ids ^ place
    placed_ids = block_order[0]
    own_block = jnp.sum(jnp.where(block_ids == place, placed_ids, 0))
    near_int = (near_ids[:, None] == block_ids[None, :]).astype(jnp.int32)
    near_true = jnp.sum(near_int * placed_ids[None, :], axis=1)
    own_hot = (block_ids == own_block).astype(F32)
    near_hot_int = (near_true[:, None] == block_ids[None, :]).astype(jnp.int32)
    near_hot = near_hot_int.astype(F32)
    mask_row = jnp.sum(block_mask[0] * (block_ids == own_block).astype(jnp.int32)[:, None], axis=0)
    opened = jnp.maximum(
        jnp.sum(near_hot_int * mask_row[None, :], axis=1), (block_ids == 0).astype(jnp.int32)
    )
    first_hot = (block_ids == 0).astype(F32)
    corner = first_hot[:, None] * first_hot[None, :]
    highest = lax.Precision.HIGHEST
    logit_near = jnp.einsum(
        "lhij,i,sj->lsh", mask_logit + gate_noise[:, 0], own_hot, near_hot, precision=highest
    )
    gate_long = jax.nn.sigmoid(logit_near)
    gate_short = jax.nn.sigmoid(mask_logit[:, None, :, 0, 0] + short_noise)
    lanes_long = jnp.repeat(gate_long, HEAD, axis=2)
    lanes_short = jnp.repeat(gate_short, HEAD, axis=2)[:, :, None, :]

    def swap_core(value):
        return lax.ppermute(value, "seq", [(i, i ^ 1) for i in range(blocks)])

    def swap_pair(value):
        return lax.ppermute(value, "seq", [(i, i ^ 2) for i in range(blocks)])

    rows_low = (short_tokens.reshape(short_rows, width), long_tokens[0])
    rows_wide = rows_low
    saved = []
    for layer in range(layers):
        w_qkv, start = qkv_of(layer)
        vec = vecs[layer]
        bias = jnp.concatenate([vec[0:1], jnp.zeros((1, width), F32), vec[1:2]], axis=1)
        qkv_short, query_long, kv = project(table, *rows_low, bias, w_qkv, half_qkv, start)
        kv_core = swap_core(kv)
        kv_pair = swap_pair(kv)
        mixed_short, raised_short, inverse_short = short_forward(qkv_short, lanes_short[layer])
        kv_pair = after(kv_pair, mixed_short)
        sources = (kv, kv_core, kv_pair, swap_core(kv_pair))
        mixed_long, raised_long, inverse_long, parts = long_forward(opened, query_long, lanes_long[layer], sources)
        w_mid, w_down = (weights[layer],), ()
        *y, hid_low, unit1, scale1, unit2, scale2, act, slope = mlp_forward(
            table, *rows_wide, mixed_short, mixed_long, vec, up_biases[layer], w_mid, w_down
        )
        saved.append(
            (
                rows_low,
                qkv_short,
                query_long,
                sources,
                mixed_short,
                raised_short,
                inverse_short,
                mixed_long,
                raised_long,
                inverse_long,
                parts,
                hid_low,
                unit1,
                scale1,
                unit2,
                scale2,
                act,
                slope,
            )
        )
        rows_low, rows_wide = y[2:], y[:2]
    outputs = rows_low

    grad = (short_cotangent.reshape(short_rows, width), long_cotangent[0])
    kept = []
    terms = []
    upper = None

    def scattered(array):
        return lax.psum_scatter(array, AXES, scatter_dimension=0, tiled=True)

    for layer in reversed(range(layers)):
        w_qkv, start = qkv_of(layer)
        w_mid, w_down = (weights[layer],), ()
        (
            rows_low,
            qkv_short,
            query_long,
            sources,
            mixed_short,
            raised_short,
            inverse_short,
            mixed_long,
            raised_long,
            inverse_long,
            parts,
            hid_low,
            unit1,
            scale1,
            unit2,
            scale2,
            act,
            slope,
        ) = saved[layer]
        d_first, d_out, d_att, d_mixed_short, d_mixed_long, sums, sums_up, d_up = mlp_backward(
            table, grad, unit2, scale2, unit1, scale1, vecs[layer], slope, w_mid, w_down
        )
        last = layer == 0
        staging = plan.staged
        if staging:
            if upper is not None:
                big_upper, qkv_upper = upper
                big_upper.wait(d_att)
                qkv_upper.wait(d_att)
                qkv_upper.first()
                d_out = after(d_out, qkv_upper.operand, *big_upper.pending)
            big = weight_grads(table, chips, act, d_out, hid_low, d_up, mixed_short, mixed_long, d_att)
            big_sum = Reduce(plan, *big)
            d_mixed_long = after(d_mixed_long, *big)
        else:
            big_sum = scattered(packed_grads(act, d_out, hid_low, d_up, mixed_short, mixed_long, d_att))
        d_query, d_own, d_near, d_core, gate_sum_long = long_backward(
            query_long, mixed_long, d_mixed_long, raised_long, inverse_long, parts, lanes_long[layer], sources
        )
        far = swap_core(d_core)
        away = (d_near.astype(F32) + far[1].astype(F32)).astype(BF16)
        passed = swap_pair(away)
        if staging:
            big_sum.wait(d_query, away)
            big_sum.second(passed)
            d_mixed_short = after(d_mixed_short, big_sum.operand)
            if upper is not None:
                qkv_upper.wait(d_query)
                qkv_upper.line()
                d_mixed_short = after(d_mixed_short, qkv_upper.operand)
        d_short, gate_sum_short = short_backward(
            qkv_short, mixed_short, d_mixed_short, raised_short, inverse_short, lanes_short[layer]
        )
        d_kv = (d_own.astype(F32) + far[0].astype(F32) + passed.astype(F32)).astype(BF16)
        qkv_own, qkv_other, columns = qkv_grads(table, chips, *rows_low, d_short, d_query, d_kv)
        d_first = after(d_first, qkv_own, qkv_other)
        qkv_sum = Reduce(plan, qkv_own, qkv_other) if staging else (qkv_own, qkv_other)
        if staging:
            big_sum.wait(qkv_own)
            big_sum.first()
            d_first = after(d_first, big_sum.operand)
            if upper is not None:
                d_first = after(d_first, *qkv_upper.pending)
        grad = input_grad(
            table, d_short, d_query, d_kv, d_first, w_qkv, half_qkv, start, BF16 if last else F32
        )
        if staging:
            big_sum.wait(grad[0])
            qkv_sum.wait(grad[0])
            big_sum.line()
            qkv_sum.second()
            if not last:
                grad = (after(grad[0], big_sum.operand, qkv_sum.operand), grad[1])
        upper = (big_sum, qkv_sum)
        kept.append(upper)
        sums = jnp.concatenate([columns[:, :width], columns[:, 2 * width :], sums[2:]], axis=0)
        short_term = jnp.sum(
            gate_sum_short.reshape(shorts, HEADS, HEAD).sum(-1) * (1.0 - gate_short[layer]), axis=0
        )
        long_term = gate_sum_long.reshape(blocks, HEADS, HEAD).sum(-1) * (1.0 - gate_long[layer])
        logit_term = (
            jnp.einsum("sh,i,sj->hij", long_term, own_hot, near_hot, precision=highest)
            + short_term[:, None, None] * corner[None]
        )
        terms.append((sums, sums_up, logit_term))
    kept, terms = kept[::-1], terms[::-1]

    packed_sums = jnp.concatenate(
        [
            jnp.stack([term[0] for term in terms]).reshape(-1),
            jnp.stack([term[1] for term in terms]).reshape(-1),
            jnp.stack([term[2] for term in terms]).reshape(-1),
        ]
    )
    count = packed_sums.shape[0]
    packed_sums = jnp.pad(packed_sums, (0, -count % 1024)).reshape(-1, 128)
    if plan.staged:
        big_sum, qkv_sum = kept[0]
        sums = Butterfly(plan, packed_sums)
        sums.step()
        sums.step(big_sum.operand, qkv_sum.operand)
        qkv_sum.first()
        sums.step(qkv_sum.operand)
        qkv_sum.wait(*big_sum.pending)
        qkv_sum.line()
        sums.step(qkv_sum.operand)
        sums.step(*big_sum.pending)
        packed_sums = sums.finish()
    else:
        packed_sums = lax.psum(packed_sums, AXES)
    packed_sums = packed_sums.reshape(-1)
    edge = layers * 8 * width
    vectors_all = packed_sums[:edge].reshape(layers, 8, width)
    vectors_grad = lax.dynamic_slice_in_dim(vectors_all, device * own_rows, own_rows, 2).transpose(0, 2, 1)
    bias_all = packed_sums[edge : edge + layers * inner].reshape(layers, inner)
    up_bias_grad = []
    for layer in range(layers):
        biases = bias_all[layer].reshape(per_row, width)
        up_bias_grad.append(lax.dynamic_slice_in_dim(biases, device * own_rows, own_rows, 1).reshape(-1))
    up_bias_grad = jnp.stack(up_bias_grad)
    logit_grad = packed_sums[edge + layers * inner : count].reshape(mask_logit.shape)

    qkv_grad, out_grad, up_grad, down_grad = [], [], [], []
    for layer in range(layers):
        big, qkv_parts = kept[layer]
        if plan.staged:
            qkv_sum = qkv_parts.finish()

            def part_of(which):
                return lax.dynamic_slice_in_dim(qkv_sum, which * own_rows, own_rows, 0)

            mine, got = part_of(core), send(part_of(1 - core), plan.cores)
            qkv_grad.append(join(core, mine, got))
        else:
            sides = [array.reshape(width, half_qkv) for array in qkv_parts]
            qkv_grad.append(scattered(jnp.concatenate(sides, axis=1)).astype(F32))
        if plan.staged:
            big_sum = big.finish()
            span = per_row * half

            def big_of(which):
                return lax.dynamic_slice_in_dim(big_sum, which * own_rows, own_rows, 0)

            mine, got = big_of(core), send(big_of(1 - core), plan.cores)

            def unfold(array):
                array = array.reshape(own_rows, per_row, half).transpose(1, 0, 2)
                return array.reshape(per_row * own_rows, half)

            down_grad.append(join(core, unfold(mine[:, :span]), unfold(got[:, :span])))
            up = join(core, mine[:, span : span + half_up], got[:, span : span + half_up])
            out_grad.append(join(core, mine[:, span + half_up :], got[:, span + half_up :]))
        else:
            total = big.astype(F32)
            down = total[:, :inner].reshape(own_rows, per_row, width).transpose(1, 0, 2)
            down_grad.append(down.reshape(per_row * own_rows, width))
            up = total[:, inner : 2 * inner]
            out_grad.append(total[:, 2 * inner :])
        up = up.reshape(own_rows, per_row, plan.devices, own_rows)
        up_grad.append(up.transpose(0, 2, 1, 3).reshape(own_rows, inner))
    return (
        outputs[0].reshape(shorts, block_rows, width),
        outputs[1][None],
        grad[0].reshape(shorts, block_rows, width),
        grad[1][None],
        jnp.stack(qkv_grad),
        jnp.stack(out_grad),
        jnp.stack(up_grad),
        jnp.stack(down_grad),
        vectors_grad,
        up_bias_grad,
        logit_grad,
    )


def join(core, mine, got):
    return jnp.where(
        core == 0, jnp.concatenate([mine, got], axis=1), jnp.concatenate([got, mine], axis=1)
    )


def solution(mesh):
    split = ("dp", "seq")
    in_specs = (
        P(split, None, None),
        P("dp", "seq", None),
        P(split, None, None),
        P("dp", "seq", None),
        P(None, split, None),
        P(None, split, None),
        P(None, split, None),
        P(None, split, None),
        P(None, split, None),
        P(None, split),
        P(),
        P(None, split, None),
        P(None, "dp", None, None, None),
        P("dp", None, None),
        P("dp", None),
    )
    out_specs = (
        P(split, None, None),
        P("dp", "seq", None),
        P(split, None, None),
        P("dp", "seq", None),
        P(None, split, None),
        P(None, split, None),
        P(None, split, None),
        P(None, split, None),
        P(None, split, None),
        P(None, split),
        P(),
    )

    def build(*arrays):
        plan = Plan(mesh, arrays[4].shape[1])
        return jax.shard_map(
            functools.partial(on_device, plan),
            mesh=mesh,
            in_specs=in_specs,
            out_specs=out_specs,
            check_vma=False,
        )(*arrays)

    return build
```

```python
import functools

import jax
import jax.numpy as jnp
from jax import lax
from jax.experimental import pallas as pl
from jax.experimental.pallas import tpu as pltpu
from jax.sharding import PartitionSpec as P

HEADS = 12
HEAD = 64
BLOCK = 128
AXES = ("dp", "seq")
BF16 = jnp.bfloat16
F32 = jnp.float32
VMEM = pl.BlockSpec(memory_space=pltpu.VMEM)
SMEM = pl.BlockSpec(memory_space=pltpu.SMEM)
ANY = pl.BlockSpec(memory_space=pl.ANY)
SMALL = 128
ROOT_HALF = 0.7071067811865476
ROOT_TWO_PI_INV = 0.3989422804014327


def sds(shape, dtype):
    return jax.ShapeDtypeStruct(shape, dtype)


def params(mib=60):
    return pltpu.CompilerParams(vmem_limit_bytes=mib * 2**20)


def cost(us):
    return pl.CostEstimate(flops=0, bytes_accessed=int(us * 3.3e6), transcendentals=0)


def dot(left, right):
    return jnp.dot(left, right, preferred_element_type=F32)


def dot_rt(left, right):
    return lax.dot_general(left, right, (((1,), (1,)), ((), ())), preferred_element_type=F32)


def dot_lt(left, right):
    return lax.dot_general(left, right, (((0,), (0,)), ((), ())), preferred_element_type=F32)


class Plan:
    def __init__(self, mesh, width):
        dp, seq = mesh.shape["dp"], mesh.shape["seq"]
        self.dp, self.seq, self.devices = dp, seq, dp * seq
        depth = dp // 2
        chips = depth * 4
        self.staged = (
            seq == 4
            and dp % 2 == 0
            and depth & (depth - 1) == 0
            and width % chips == 0
            and (width // chips) % 16 == 0
        )
        self.depth, self.chips = depth, chips if self.staged else 16
        if self.staged:
            self.z_perms = [self.flip(z=step) for step in range(1, depth)]
            self.first = self.flip_by_core((0, 1), (1, 0))
            self.second = self.flip_by_core((1, 0), (0, 1))
            self.cores = self.flip(core=1)

    def flip(self, z=0, x=0, y=0, core=0):
        pairs = []
        for dev in range(self.devices):
            pairs.append((dev, dev ^ (z * 8 + x * 4 + y * 2 + core)))
        return pairs

    def flip_by_core(self, even, odd):
        pairs = []
        for dev in range(self.devices):
            x, y = even if dev % 2 == 0 else odd
            pairs.append((dev, dev ^ (x * 4 + y * 2)))
        return pairs

    def tables(self):
        slots = jnp.arange(self.chips, dtype=jnp.int32)
        if not self.staged:
            return jnp.concatenate([slots, slots, jnp.zeros((8,), jnp.int32), slots, slots])
        me = lax.axis_index("dp") * 4 + lax.axis_index("seq")
        core, chip = me % 2, me // 2
        away = slots ^ chip
        z, x, y = away // 4, (away // 2) % 2, away % 2
        y_slot = (x * 2 + y) * self.depth + z
        x_slot = (y * 2 + x) * self.depth + z
        steps, a, b = slots % self.depth, (slots // self.depth) % 2, slots // (2 * self.depth)
        y_chip = (steps * 4 + b * 2 + a) ^ chip
        x_chip = (steps * 4 + a * 2 + b) ^ chip
        even = core == 0
        return jnp.concatenate(
            [
                jnp.where(even, y_slot, x_slot),
                jnp.where(even, x_slot, y_slot),
                jnp.full((8,), core, jnp.int32),
                jnp.where(even, y_chip, x_chip),
                jnp.where(even, x_chip, y_chip),
            ]
        ).astype(jnp.int32)


def gather(plan, first, second, core):
    even = core == 0
    got = send(jnp.where(even, second, first), plan.cores)
    mine = jnp.where(even, first, second)
    base = jnp.where(even, jnp.concatenate([mine, got]), jnp.concatenate([got, mine]))
    line = jnp.stack([base] + [send(base, pairs) for pairs in plan.z_perms])
    near = jnp.concatenate([line, send(line, plan.first)])
    far = send(near, plan.second)
    return (near, far, send(near, plan.cores), send(far, plan.cores))


def send(value, pairs):
    return lax.ppermute(value, AXES, pairs)


def after(value, *earlier):
    return lax.optimization_barrier((value, *earlier))[0]


class Reduce:
    def __init__(self, plan, own, other):
        self.plan, self.own = plan, own
        self.part = plan.chips // 2
        self.quarter = self.part // 2
        self.pending = send(other, plan.cores)

    def wait(self, *values):
        if isinstance(self.pending, list):
            self.pending = [after(value, *values) for value in self.pending]
        else:
            self.pending = after(self.pending, *values)

    def second(self, *earlier):
        part = self.part
        self.got = self.pending
        away = self.own[part:].astype(F32) + self.got[part:].astype(F32)
        self.operand = after(away.astype(BF16), *earlier) if earlier else away.astype(BF16)
        self.pending = send(self.operand, self.plan.second)

    def first(self):
        part, quarter = self.part, self.quarter
        self.got_b = self.pending
        near = self.own[quarter:part].astype(F32) + self.got[quarter:part].astype(F32)
        near = near + self.got_b[quarter:].astype(F32)
        self.operand = near.astype(BF16)
        self.pending = send(self.operand, self.plan.first)

    def line(self):
        quarter = self.quarter
        line = self.own[:quarter].astype(F32) + self.got[:quarter].astype(F32)
        line = line + self.got_b[:quarter].astype(F32) + self.pending.astype(F32)
        self.operand = low = line.astype(BF16)
        self.total = line[0]
        self.pending = [send(low[step + 1], pairs) for step, pairs in enumerate(self.plan.z_perms)]

    def finish(self):
        total = self.total
        for value in self.pending:
            total = total + value.astype(F32)
        return total


class Butterfly:
    def __init__(self, plan, value):
        self.plan, self.value, self.bit, self.pending = plan, value, 1, None

    def step(self, *earlier):
        if self.pending is not None:
            self.value = self.value + after(self.pending, *earlier)
        self.pending = None
        if self.bit < self.plan.devices:
            pairs = [(dev, dev ^ self.bit) for dev in range(self.plan.devices)]
            self.pending = send(self.value, pairs)
            self.bit *= 2

    def finish(self):
        while self.pending is not None:
            self.step()
        return self.value


class Copies:
    def __init__(self, sems):
        self.sems, self.count = sems, 0

    def start(self, source, target):
        copy = pltpu.make_async_copy(source, target, self.sems.at[self.count])
        self.count += 1
        copy.start()
        return copy


def wait_all(copies):
    for copy in copies:
        copy.wait()


def load_staged(copies, table, pieces, low, high, target):
    begun = []
    slots, rows, _ = pieces[0].shape
    count = 2 * slots
    core = table[2 * count]
    for place, piece in enumerate(pieces):
        half = core if place < 2 else 1 - core
        lanes = pl.ds(pl.multiple_of(half * (high - low), 128), high - low)
        for slot in range(slots):
            chip = table[2 * count + 8 + place * slots + slot]
            here = pl.ds(pl.multiple_of(chip * rows, 16), rows)
            begun.append(copies.start(piece.at[slot, :, low:high], target.at[here, lanes]))
    return begun


def project_kernel(start, table, rows_short, rows_long, vec, *rest):
    *weights_in, out_short, out_query, out_kv, rows, weight, out, sems = rest
    copies = Copies(sems)
    short, width = rows_short.shape
    begun = [
        copies.start(rows_short, rows.at[:short, :]),
        copies.start(rows_long, rows.at[short:, :]),
    ]
    loads = []
    if len(weights_in) > 1:
        begun += load_staged(copies, table, weights_in, 0, 3 * width // 2, weight)
    else:
        for part in range(3):
            here = slice(start + part * width, start + (part + 1) * width)
            loads.append(
                copies.start(weights_in[0].at[:, here], weight.at[:, part * width : (part + 1) * width])
            )
    wait_all(begun)
    done = []
    for part in range(3):
        lanes = slice(part * width, (part + 1) * width)
        wait_all(loads[part : part + 1])
        result = dot(rows[...], weight[:, lanes])
        if part != 1:
            result = result + vec[part // 2 : part // 2 + 1, :]
        out[:, lanes] = result.astype(BF16)
        if part == 0:
            target = out_query
        else:
            target = out_kv.at[:, (part - 1) * width : part * width]
        done.append(copies.start(out.at[short:, lanes], target))
        done.append(copies.start(out.at[:short, lanes], out_short.at[:, lanes]))
    wait_all(done)


def project(table, rows_short, rows_long, vec, weights, start):
    short, width = rows_short.shape
    count = short + rows_long.shape[0]
    return pl.pallas_call(
        functools.partial(project_kernel, start),
        out_shape=[
            sds((short, 3 * width), BF16),
            sds((count - short, width), BF16),
            sds((count - short, 2 * width), BF16),
        ],
        in_specs=[SMEM, ANY, ANY, VMEM] + [ANY] * len(weights),
        out_specs=[ANY] * 3,
        scratch_shapes=[
            pltpu.VMEM((count, width), BF16),
            pltpu.VMEM((width, 3 * width), BF16),
            pltpu.VMEM((count, 3 * width), BF16),
            pltpu.SemaphoreType.DMA((48,)),
        ],
        compiler_params=params(),
        cost_estimate=cost(10),
        name="project",
    )(table, rows_short, rows_long, vec, *weights)


def head_masks():
    lane = lax.broadcasted_iota(jnp.int32, (BLOCK, BLOCK), 1)
    low = jnp.where(lane < HEAD, 1.0, 0.0).astype(BF16)
    high = jnp.where(lane < HEAD, 0.0, 1.0).astype(BF16)
    return low, high


def spread(pair, low, high):
    return jnp.concatenate([pair * low, pair * high], axis=0)


def short_forward_kernel(qkv, gate, mixed, raised, inverse):
    low, high = head_masks()
    ones = jnp.concatenate([low, high], axis=0)
    width = mixed.shape[1]
    for pair in range(HEADS // 2):
        lanes = slice(pair * 128, pair * 128 + 128)
        query = qkv[:, lanes] * 0.125
        keys = spread(qkv[:, width + pair * 128 : width + pair * 128 + 128], low, high)
        values = spread(qkv[:, 2 * width + pair * 128 : 2 * width + pair * 128 + 128], low, high)
        scores = dot_rt(query, keys)
        left, right = scores[:, :BLOCK], scores[:, BLOCK:]
        left = jnp.exp(left - jnp.max(left, axis=1, keepdims=True))
        right = jnp.exp(right - jnp.max(right, axis=1, keepdims=True))
        prob = jnp.concatenate([left, right], axis=1).astype(BF16)
        both = dot(prob, jnp.concatenate([values, ones], axis=1))
        inv = 1.0 / both[:, BLOCK:]
        raised[0, pair] = prob
        inverse[:, lanes] = inv
        mixed[:, lanes] = (both[:, :BLOCK] * inv * gate[0, :, lanes]).astype(BF16)


def short_forward(qkv, gate):
    rows = qkv.shape[0]
    width = qkv.shape[1] // 3
    count = rows // BLOCK
    pairs = HEADS // 2
    return pl.pallas_call(
        short_forward_kernel,
        grid=(count,),
        out_shape=[
            sds((rows, width), BF16),
            sds((count, pairs, BLOCK, 2 * BLOCK), BF16),
            sds((rows, width), F32),
        ],
        in_specs=[
            pl.BlockSpec((BLOCK, 3 * width), lambda i: (i, 0)),
            pl.BlockSpec((1, 1, width), lambda i: (i, 0, 0)),
        ],
        out_specs=[
            pl.BlockSpec((BLOCK, width), lambda i: (i, 0)),
            pl.BlockSpec((1, pairs, BLOCK, 2 * BLOCK), lambda i: (i, 0, 0, 0)),
            pl.BlockSpec((BLOCK, width), lambda i: (i, 0)),
        ],
        compiler_params=params(),
        cost_estimate=cost(7),
        name="short_forward",
    )(qkv, gate)


def long_forward_kernel(blocks, opened, queries, gate, *rest):
    sources, (mixed, raised, inverse, parts) = rest[:blocks], rest[blocks:]
    low, high = head_masks()
    ones = jnp.concatenate([low, high], axis=0)
    width = mixed.shape[1]
    for pair in range(HEADS // 2):
        lanes = slice(pair * 128, pair * 128 + 128)
        query = queries[:, lanes] * 0.125
        scores, values = [], []
        for index in range(blocks):
            source = sources[index]
            keys = spread(source[:, lanes], low, high)
            values.append(spread(source[:, width + pair * 128 : width + pair * 128 + 128], low, high))
            score = dot_rt(query, keys)
            scores.append(jnp.where(opened[index] > 0, score, -1e30))
        top = functools.reduce(jnp.maximum, scores)
        top_left = jnp.max(top[:, :BLOCK], axis=1, keepdims=True)
        top_right = jnp.max(top[:, BLOCK:], axis=1, keepdims=True)
        both = []
        for index in range(blocks):
            left = jnp.exp(scores[index][:, :BLOCK] - top_left)
            right = jnp.exp(scores[index][:, BLOCK:] - top_right)
            prob = jnp.concatenate([left, right], axis=1).astype(BF16)
            raised[pair, index] = prob
            both.append(dot(prob, jnp.concatenate([values[index], ones], axis=1)))
        inv = 1.0 / sum(value[:, BLOCK:] for value in both)
        inverse[:, lanes] = inv
        total = 0.0
        for index in range(blocks):
            part = both[index][:, :BLOCK] * inv
            parts[index, :, lanes] = part.astype(BF16)
            total = total + part * gate[index : index + 1, lanes]
        mixed[:, lanes] = total.astype(BF16)


def long_forward(opened, queries, gate, sources):
    rows, width = queries.shape
    blocks = len(sources)
    return pl.pallas_call(
        functools.partial(long_forward_kernel, blocks),
        out_shape=[
            sds((rows, width), BF16),
            sds((HEADS // 2, blocks, BLOCK, 2 * BLOCK), BF16),
            sds((rows, width), F32),
            sds((blocks, rows, width), BF16),
        ],
        in_specs=[SMEM, VMEM, VMEM] + [VMEM] * blocks,
        out_specs=[VMEM] * 4,
        compiler_params=params(),
        cost_estimate=cost(5.3),
        name="long_forward",
    )(opened, queries, gate, *sources)


def norm_rows(rows, gain, shift):
    inverse = 1.0 / rows.shape[1]
    center = rows - jnp.sum(rows, axis=1, keepdims=True) * inverse
    spread_ = jnp.sum(center * center, axis=1, keepdims=True) * inverse
    scale = lax.rsqrt(spread_ + 1e-05)
    unit = center * scale
    return unit, scale, unit * gain + shift


def mlp_forward_kernel(
    wide,
    starts,
    rows_short,
    rows_long,
    mixed_short,
    mixed_long,
    vec,
    packed,
    *rest,
):
    (
        y_short,
        y_long,
        y_low_short,
        y_low_long,
        hid_low_out,
        unit1_out,
        scale1,
        unit2_out,
        scale2,
        act_out,
        slope_out,
        weight_out,
        weight_up,
        weight_down,
        mixed,
        hidden,
        hid_low,
        unit,
        y_low,
        act,
        slope,
        sems,
        sem_w,
        sem_o,
        sem_y,
    ) = rest
    out_start, up_start, down_start = starts
    copies = Copies(sems)
    total, width = hidden.shape
    inner = act.shape[1]
    short = rows_short.shape[0]
    tile = width
    steps = inner // tile
    begun = [
        copies.start(mixed_short, mixed.at[:short, :]),
        copies.start(mixed_long, mixed.at[short:, :]),
        copies.start(packed.at[:, out_start : out_start + width], weight_out),
    ]
    downs = []
    for step in range(steps):
        lanes = slice(step * tile, (step + 1) * tile)
        here = slice(up_start + step * tile, up_start + (step + 1) * tile)
        pltpu.make_async_copy(packed.at[:, here], weight_up.at[:, lanes], sem_w.at[step]).start()
    for group in range(inner // width):
        start = down_start + group * width
        downs.append(
            copies.start(packed.at[:, start : start + width], weight_down.at[group * width : (group + 1) * width, :])
        )
    wait_all(begun)
    for step in range(width // 256):
        lanes = slice(step * 256, step * 256 + 256)
        summed = dot(mixed[...], weight_out[:, lanes]) + vec[2:3, lanes]
        hidden[:short, lanes] = summed[:short] + rows_short[:, lanes].astype(F32)
        hidden[short:, lanes] = summed[short:] + rows_long[:, lanes].astype(F32)

    @pl.loop(0, total // BLOCK)
    def _(step):
        here = pl.ds(pl.multiple_of(step * BLOCK, BLOCK), BLOCK)
        level, scale, hid = norm_rows(hidden[here, :], vec[3:4, :], vec[4:5, :])
        unit[here, :] = level.astype(BF16)
        scale1[here, :] = scale
        hidden[here, :] = hid
        hid_low[here, :] = hid.astype(BF16)

    done = [copies.start(unit, unit1_out), copies.start(hid_low, hid_low_out)]

    @pl.loop(0, steps)
    def _(step):
        place = pl.ds(pl.multiple_of(step * tile, tile), tile)
        pltpu.make_async_copy(weight_up.at[:, place], weight_up.at[:, place], sem_w.at[step]).wait()
        upper = dot(hid_low[...], weight_up[:, place]) + vec[pl.ds(8 + step, 1), :]
        below = 0.5 + 0.5 * lax.erf(upper * ROOT_HALF)
        act[:, place] = (upper * below).astype(BF16)
        bell = ROOT_TWO_PI_INV * jnp.exp(-0.5 * upper * upper)
        slope[:, place] = (below + upper * bell).astype(BF16)
        pltpu.make_async_copy(act.at[:, place], act_out.at[:, place], sem_o.at[0, step]).start()
        pltpu.make_async_copy(slope.at[:, place], slope_out.at[:, place], sem_o.at[1, step]).start()

    wait_all(downs)
    for step in range(width // 256):
        lanes = slice(step * 256, step * 256 + 256)
        hidden[:, lanes] = hidden[:, lanes] + dot(act[...], weight_down[:, lanes]) + vec[5:6, lanes]
    wait_all(done)

    @pl.loop(0, total // BLOCK)
    def _(step):
        here = pl.ds(pl.multiple_of(step * BLOCK, BLOCK), BLOCK)
        level, scale, y = norm_rows(hidden[here, :], vec[6:7, :], vec[7:8, :])
        unit[here, :] = level.astype(BF16)
        scale2[here, :] = scale
        hidden[here, :] = y
        y_low[here, :] = y.astype(BF16)
        if wide:

            @pl.when(step < short // BLOCK)
            def _():
                pltpu.make_async_copy(hidden.at[here, :], y_short.at[here, :], sem_y.at[step]).start()

    done = [
        copies.start(unit, unit2_out),
        copies.start(y_low.at[:short, :], y_low_short),
        copies.start(y_low.at[short:, :], y_low_long),
    ]
    if wide:
        done.append(copies.start(hidden.at[short:, :], y_long))

        @pl.loop(0, short // BLOCK)
        def _(step):
            here = pl.ds(pl.multiple_of(step * BLOCK, BLOCK), BLOCK)
            pltpu.make_async_copy(hidden.at[here, :], y_short.at[here, :], sem_y.at[step]).wait()

    @pl.loop(0, steps)
    def _(step):
        place = pl.ds(pl.multiple_of(step * tile, tile), tile)
        pltpu.make_async_copy(act.at[:, place], act_out.at[:, place], sem_o.at[0, step]).wait()
        pltpu.make_async_copy(slope.at[:, place], slope_out.at[:, place], sem_o.at[1, step]).wait()

    wait_all(done)


def mlp_forward(wide, rows_short, rows_long, mixed_short, mixed_long, vec, inner, source):
    rows = rows_short.shape[0] + rows_long.shape[0]
    width = rows_short.shape[1]
    return pl.pallas_call(
        functools.partial(mlp_forward_kernel, wide, source.starts),
        out_shape=[
            sds(rows_short.shape if wide else (8, 128), F32),
            sds(rows_long.shape if wide else (8, 128), F32),
            sds(rows_short.shape, BF16),
            sds(rows_long.shape, BF16),
            sds((rows, width), BF16),
            sds((rows, width), BF16),
            sds((rows, 1), F32),
            sds((rows, width), BF16),
            sds((rows, 1), F32),
            sds((rows, inner), BF16),
            sds((rows, inner), BF16),
        ],
        in_specs=[VMEM, VMEM, ANY, ANY, VMEM, ANY],
        out_specs=[ANY] * 6 + [VMEM, ANY, VMEM, ANY, ANY],
        scratch_shapes=[
            pltpu.VMEM((width, width), BF16),
            pltpu.VMEM((width, inner), BF16),
            pltpu.VMEM((inner, width), BF16),
            pltpu.VMEM((rows, width), BF16),
            pltpu.VMEM((rows, width), F32),
            pltpu.VMEM((rows, width), BF16),
            pltpu.VMEM((rows, width), BF16),
            pltpu.VMEM((rows, width), BF16),
            pltpu.VMEM((rows, inner), BF16),
            pltpu.VMEM((rows, inner), BF16),
            pltpu.SemaphoreType.DMA((24,)),
            pltpu.SemaphoreType.DMA((inner // width,)),
            pltpu.SemaphoreType.DMA((2, inner // width)),
            pltpu.SemaphoreType.DMA((rows // BLOCK,)),
        ],
        compiler_params=params(),
        cost_estimate=cost(28),
        name="mlp_forward",
    )(rows_short, rows_long, mixed_short, mixed_long, vec, source.packed)


def norm_back(grad, unit, scale, gain):
    inverse = 1.0 / grad.shape[1]
    pulled = grad * gain
    mean = jnp.sum(pulled, axis=1, keepdims=True) * inverse
    along = jnp.sum(pulled * unit, axis=1, keepdims=True) * inverse
    return scale * (pulled - mean - unit * along)


def ffn_backward_kernel(
    down_start,
    grad_short,
    grad_long,
    unit2,
    scale2,
    vec,
    slope_in,
    packed,
    second_out,
    d_out_out,
    sums,
    sums_up,
    d_up_out,
    weight,
    second,
    d_out,
    slope,
    d_up,
    sems,
    sem_w,
    sem_s,
    sem_o,
):
    copies = Copies(sems)
    total, width = second.shape
    inner = slope.shape[1]
    short = grad_short.shape[0]
    tile = 512
    steps = inner // tile
    loads = []
    for group in range(inner // width):
        start = down_start + group * width
        loads.append(
            copies.start(packed.at[:, start : start + width], weight.at[group * width : (group + 1) * width, :])
        )
    for step in range(steps):
        lanes = slice(step * tile, (step + 1) * tile)
        pltpu.make_async_copy(slope_in.at[:, lanes], slope.at[:, lanes], sem_s.at[step]).start()
    sums[...] = jnp.zeros_like(sums)

    def begin(here, grad):
        dy = grad.astype(F32)
        unit = unit2[here, :].astype(F32)
        dr = norm_back(dy, unit, scale2[here, :], vec[6:7, :])
        second[here, :] = dr
        low = dr.astype(BF16)
        d_out[here, :] = low
        sums[5:6, :] += jnp.sum(low.astype(F32), axis=0, keepdims=True)
        sums[6:7, :] += jnp.sum(dy * unit, axis=0, keepdims=True)
        sums[7:8, :] += jnp.sum(dy, axis=0, keepdims=True)

    @pl.loop(0, short // BLOCK)
    def _(step):
        here = pl.ds(pl.multiple_of(step * BLOCK, BLOCK), BLOCK)
        begin(here, grad_short[here, :])

    begin(slice(short, total), grad_long[...])
    done = [copies.start(second, second_out), copies.start(d_out, d_out_out)]
    wait_all(loads)

    @pl.loop(0, steps)
    def _(step):
        place = pl.ds(pl.multiple_of(step * tile, tile), tile)
        pltpu.make_async_copy(slope_in.at[:, place], slope.at[:, place], sem_s.at[step]).wait()
        low = (dot_rt(d_out[...], weight[place, :]) * slope[:, place].astype(F32)).astype(BF16)
        d_up[:, place] = low
        sums_up[:, place] = jnp.sum(low.astype(F32), axis=0, keepdims=True)
        pltpu.make_async_copy(d_up.at[:, place], d_up_out.at[:, place], sem_o.at[step]).start()

    @pl.loop(0, steps)
    def _(step):
        place = pl.ds(pl.multiple_of(step * tile, tile), tile)
        pltpu.make_async_copy(d_up.at[:, place], d_up_out.at[:, place], sem_o.at[step]).wait()

    wait_all(done)


def ffn_backward(grad, unit2, scale2, vec, slope, source):
    rows, width = unit2.shape
    inner = slope.shape[1]
    return pl.pallas_call(
        functools.partial(ffn_backward_kernel, source.starts[2]),
        out_shape=[
            sds((rows, width), F32),
            sds((rows, width), BF16),
            sds((8, width), F32),
            sds((1, inner), F32),
            sds((rows, inner), BF16),
        ],
        in_specs=[VMEM] * 5 + [ANY, ANY],
        out_specs=[ANY, ANY, VMEM, VMEM, ANY],
        scratch_shapes=[
            pltpu.VMEM((inner, width), BF16),
            pltpu.VMEM((rows, width), F32),
            pltpu.VMEM((rows, width), BF16),
            pltpu.VMEM((rows, inner), BF16),
            pltpu.VMEM((rows, inner), BF16),
            pltpu.SemaphoreType.DMA((inner // width + 2,)),
            pltpu.SemaphoreType.DMA((1,)),
            pltpu.SemaphoreType.DMA((inner // 512,)),
            pltpu.SemaphoreType.DMA((inner // 512,)),
        ],
        compiler_params=params(),
        cost_estimate=cost(14),
        name="ffn_backward",
    )(*grad, unit2, scale2, vec, slope, source.packed)


def mid_backward_kernel(starts, second_in, d_up_in, unit1_in, scale1, vec, packed, *rest):
    (
        d_first_out,
        d_att_out,
        d_mixed_short,
        d_mixed_long,
        sums,
        weight_out,
        weight_up,
        second,
        partial,
        unit1,
        d_up,
        d_att,
        d_mixed,
        sems,
    ) = rest
    out_start, up_start, _ = starts
    copies = Copies(sems)
    total, width = second.shape
    inner = d_up.shape[1]
    short = d_mixed_short.shape[0]
    spans = [slice(0, width), slice(width, inner)]
    loads = []
    for span in spans:
        here = slice(up_start + span.start, up_start + span.stop)
        loads.append(
            [
                copies.start(d_up_in.at[:, span], d_up.at[:, span]),
                copies.start(packed.at[:, here], weight_up.at[:, span]),
            ]
        )
    rest = [
        copies.start(second_in, second),
        copies.start(unit1_in, unit1),
        copies.start(packed.at[:, out_start : out_start + width], weight_out),
    ]
    sums[...] = jnp.zeros_like(sums)
    for part, span in enumerate(spans):
        wait_all(loads[part])
        for step in range(width // 256):
            lanes = slice(step * 256, step * 256 + 256)
            piece = dot_rt(d_up[:, span], weight_up[lanes, span])
            partial[:, lanes] = piece if part == 0 else partial[:, lanes] + piece
    wait_all(rest)

    @pl.loop(0, total // BLOCK)
    def _(step):
        here = pl.ds(pl.multiple_of(step * BLOCK, BLOCK), BLOCK)
        dh = second[here, :] + partial[here, :]
        unit = unit1[here, :].astype(F32)
        dr = norm_back(dh, unit, scale1[here, :], vec[3:4, :])
        second[here, :] = dr
        low = dr.astype(BF16)
        d_att[here, :] = low
        sums[2:3, :] += jnp.sum(low.astype(F32), axis=0, keepdims=True)
        sums[3:4, :] += jnp.sum(dh * unit, axis=0, keepdims=True)
        sums[4:5, :] += jnp.sum(dh, axis=0, keepdims=True)

    done = [copies.start(second, d_first_out), copies.start(d_att, d_att_out)]
    for step in range(width // 256):
        lanes = slice(step * 256, step * 256 + 256)
        d_mixed[:, lanes] = dot_rt(d_att[...], weight_out[lanes, :]).astype(BF16)
        done.append(copies.start(d_mixed.at[:short, lanes], d_mixed_short.at[:, lanes]))
        done.append(copies.start(d_mixed.at[short:, lanes], d_mixed_long.at[:, lanes]))
    wait_all(done)


def mid_backward(second, d_up, unit1, scale1, vec, source, short):
    rows, width = second.shape
    inner = d_up.shape[1]
    return pl.pallas_call(
        functools.partial(mid_backward_kernel, source.starts),
        out_shape=[
            sds((rows, width), F32),
            sds((rows, width), BF16),
            sds((short, width), BF16),
            sds((rows - short, width), BF16),
            sds((8, width), F32),
        ],
        in_specs=[ANY, ANY, ANY, VMEM, VMEM, ANY],
        out_specs=[ANY] * 4 + [VMEM],
        scratch_shapes=[
            pltpu.VMEM((width, width), BF16),
            pltpu.VMEM((width, inner), BF16),
            pltpu.VMEM((rows, width), F32),
            pltpu.VMEM((rows, width), F32),
            pltpu.VMEM((rows, width), BF16),
            pltpu.VMEM((rows, inner), BF16),
            pltpu.VMEM((rows, width), BF16),
            pltpu.VMEM((rows, width), BF16),
            pltpu.SemaphoreType.DMA((24,)),
        ],
        compiler_params=params(),
        cost_estimate=cost(14),
        name="mid_backward",
    )(second, d_up, unit1, scale1, vec, source.packed)


def put_rows(table, result, buffer, part, lanes):
    chips, block = buffer.shape[1:3]
    far = jnp.bitwise_xor(table[2 * chips], part)
    for chip in range(chips):
        slot = table[far * chips + chip]
        buffer[far, slot, :, lanes] = result[chip * block : (chip + 1) * block, :]


def ffn_grads_kernel(
    table, act_in, d_out_in, hid_in, d_up_in, own, other, act, d_out, hid_low, d_up, turned, buffer, sem_i, sem_o
):
    inner = act.shape[1]
    width = d_out.shape[1]
    half_up, half = inner // 2, width // 2
    groups = inner // width
    tile = 768
    loads, ups = Copies(sem_i), []
    begun = [loads.start(d_out_in, d_out)]
    acts = []
    for step in range(groups):
        place = slice(step * width, step * width + width)
        acts.append(loads.start(act_in.at[:, place], act.at[:, place]))
        if step == 0:
            turning = loads.start(hid_in, hid_low)
    for step in range(inner // tile):
        place = slice(step * tile, step * tile + tile)
        ups.append(loads.start(d_up_in.at[:, place], d_up.at[:, place]))
    stores, done = Copies(sem_o), []

    def flush(lanes):
        done.append(stores.start(buffer.at[0, :, :, lanes], own.at[:, :, lanes]))
        done.append(stores.start(buffer.at[1, :, :, lanes], other.at[:, :, lanes]))

    wait_all(begun)
    for step in range(groups):
        acts[step].wait()
        result = dot_lt(act[:, step * width : (step + 1) * width], d_out[...]).astype(BF16)
        lanes = slice(step * half, (step + 1) * half)
        for part in range(2):
            put_rows(table, result[:, part * half : (part + 1) * half], buffer, part, lanes)
        flush(lanes)
    base = groups * half
    turning.wait()
    turned[...] = hid_low[...].T
    for place in range(0, half_up, tile):
        for part in range(2):
            step = (part * half_up + place) // tile
            ups[step].wait()
            result = dot(turned[...], d_up[:, step * tile : (step + 1) * tile]).astype(BF16)
            put_rows(table, result, buffer, part, slice(base + place, base + place + tile))
        flush(slice(base + place, base + place + tile))
    wait_all(done)


def ffn_grads(table, chips, act, d_out, hid_low, d_up):
    rows, inner = act.shape
    width = d_out.shape[1]
    block = width // chips
    groups = inner // width
    cols = groups * width // 2 + inner // 2
    return pl.pallas_call(
        ffn_grads_kernel,
        out_shape=[sds((chips, block, cols), BF16)] * 2,
        in_specs=[SMEM, ANY, ANY, ANY, ANY],
        out_specs=[ANY, ANY],
        scratch_shapes=[
            pltpu.VMEM((rows, inner), BF16),
            pltpu.VMEM((rows, width), BF16),
            pltpu.VMEM((rows, width), BF16),
            pltpu.VMEM((rows, inner), BF16),
            pltpu.VMEM((width, rows), BF16),
            pltpu.VMEM((2, chips, block, cols), BF16),
            pltpu.SemaphoreType.DMA((groups + inner // 768 + 2,)),
            pltpu.SemaphoreType.DMA((2 * groups + 2 * (inner // 1536),)),
        ],
        compiler_params=params(),
        cost_estimate=cost(16),
        name="ffn_grads",
    )(table, act, d_out, hid_low, d_up)


def att_grads_kernel(
    table,
    mixed_short,
    mixed_long,
    d_att_in,
    rows_short,
    rows_long,
    d_short,
    d_query,
    d_own,
    far,
    passed,
    own,
    other,
    columns,
    d_att,
    mixed,
    rows,
    grad,
    turned,
    buffer,
    sem_i,
    sem_o,
    sem_q,
):
    short, width = rows_short.shape
    half = width // 2
    half_qkv = 3 * half
    loads = Copies(sem_i)
    first = [
        loads.start(d_att_in, d_att),
        loads.start(mixed_short, mixed.at[:short, :]),
        loads.start(mixed_long, mixed.at[short:, :]),
    ]
    second = [
        loads.start(rows_short, rows.at[:short, :]),
        loads.start(rows_long, rows.at[short:, :]),
    ]
    third = [
        loads.start(d_query, grad.at[short:, :width]),
        loads.start(d_short, grad.at[:short, :]),
    ]
    total = d_own[...].astype(F32) + far[0].astype(F32) + passed[...].astype(F32)
    grad[short:, width:] = total.astype(BF16)
    stores, done = Copies(sem_o), []

    def flush(lanes):
        done.append(stores.start(buffer.at[0, :, :, lanes], own.at[:, :, lanes]))
        done.append(stores.start(buffer.at[1, :, :, lanes], other.at[:, :, lanes]))

    wait_all(first)
    result = dot_lt(mixed[...], d_att[...]).astype(BF16)
    for part in range(2):
        put_rows(table, result[:, part * half : (part + 1) * half], buffer, part, slice(0, half))
    flush(slice(0, half))
    wait_all(second)
    turned[...] = rows[...].T
    wait_all(third)
    for step in range(3):
        lanes = slice(step * width, (step + 1) * width)
        piece = grad[:, lanes]
        columns[:, lanes] = jnp.sum(piece.astype(F32), axis=0, keepdims=True)
        result = dot(turned[...], piece).astype(BF16)
        for place in range(0, width, half):
            part, start = divmod(step * width + place, half_qkv)
            put_rows(
                table, result[:, place : place + half], buffer, part, slice(half + start, half + start + half)
            )
            far_part = jnp.bitwise_xor(table[2 * buffer.shape[1]], part)
            lanes_out = slice(half + start, half + start + half)
            index = 2 * step + place // half
            for which, target in enumerate((own, other)):

                @pl.when(far_part == which)
                def _(which=which, target=target, lanes_out=lanes_out, index=index):
                    pltpu.make_async_copy(
                        buffer.at[which, :, :, lanes_out], target.at[:, :, lanes_out], sem_q.at[index]
                    ).start()

    for index in range(6):
        part, start = divmod(index * half, half_qkv)
        lanes_out = slice(half + start, half + start + half)
        pltpu.make_async_copy(buffer.at[0, :, :, lanes_out], own.at[:, :, lanes_out], sem_q.at[index]).wait()
    wait_all(done)


def att_grads(
    table, chips, mixed_short, mixed_long, d_att, rows_short, rows_long, d_short, d_query, d_own, far, passed
):
    short, width = rows_short.shape
    rows = short + rows_long.shape[0]
    block = width // chips
    cols = 2 * width
    return pl.pallas_call(
        att_grads_kernel,
        out_shape=[sds((chips, block, cols), BF16)] * 2 + [sds((1, 3 * width), F32)],
        in_specs=[SMEM] + [ANY] * 7 + [VMEM] * 3,
        out_specs=[ANY, ANY, VMEM],
        scratch_shapes=[
            pltpu.VMEM((rows, width), BF16),
            pltpu.VMEM((rows, width), BF16),
            pltpu.VMEM((rows, width), BF16),
            pltpu.VMEM((rows, 3 * width), BF16),
            pltpu.VMEM((width, rows), BF16),
            pltpu.VMEM((2, chips, block, cols), BF16),
            pltpu.SemaphoreType.DMA((7,)),
            pltpu.SemaphoreType.DMA((2,)),
            pltpu.SemaphoreType.DMA((6,)),
        ],
        compiler_params=params(),
        cost_estimate=cost(12),
        name="att_grads",
    )(table, mixed_short, mixed_long, d_att, rows_short, rows_long, d_short, d_query, d_own, far, passed)


def input_grad_kernel(start, table, d_short, d_query, d_own, far, passed, d_first, *rest):
    *weights_in, out_short, out_long, weight, grad, first, out, sems = rest
    copies = Copies(sems)
    short, width = d_short.shape[0], out_short.shape[1]
    loads = []
    if len(weights_in) > 1:
        staged = load_staged(copies, table, weights_in, 0, 3 * width // 2, weight)
    for part in range(3):
        lanes = slice(part * width, (part + 1) * width)
        loads.append([copies.start(d_short.at[:, lanes], grad.at[:short, lanes])])
        if part == 0:
            loads[0].append(copies.start(d_query, grad.at[short:, lanes]))
        if len(weights_in) == 1:
            here = slice(start + part * width, start + (part + 1) * width)
            loads[part].append(copies.start(weights_in[0].at[:, here], weight.at[:, lanes]))
        elif part == 0:
            loads[0] += staged
        if part == 0:
            adding = copies.start(d_first, first)
    total = d_own[...].astype(F32) + far[0].astype(F32) + passed[...].astype(F32)
    grad[short:, width:] = total.astype(BF16)
    done = []
    for part in range(3):
        wait_all(loads[part])
        span = slice(part * width, (part + 1) * width)
        for step in range(width // 256):
            lanes = slice(step * 256, step * 256 + 256)
            total = dot_rt(grad[:, span], weight[lanes, span])
            if part == 0 and step == 0:
                adding.wait()
            if part < 2:
                first[:, lanes] = first[:, lanes] + total
                continue
            out[:, lanes] = (first[:, lanes] + total).astype(out.dtype)
            done.append(copies.start(out.at[:short, lanes], out_short.at[:, lanes]))
            done.append(copies.start(out.at[short:, lanes], out_long.at[:, lanes]))
    wait_all(done)


def input_grad(table, d_short, d_query, d_own, far, passed, d_first, weights, start, dtype):
    rows, width = d_first.shape
    short = d_short.shape[0]
    return pl.pallas_call(
        functools.partial(input_grad_kernel, start),
        out_shape=[sds((short, width), dtype), sds((rows - short, width), dtype)],
        in_specs=[SMEM, ANY, ANY, VMEM, VMEM, VMEM, ANY] + [ANY] * len(weights),
        out_specs=[ANY] * 2,
        scratch_shapes=[
            pltpu.VMEM((width, 3 * width), BF16),
            pltpu.VMEM((rows, 3 * width), BF16),
            pltpu.VMEM((rows, width), F32),
            pltpu.VMEM((rows, width), dtype),
            pltpu.SemaphoreType.DMA((56,)),
        ],
        compiler_params=params(),
        cost_estimate=cost(10),
        name="input_grad",
    )(table, d_short, d_query, d_own, far, passed, d_first, *weights)


def short_backward_kernel(qkv, mixed, d_mixed, raised, inverse, gate, d_qkv, gate_sum):
    low, high = head_masks()
    ones = jnp.concatenate([low, high], axis=0)
    width = mixed.shape[1]
    for pair in range(HEADS // 2):
        lanes = slice(pair * 128, pair * 128 + 128)
        query = qkv[:, lanes] * 0.125
        keys = spread(qkv[:, width + pair * 128 : width + pair * 128 + 128], low, high)
        values = spread(qkv[:, 2 * width + pair * 128 : 2 * width + pair * 128 + 128], low, high)
        grad = d_mixed[:, lanes].astype(F32)
        out = mixed[:, lanes].astype(F32)
        scaled = grad * inverse[:, lanes]
        gate_sum[0, :, lanes] = jnp.sum(grad * out, axis=0, keepdims=True)
        pulled = (scaled * gate[0, :, lanes]).astype(BF16)
        inner = (scaled * out).astype(BF16)
        prob = raised[0, pair]
        bent = dot_rt(jnp.concatenate([pulled, inner], axis=1), jnp.concatenate([values, -ones], axis=1))
        score = (prob.astype(F32) * bent).astype(BF16)
        d_qkv[:, lanes] = (dot(score, keys) * 0.125).astype(BF16)
        turned = dot_lt(query, score)
        turned = jnp.concatenate([turned[:HEAD, :BLOCK], turned[HEAD:, BLOCK:]], axis=0)
        d_qkv[:, width + pair * 128 : width + pair * 128 + 128] = turned.T.astype(BF16)
        turned = dot_lt(pulled, prob)
        turned = jnp.concatenate([turned[:HEAD, :BLOCK], turned[HEAD:, BLOCK:]], axis=0)
        d_qkv[:, 2 * width + pair * 128 : 2 * width + pair * 128 + 128] = turned.T.astype(BF16)


def short_backward(qkv, mixed, d_mixed, raised, inverse, gate):
    rows, width = mixed.shape
    count = rows // BLOCK
    pairs = HEADS // 2
    narrow = pl.BlockSpec((BLOCK, width), lambda i: (i, 0))
    wide = pl.BlockSpec((BLOCK, 3 * width), lambda i: (i, 0))
    vector = pl.BlockSpec((1, 1, width), lambda i: (i, 0, 0))
    return pl.pallas_call(
        short_backward_kernel,
        grid=(count,),
        out_shape=[sds((rows, 3 * width), BF16), sds((count, 1, width), F32)],
        in_specs=[
            wide,
            narrow,
            narrow,
            pl.BlockSpec((1, pairs, BLOCK, 2 * BLOCK), lambda i: (i, 0, 0, 0)),
            narrow,
            vector,
        ],
        out_specs=[wide, vector],
        compiler_params=params(),
        cost_estimate=cost(11.6),
        name="short_backward",
    )(qkv, mixed, d_mixed, raised, inverse, gate)


def long_backward_kernel(blocks, queries, mixed, d_mixed, raised, inverse, parts, gate, *rest):
    sources, (d_query, d_own, d_near, d_core, gate_sum) = rest[:blocks], rest[blocks:]
    low, high = head_masks()
    ones = jnp.concatenate([low, high], axis=0)
    width = mixed.shape[1]
    for pair in range(HEADS // 2):
        lanes = slice(pair * 128, pair * 128 + 128)
        query = queries[:, lanes] * 0.125
        grad = d_mixed[:, lanes].astype(F32)
        out = mixed[:, lanes].astype(F32)
        scaled = grad * inverse[:, lanes]
        inner = (scaled * out).astype(BF16)
        total = 0.0
        for index in range(blocks):
            source = sources[index]
            keys = spread(source[:, lanes], low, high)
            values = spread(source[:, width + pair * 128 : width + pair * 128 + 128], low, high)
            strength = gate[index : index + 1, lanes]
            pulled = (scaled * strength).astype(BF16)
            prob = raised[pair, index]
            bent = dot_rt(jnp.concatenate([pulled, inner], axis=1), jnp.concatenate([values, -ones], axis=1))
            score = (prob.astype(F32) * bent).astype(BF16)
            total = total + dot(score, keys)
            gate_sum[index : index + 1, lanes] = strength * jnp.sum(
                grad * parts[index, :, lanes].astype(F32), axis=0, keepdims=True
            )
            target = (d_own, d_core.at[0], d_near, d_core.at[1])[index]
            turned = dot_lt(query, score)
            turned = jnp.concatenate([turned[:HEAD, :BLOCK], turned[HEAD:, BLOCK:]], axis=0)
            target[:, lanes] = turned.T.astype(BF16)
            turned = dot_lt(pulled, prob)
            turned = jnp.concatenate([turned[:HEAD, :BLOCK], turned[HEAD:, BLOCK:]], axis=0)
            target[:, width + pair * 128 : width + pair * 128 + 128] = turned.T.astype(BF16)
        d_query[:, lanes] = (total * 0.125).astype(BF16)


def long_backward(queries, mixed, d_mixed, raised, inverse, parts, gate, sources):
    rows, width = mixed.shape
    blocks = len(sources)
    return pl.pallas_call(
        functools.partial(long_backward_kernel, blocks),
        out_shape=[
            sds((rows, width), BF16),
            sds((rows, 2 * width), BF16),
            sds((rows, 2 * width), BF16),
            sds((2, rows, 2 * width), BF16),
            sds((blocks, width), F32),
        ],
        in_specs=[VMEM] * (7 + blocks),
        out_specs=[VMEM] * 5,
        compiler_params=params(),
        cost_estimate=cost(8.7),
        name="long_backward",
    )(queries, mixed, d_mixed, raised, inverse, parts, gate, *sources)


class Source:
    def __init__(self, rows, packed, pieces, starts, qkv_start):
        self.rows, self.packed, self.pieces, self.starts, self.qkv_start = rows, packed, pieces, starts, qkv_start

    def qkv(self):
        return self.pieces if self.pieces else (self.packed,)


def on_device(
    plan,
    short_tokens,
    long_tokens,
    short_cotangent,
    long_cotangent,
    qkv_weight,
    out_weight,
    up_weight,
    down_weight,
    vectors,
    up_bias,
    mask_logit,
    short_noise,
    gate_noise,
    block_mask,
    block_order,
):
    shorts, block_rows, width = short_tokens.shape
    blocks = lax.axis_size("seq")
    place = lax.axis_index("seq")
    device = lax.axis_index("dp") * plan.seq + place
    layers = qkv_weight.shape[0]
    inner = up_weight.shape[2]
    own_rows = qkv_weight.shape[1]
    short_rows = shorts * block_rows
    half = width // 2
    half_up = inner // 2
    core = place % 2
    table = plan.tables()
    chips = plan.chips

    per_row = inner // width

    def whole(array):
        return lax.all_gather(array, AXES, axis=0, tiled=True)

    def packed(layer):
        up = up_weight[layer].reshape(own_rows, plan.devices, per_row, own_rows)
        up = up.transpose(0, 2, 1, 3).reshape(own_rows, inner)
        down = down_weight[layer].reshape(per_row, own_rows, width).transpose(1, 0, 2)
        return [out_weight[layer], up, down.reshape(own_rows, inner)]

    def small(layer):
        biases = up_bias[layer].reshape(per_row, own_rows).T
        return jnp.concatenate(
            [vectors[layer], biases, jnp.zeros((own_rows, SMALL - 8 - per_row), BF16)], axis=1
        )

    sources = []
    for layer in range(layers):
        w_out, w_up, w_down = packed(layer)
        if layer == 0:
            parts = [w_out, w_up, w_down, qkv_weight[0]] + [small(which) for which in range(layers)]
            starts, qkv_start, pieces = (0, width, width + inner), width + 2 * inner, ()
        elif plan.staged:
            parts = [w_out, w_up, w_down]
            starts, qkv_start = (0, width, width + inner), None
            sides = (qkv_weight[layer][:, : 3 * half], qkv_weight[layer][:, 3 * half :])
            pieces = gather(plan, *sides, core)
        else:
            parts = [w_out, w_up, w_down, qkv_weight[layer]]
            starts, qkv_start, pieces = (0, width, width + inner), width + 2 * inner, ()
        rows = jnp.concatenate(parts, axis=1)
        if layer > 0:
            rows = after(rows, sources[-1].packed, *pieces)
        sources.append(Source(rows, whole(rows), pieces, starts, qkv_start))

    smalls = sources[0].packed[:, 4 * width + 2 * inner :].astype(F32)
    ordered = smalls.reshape(width, layers, SMALL).transpose(1, 2, 0)
    vecs = [ordered[layer, :16] for layer in range(layers)]

    block_ids = jnp.arange(blocks, dtype=jnp.int32)
    near_ids = block_ids ^ place
    placed_ids = block_order[0]
    own_block = jnp.sum(jnp.where(block_ids == place, placed_ids, 0))
    near_int = (near_ids[:, None] == block_ids[None, :]).astype(jnp.int32)
    near_true = jnp.sum(near_int * placed_ids[None, :], axis=1)
    own_hot = (block_ids == own_block).astype(F32)
    near_hot_int = (near_true[:, None] == block_ids[None, :]).astype(jnp.int32)
    near_hot = near_hot_int.astype(F32)
    mask_row = jnp.sum(block_mask[0] * (block_ids == own_block).astype(jnp.int32)[:, None], axis=0)
    opened = jnp.maximum(
        jnp.sum(near_hot_int * mask_row[None, :], axis=1), (block_ids == 0).astype(jnp.int32)
    )
    first_hot = (block_ids == 0).astype(F32)
    corner = first_hot[:, None] * first_hot[None, :]
    highest = lax.Precision.HIGHEST
    logit_near = jnp.einsum(
        "lhij,i,sj->lsh", mask_logit + gate_noise[:, 0], own_hot, near_hot, precision=highest
    )
    gate_long = jax.nn.sigmoid(logit_near)
    gate_short = jax.nn.sigmoid(mask_logit[:, None, :, 0, 0] + short_noise)
    lanes_long = jnp.repeat(gate_long, HEAD, axis=2)
    lanes_short = jnp.repeat(gate_short, HEAD, axis=2)[:, :, None, :]
    head_hot = (jnp.arange(width)[:, None] // HEAD == jnp.arange(HEADS)[None, :]).astype(F32)

    def swap_core(value):
        return lax.ppermute(value, "seq", [(i, i ^ 1) for i in range(blocks)])

    def swap_pair(value):
        return lax.ppermute(value, "seq", [(i, i ^ 2) for i in range(blocks)])

    rows_low = (short_tokens.reshape(short_rows, width), long_tokens[0])
    rows_wide = rows_low
    saved = []
    for layer in range(layers):
        source = sources[layer]
        vec = vecs[layer]
        if layer == 0:
            vec = after(vec, *[piece for later in sources[1:] for piece in later.pieces])
        qkv_short, query_long, kv = project(table, *rows_low, vec, source.qkv(), source.qkv_start)
        kv_core = swap_core(kv)
        kv_pair = swap_pair(kv)
        mixed_short, raised_short, inverse_short = short_forward(qkv_short, lanes_short[layer])
        kv_pair = after(kv_pair, mixed_short)
        key_values = (kv, kv_core, kv_pair, swap_core(kv_pair))
        mixed_long, raised_long, inverse_long, parts = long_forward(
            opened, query_long, lanes_long[layer], key_values
        )
        *y, hid_low, unit1, scale1, unit2, scale2, act, slope = mlp_forward(
            layer + 1 < layers, *rows_wide, mixed_short, mixed_long, vec, inner, source
        )
        saved.append(
            (
                rows_low,
                qkv_short,
                query_long,
                key_values,
                mixed_short,
                raised_short,
                inverse_short,
                mixed_long,
                raised_long,
                inverse_long,
                parts,
                vec,
                hid_low,
                unit1,
                scale1,
                unit2,
                scale2,
                act,
                slope,
            )
        )
        rows_low, rows_wide = y[2:], y[:2]
    outputs = rows_low

    grad = (short_cotangent.reshape(short_rows, width), long_cotangent[0])
    kept = []
    terms = []
    upper = None
    staging = plan.staged
    for layer in reversed(range(layers)):
        last = layer == 0
        source = sources[layer]
        (
            rows_low,
            qkv_short,
            query_long,
            key_values,
            mixed_short,
            raised_short,
            inverse_short,
            mixed_long,
            raised_long,
            inverse_long,
            parts,
            vec,
            hid_low,
            unit1,
            scale1,
            unit2,
            scale2,
            act,
            slope,
        ) = saved[layer]
        second, d_out, sums_ffn, sums_up, d_up = ffn_backward(grad, unit2, scale2, vec, slope, source)
        if upper is not None:
            if staging:
                ffn_upper.wait(d_out)
                ffn_upper.line()
                upper[2] = after(upper[2], ffn_upper.operand, d_out)
            *att, columns = att_grads(table, chips, *upper)
            terms[-1][0] = columns
            if staging:
                att_upper = Reduce(plan, *att)
                d_out = after(d_out, *att)
            kept[-1].append(att_upper if staging else att)
        ffn = ffn_grads(table, chips, act, d_out, hid_low, d_up)
        second = after(second, *ffn)
        if staging:
            if upper is not None:
                att_upper.wait(ffn[0])
                att_upper.second()
                second = after(second, att_upper.operand, *ffn_upper.pending)
            ffn_sum = Reduce(plan, *ffn)
        d_first, d_att, d_mixed_short, d_mixed_long, sums_mid = mid_backward(
            second, d_up, unit1, scale1, vec, source, short_rows
        )
        if staging and upper is not None:
            att_upper.wait(d_att)
            att_upper.first()
            d_mixed_long = after(d_mixed_long, att_upper.operand)
        d_query, d_own, d_near, d_core, gate_sum_long = long_backward(
            query_long, mixed_long, d_mixed_long, raised_long, inverse_long, parts, lanes_long[layer], key_values
        )
        far = swap_core(d_core)
        away = (d_near.astype(F32) + far[1].astype(F32)).astype(BF16)
        passed = swap_pair(away)
        if staging:
            ffn_sum.wait(d_query, away)
            ffn_sum.second(passed)
            d_mixed_short = after(d_mixed_short, ffn_sum.operand)
            if upper is not None:
                att_upper.wait(d_query)
                att_upper.line()
                d_mixed_short = after(d_mixed_short, att_upper.operand)
        d_short, gate_sum_short = short_backward(
            qkv_short, mixed_short, d_mixed_short, raised_short, inverse_short, lanes_short[layer]
        )
        if staging and upper is not None:
            d_att = after(d_att, *att_upper.pending)
        upper = [mixed_short, mixed_long, d_att, *rows_low, d_short, d_query, d_own, far, passed]
        kept.append([ffn_sum if staging else ffn])
        if last:
            *att, columns = att_grads(table, chips, *upper)
            d_first = after(d_first, *att)
            if staging:
                att_sum = Reduce(plan, *att)
                ffn_sum.wait(att[0])
                ffn_sum.first()
                d_first = after(d_first, ffn_sum.operand)
            kept[-1].append(att_sum if staging else att)
        grad = input_grad(
            table,
            d_short,
            d_query,
            d_own,
            far,
            passed,
            d_first,
            source.qkv(),
            source.qkv_start,
            BF16 if last else F32,
        )
        if staging:
            ffn_sum.wait(grad[0])
            if last:
                ffn_sum.line()
                att_sum.wait(grad[0])
                att_sum.second()
            else:
                ffn_sum.first()
                grad = (after(grad[0], ffn_sum.operand), grad[1])
                ffn_upper = ffn_sum
        heads = jnp.dot(
            jnp.concatenate([gate_sum_short[:, 0], gate_sum_long]), head_hot, precision=highest
        )
        short_term = jnp.sum(heads[:shorts] * (1.0 - gate_short[layer]), axis=0)
        long_term = heads[shorts:] * (1.0 - gate_long[layer])
        logit_term = (
            jnp.einsum("sh,i,sj->hij", long_term, own_hot, near_hot, precision=highest)
            + short_term[:, None, None] * corner[None]
        )
        terms.append([columns if last else None, sums_mid[2:5], sums_ffn[5:8], sums_up, logit_term])
    kept, terms = kept[::-1], terms[::-1]

    packed_sums = jnp.concatenate(
        [
            jnp.concatenate(
                [
                    rows
                    for columns, mid, ffn, _, _ in terms
                    for rows in (columns[:, :width], columns[:, 2 * width :], mid, ffn)
                ]
            ).reshape(-1, 128),
            jnp.concatenate([term[3] for term in terms]).reshape(-1, 128),
            jnp.stack([term[4] for term in terms]).reshape(-1, 128),
        ]
    )
    count = packed_sums.shape[0]
    packed_sums = jnp.pad(packed_sums, ((0, -count % 8), (0, 0)))
    if staging:
        ffn_sum, att_sum = kept[0]
        sums = Butterfly(plan, packed_sums)
        sums.step()
        sums.step(ffn_sum.operand, att_sum.operand)
        att_sum.first()
        sums.step(att_sum.operand)
        att_sum.wait(*ffn_sum.pending)
        att_sum.line()
        sums.step(att_sum.operand)
        sums.step(*ffn_sum.pending)
        packed_sums = sums.finish()
    else:
        packed_sums = lax.psum(packed_sums, AXES)
    edge = layers * 8 * width // 128
    more = edge + layers * inner // 128
    vectors_all = packed_sums[:edge].reshape(layers, 8, width)
    vectors_grad = lax.dynamic_slice_in_dim(vectors_all, device * own_rows, own_rows, 2).transpose(0, 2, 1)
    bias_all = packed_sums[edge:more].reshape(layers, per_row, width)
    up_bias_grad = lax.dynamic_slice_in_dim(bias_all, device * own_rows, own_rows, 2).reshape(layers, -1)
    logit_grad = packed_sums[more:count].reshape(mask_logit.shape)

    def scattered(sides):
        rows = jnp.concatenate([side.reshape(width, side.shape[-1]) for side in sides], axis=1)
        rows = lax.psum_scatter(rows, AXES, scatter_dimension=0, tiled=True).astype(F32)
        count = rows.shape[1] // 2
        return rows[:, :count], rows[:, count:]

    def owned(total):
        part = [lax.dynamic_slice_in_dim(total, which * own_rows, own_rows, 0) for which in (core, 1 - core)]
        mine, got = part[0], send(part[1], plan.cores)
        return jnp.where(core == 0, mine, got), jnp.where(core == 0, got, mine)

    qkv_grad, out_grad, up_grad, down_grad = [], [], [], []
    for layer in range(layers):
        ffn, att = kept[layer]
        if staging:
            ffn, att = ffn.finish(), att.finish()
            ffn, att = owned(ffn), owned(att)
        else:
            ffn, att = scattered(ffn), scattered(att)
        span = per_row * half
        down = [side[:, :span].reshape(own_rows, per_row, half) for side in ffn]
        down = jnp.concatenate(down, axis=2).transpose(1, 0, 2)
        down_grad.append(down.reshape(per_row * own_rows, width))
        up = jnp.concatenate([side[:, span:] for side in ffn], axis=1)
        up = up.reshape(own_rows, per_row, plan.devices, own_rows).transpose(0, 2, 1, 3)
        up_grad.append(up.reshape(own_rows, inner))
        out_grad.append(jnp.concatenate([side[:, :half] for side in att], axis=1))
        qkv_grad.append(jnp.concatenate([side[:, half:] for side in att], axis=1))
    return (
        outputs[0].reshape(shorts, block_rows, width),
        outputs[1][None],
        grad[0].reshape(shorts, block_rows, width),
        grad[1][None],
        jnp.stack(qkv_grad),
        jnp.stack(out_grad),
        jnp.stack(up_grad),
        jnp.stack(down_grad),
        vectors_grad,
        up_bias_grad,
        logit_grad,
    )


def solution(mesh):
    split = ("dp", "seq")
    in_specs = (
        P(split, None, None),
        P("dp", "seq", None),
        P(split, None, None),
        P("dp", "seq", None),
        P(None, split, None),
        P(None, split, None),
        P(None, split, None),
        P(None, split, None),
        P(None, split, None),
        P(None, split),
        P(),
        P(None, split, None),
        P(None, "dp", None, None, None),
        P("dp", None, None),
        P("dp", None),
    )
    out_specs = (
        P(split, None, None),
        P("dp", "seq", None),
        P(split, None, None),
        P("dp", "seq", None),
        P(None, split, None),
        P(None, split, None),
        P(None, split, None),
        P(None, split, None),
        P(None, split, None),
        P(None, split),
        P(),
    )

    def build(*arrays):
        plan = Plan(mesh, arrays[4].shape[1])
        return jax.shard_map(
            functools.partial(on_device, plan),
            mesh=mesh,
            in_specs=in_specs,
            out_specs=out_specs,
            check_vma=False,
        )(*arrays)

    return build
```

```python
import functools

import jax
import jax.numpy as jnp
from jax import lax
from jax.experimental import pallas as pl
from jax.experimental.pallas import tpu as pltpu
from jax.sharding import PartitionSpec as P

HEADS = 12
HEAD = 64
BLOCK = 128
AXES = ("dp", "seq")
BF16 = jnp.bfloat16
F32 = jnp.float32
VMEM = pl.BlockSpec(memory_space=pltpu.VMEM)
SMEM = pl.BlockSpec(memory_space=pltpu.SMEM)
ANY = pl.BlockSpec(memory_space=pl.ANY)
SMALL = 128
ROOT_HALF = 0.7071067811865476
ROOT_TWO_PI_INV = 0.3989422804014327


def sds(shape, dtype):
    return jax.ShapeDtypeStruct(shape, dtype)


def params(mib=60):
    return pltpu.CompilerParams(vmem_limit_bytes=mib * 2**20)


def cost(us):
    return pl.CostEstimate(flops=int(us * 0.7e9), bytes_accessed=int(us * 3.3e6), transcendentals=0)


def dot(left, right):
    return jnp.dot(left, right, preferred_element_type=F32)


def dot_rt(left, right):
    return lax.dot_general(left, right, (((1,), (1,)), ((), ())), preferred_element_type=F32)


def dot_lt(left, right):
    return lax.dot_general(left, right, (((0,), (0,)), ((), ())), preferred_element_type=F32)


class Plan:
    def __init__(self, mesh, width):
        dp, seq = mesh.shape["dp"], mesh.shape["seq"]
        self.dp, self.seq, self.devices = dp, seq, dp * seq
        depth = dp // 2
        chips = depth * 4
        self.staged = (
            seq == 4
            and dp % 2 == 0
            and depth & (depth - 1) == 0
            and width % chips == 0
            and (width // chips) % 16 == 0
        )
        self.depth, self.chips = depth, chips if self.staged else 16
        if self.staged:
            self.z_perms = [self.flip(z=step) for step in range(1, depth)]
            self.first = self.flip_by_core((0, 1), (1, 0))
            self.second = self.flip_by_core((1, 0), (0, 1))
            self.cores = self.flip(core=1)

    def flip(self, z=0, x=0, y=0, core=0):
        pairs = []
        for dev in range(self.devices):
            pairs.append((dev, dev ^ (z * 8 + x * 4 + y * 2 + core)))
        return pairs

    def flip_by_core(self, even, odd):
        pairs = []
        for dev in range(self.devices):
            x, y = even if dev % 2 == 0 else odd
            pairs.append((dev, dev ^ (x * 4 + y * 2)))
        return pairs

    def tables(self):
        slots = jnp.arange(self.chips, dtype=jnp.int32)
        if not self.staged:
            return jnp.concatenate([slots, slots, jnp.zeros((8,), jnp.int32), slots, slots])
        me = lax.axis_index("dp") * 4 + lax.axis_index("seq")
        core, chip = me % 2, me // 2
        away = slots ^ chip
        z, x, y = away // 4, (away // 2) % 2, away % 2
        y_slot = (x * 2 + y) * self.depth + z
        x_slot = (y * 2 + x) * self.depth + z
        steps, a, b = slots % self.depth, (slots // self.depth) % 2, slots // (2 * self.depth)
        y_chip = (steps * 4 + b * 2 + a) ^ chip
        x_chip = (steps * 4 + a * 2 + b) ^ chip
        even = core == 0
        return jnp.concatenate(
            [
                jnp.where(even, y_slot, x_slot),
                jnp.where(even, x_slot, y_slot),
                jnp.full((8,), core, jnp.int32),
                jnp.where(even, y_chip, x_chip),
                jnp.where(even, x_chip, y_chip),
            ]
        ).astype(jnp.int32)


def gather(plan, first, second, core):
    even = core == 0
    got = send(jnp.where(even, second, first), plan.cores)
    mine = jnp.where(even, first, second)
    base = jnp.where(even, jnp.concatenate([mine, got]), jnp.concatenate([got, mine]))
    line = jnp.stack([base] + [send(base, pairs) for pairs in plan.z_perms])
    near = jnp.concatenate([line, send(line, plan.first)])
    far = send(near, plan.second)
    return (near, far, send(near, plan.cores), send(far, plan.cores))


def send(value, pairs):
    return lax.ppermute(value, AXES, pairs)


def after(value, *earlier):
    return lax.optimization_barrier((value, *earlier))[0]


class Reduce:
    def __init__(self, plan, own, other):
        self.plan, self.own = plan, own
        self.part = plan.chips // 2
        self.quarter = self.part // 2
        self.pending = send(other, plan.cores)

    def wait(self, *values):
        if isinstance(self.pending, list):
            self.pending = [after(value, *values) for value in self.pending]
        else:
            self.pending = after(self.pending, *values)

    def second(self, *earlier):
        part = self.part
        self.got = self.pending
        away = self.own[part:].astype(F32) + self.got[part:].astype(F32)
        self.operand = after(away.astype(BF16), *earlier) if earlier else away.astype(BF16)
        self.pending = send(self.operand, self.plan.second)

    def first(self):
        part, quarter = self.part, self.quarter
        self.got_b = self.pending
        near = self.own[quarter:part].astype(F32) + self.got[quarter:part].astype(F32)
        near = near + self.got_b[quarter:].astype(F32)
        self.operand = near.astype(BF16)
        self.pending = send(self.operand, self.plan.first)

    def line(self):
        quarter = self.quarter
        line = self.own[:quarter].astype(F32) + self.got[:quarter].astype(F32)
        line = line + self.got_b[:quarter].astype(F32) + self.pending.astype(F32)
        low = line.astype(BF16)
        self.total = line[0]
        self.operand = lax.optimization_barrier(tuple(low[step] for step in range(1, self.plan.depth)))
        self.pending = [send(part, pairs) for part, pairs in zip(self.operand, self.plan.z_perms)]

    def finish(self):
        total = self.total
        for value in self.pending:
            total = total + value.astype(F32)
        return total


class Butterfly:
    def __init__(self, plan, value):
        self.plan, self.value, self.bit, self.pending = plan, value, 1, None

    def step(self, *earlier):
        if self.pending is not None:
            self.value = self.value + after(self.pending, *earlier)
        self.pending = None
        if self.bit < self.plan.devices:
            pairs = [(dev, dev ^ self.bit) for dev in range(self.plan.devices)]
            self.pending = send(self.value, pairs)
            self.bit *= 2

    def finish(self):
        while self.pending is not None:
            self.step()
        return self.value


class Copies:
    def __init__(self, sems):
        self.sems, self.count = sems, 0

    def start(self, source, target):
        copy = pltpu.make_async_copy(source, target, self.sems.at[self.count])
        self.count += 1
        copy.start()
        return copy


def wait_all(copies):
    for copy in copies:
        copy.wait()


def load_staged(copies, table, pieces, low, high, target):
    begun = []
    slots, rows, _ = pieces[0].shape
    count = 2 * slots
    core = table[2 * count]
    for place, piece in enumerate(pieces):
        half = core if place < 2 else 1 - core
        lanes = pl.ds(pl.multiple_of(half * (high - low), 128), high - low)
        for slot in range(slots):
            chip = table[2 * count + 8 + place * slots + slot]
            here = pl.ds(pl.multiple_of(chip * rows, 16), rows)
            begun.append(copies.start(piece.at[slot, :, low:high], target.at[here, lanes]))
    return begun


def project_kernel(start, given, table, rows_short, rows_long, *rest):
    if given:
        vec, *weights_in, out_short, out_query, out_kv, rows, weight, out, small, sems = rest
    else:
        *weights_in, out_short, out_query, out_kv, vec, rows, weight, out, small, sems = rest
    copies = Copies(sems)
    short, width = rows_short.shape
    begun = [
        copies.start(rows_short, rows.at[:short, :]),
        copies.start(rows_long, rows.at[short:, :]),
    ]
    loads = []
    half = 3 * width // 2
    if len(weights_in) > 1:
        begun += load_staged(copies, table, weights_in, 0, half, weight)
        if not given:
            begun += load_staged(copies, table, weights_in, half, half + SMALL, small)
    else:
        if not given:
            here = slice(start + 3 * width, start + 3 * width + small.shape[1])
            begun.append(copies.start(weights_in[0].at[:, here], small))
        for part in range(3):
            here = slice(start + part * width, start + (part + 1) * width)
            loads.append(
                copies.start(weights_in[0].at[:, here], weight.at[:, part * width : (part + 1) * width])
            )
    wait_all(begun)
    if not given:
        turned = small[...].T
        for layer in range(small.shape[1] // SMALL):
            vec[layer] = turned[layer * SMALL : layer * SMALL + 16, :].astype(F32)
        first = vec.at[0]
    else:
        first = vec
    done = []
    for part in range(3):
        lanes = slice(part * width, (part + 1) * width)
        wait_all(loads[part : part + 1])
        result = dot(rows[...], weight[:, lanes])
        if part != 1:
            result = result + first[part // 2 : part // 2 + 1, :]
        out[:, lanes] = result.astype(BF16)
        if part == 0:
            target = out_query
        else:
            target = out_kv.at[:, (part - 1) * width : part * width]
        done.append(copies.start(out.at[short:, lanes], target))
        done.append(copies.start(out.at[:short, lanes], out_short.at[:, lanes]))
    wait_all(done)


def project(table, rows_short, rows_long, vec, layers, weights, start):
    short, width = rows_short.shape
    count = short + rows_long.shape[0]
    given = vec is not None
    return pl.pallas_call(
        functools.partial(project_kernel, start, given),
        out_shape=[
            sds((short, 3 * width), BF16),
            sds((count - short, width), BF16),
            sds((count - short, 2 * width), BF16),
        ]
        + ([] if given else [sds((layers, 16, width), F32)]),
        in_specs=[SMEM, ANY, ANY] + [VMEM] * given + [ANY] * len(weights),
        out_specs=[ANY] * 3 + [VMEM] * (not given),
        scratch_shapes=[
            pltpu.VMEM((count, width), BF16),
            pltpu.VMEM((width, 3 * width), BF16),
            pltpu.VMEM((count, 3 * width), BF16),
            pltpu.VMEM((width, layers * SMALL), BF16),
            pltpu.SemaphoreType.DMA((80,)),
        ],
        compiler_params=params(),
        cost_estimate=cost(10),
        name="project",
    )(table, rows_short, rows_long, *([vec] if given else []), *weights)


def head_masks():
    lane = lax.broadcasted_iota(jnp.int32, (BLOCK, BLOCK), 1)
    low = jnp.where(lane < HEAD, 1.0, 0.0).astype(BF16)
    high = jnp.where(lane < HEAD, 0.0, 1.0).astype(BF16)
    return low, high


def spread(pair, low, high):
    return jnp.concatenate([pair * low, pair * high], axis=0)


def short_forward_kernel(qkv, gate, mixed, raised, inverse):
    low, high = head_masks()
    ones = jnp.concatenate([low, high], axis=0)
    width = mixed.shape[1]
    for pair in range(HEADS // 2):
        lanes = slice(pair * 128, pair * 128 + 128)
        query = qkv[:, lanes] * 0.125
        keys = spread(qkv[:, width + pair * 128 : width + pair * 128 + 128], low, high)
        values = spread(qkv[:, 2 * width + pair * 128 : 2 * width + pair * 128 + 128], low, high)
        scores = dot_rt(query, keys)
        left, right = scores[:, :BLOCK], scores[:, BLOCK:]
        left = jnp.exp(left - jnp.max(left, axis=1, keepdims=True))
        right = jnp.exp(right - jnp.max(right, axis=1, keepdims=True))
        prob = jnp.concatenate([left, right], axis=1).astype(BF16)
        both = dot(prob, jnp.concatenate([values, ones], axis=1))
        inv = 1.0 / both[:, BLOCK:]
        raised[0, pair] = prob
        inverse[:, lanes] = inv
        mixed[:, lanes] = (both[:, :BLOCK] * inv * gate[0, :, lanes]).astype(BF16)


def short_forward(qkv, gate):
    rows = qkv.shape[0]
    width = qkv.shape[1] // 3
    count = rows // BLOCK
    pairs = HEADS // 2
    return pl.pallas_call(
        short_forward_kernel,
        grid=(count,),
        out_shape=[
            sds((rows, width), BF16),
            sds((count, pairs, BLOCK, 2 * BLOCK), BF16),
            sds((rows, width), F32),
        ],
        in_specs=[
            pl.BlockSpec((BLOCK, 3 * width), lambda i: (i, 0)),
            pl.BlockSpec((1, 1, width), lambda i: (i, 0, 0)),
        ],
        out_specs=[
            pl.BlockSpec((BLOCK, width), lambda i: (i, 0)),
            pl.BlockSpec((1, pairs, BLOCK, 2 * BLOCK), lambda i: (i, 0, 0, 0)),
            pl.BlockSpec((BLOCK, width), lambda i: (i, 0)),
        ],
        compiler_params=params(),
        cost_estimate=cost(7),
        name="short_forward",
    )(qkv, gate)


def long_forward_kernel(blocks, opened, queries, gate, *rest):
    sources, (mixed, raised, inverse, parts) = rest[:blocks], rest[blocks:]
    low, high = head_masks()
    ones = jnp.concatenate([low, high], axis=0)
    width = mixed.shape[1]
    for pair in range(HEADS // 2):
        lanes = slice(pair * 128, pair * 128 + 128)
        query = queries[:, lanes] * 0.125
        scores, values = [], []
        for index in range(blocks):
            source = sources[index]
            keys = spread(source[:, lanes], low, high)
            values.append(spread(source[:, width + pair * 128 : width + pair * 128 + 128], low, high))
            score = dot_rt(query, keys)
            scores.append(jnp.where(opened[index] > 0, score, -1e30))
        top = functools.reduce(jnp.maximum, scores)
        top_left = jnp.max(top[:, :BLOCK], axis=1, keepdims=True)
        top_right = jnp.max(top[:, BLOCK:], axis=1, keepdims=True)
        both = []
        for index in range(blocks):
            left = jnp.exp(scores[index][:, :BLOCK] - top_left)
            right = jnp.exp(scores[index][:, BLOCK:] - top_right)
            prob = jnp.concatenate([left, right], axis=1).astype(BF16)
            raised[pair, index] = prob
            both.append(dot(prob, jnp.concatenate([values[index], ones], axis=1)))
        inv = 1.0 / sum(value[:, BLOCK:] for value in both)
        inverse[:, lanes] = inv
        total = 0.0
        for index in range(blocks):
            part = both[index][:, :BLOCK] * inv
            parts[index, :, lanes] = part.astype(BF16)
            total = total + part * gate[index : index + 1, lanes]
        mixed[:, lanes] = total.astype(BF16)


def long_forward(opened, queries, gate, sources):
    rows, width = queries.shape
    blocks = len(sources)
    return pl.pallas_call(
        functools.partial(long_forward_kernel, blocks),
        out_shape=[
            sds((rows, width), BF16),
            sds((HEADS // 2, blocks, BLOCK, 2 * BLOCK), BF16),
            sds((rows, width), F32),
            sds((blocks, rows, width), BF16),
        ],
        in_specs=[SMEM, VMEM, VMEM] + [VMEM] * blocks,
        out_specs=[VMEM] * 4,
        compiler_params=params(),
        cost_estimate=cost(5.3),
        name="long_forward",
    )(opened, queries, gate, *sources)


def norm_rows(rows, gain, shift):
    inverse = 1.0 / rows.shape[1]
    center = rows - jnp.sum(rows, axis=1, keepdims=True) * inverse
    spread_ = jnp.sum(center * center, axis=1, keepdims=True) * inverse
    scale = lax.rsqrt(spread_ + 1e-05)
    unit = center * scale
    return unit, scale, unit * gain + shift


def mlp_forward_kernel(
    wide,
    starts,
    rows_short,
    rows_long,
    mixed_short,
    mixed_long,
    vec,
    packed,
    *rest,
):
    (
        y_short,
        y_long,
        y_low_short,
        y_low_long,
        hid_low_out,
        unit1_out,
        scale1,
        unit2_out,
        scale2,
        act_out,
        slope_out,
        weight_out,
        weight_up,
        weight_down,
        mixed,
        hidden,
        hid_low,
        unit,
        y_low,
        act,
        slope,
        sems,
        sem_w,
        sem_o,
        sem_y,
    ) = rest
    out_start, up_start, down_start = starts
    copies = Copies(sems)
    total, width = hidden.shape
    inner = act.shape[1]
    short = rows_short.shape[0]
    tile = width
    steps = inner // tile
    begun = [
        copies.start(mixed_short, mixed.at[:short, :]),
        copies.start(mixed_long, mixed.at[short:, :]),
        copies.start(packed.at[:, out_start : out_start + width], weight_out),
    ]
    downs = []
    for step in range(steps):
        lanes = slice(step * tile, (step + 1) * tile)
        here = slice(up_start + step * tile, up_start + (step + 1) * tile)
        pltpu.make_async_copy(packed.at[:, here], weight_up.at[:, lanes], sem_w.at[step]).start()
    for group in range(inner // width):
        start = down_start + group * width
        downs.append(
            copies.start(packed.at[:, start : start + width], weight_down.at[group * width : (group + 1) * width, :])
        )
    wait_all(begun)
    for step in range(width // 256):
        lanes = slice(step * 256, step * 256 + 256)
        summed = dot(mixed[...], weight_out[:, lanes]) + vec[2:3, lanes]
        hidden[:short, lanes] = summed[:short] + rows_short[:, lanes].astype(F32)
        hidden[short:, lanes] = summed[short:] + rows_long[:, lanes].astype(F32)

    @pl.loop(0, total // BLOCK)
    def _(step):
        here = pl.ds(pl.multiple_of(step * BLOCK, BLOCK), BLOCK)
        level, scale, hid = norm_rows(hidden[here, :], vec[3:4, :], vec[4:5, :])
        unit[here, :] = level.astype(BF16)
        scale1[here, :] = scale
        hidden[here, :] = hid
        hid_low[here, :] = hid.astype(BF16)

    done = [copies.start(unit, unit1_out), copies.start(hid_low, hid_low_out)]

    @pl.loop(0, steps)
    def _(step):
        place = pl.ds(pl.multiple_of(step * tile, tile), tile)
        pltpu.make_async_copy(weight_up.at[:, place], weight_up.at[:, place], sem_w.at[step]).wait()
        upper = dot(hid_low[...], weight_up[:, place]) + vec[pl.ds(8 + step, 1), :]
        below = 0.5 + 0.5 * lax.erf(upper * ROOT_HALF)
        act[:, place] = (upper * below).astype(BF16)
        bell = ROOT_TWO_PI_INV * jnp.exp(-0.5 * upper * upper)
        slope[:, place] = (below + upper * bell).astype(BF16)
        pltpu.make_async_copy(act.at[:, place], act_out.at[:, place], sem_o.at[0, step]).start()
        pltpu.make_async_copy(slope.at[:, place], slope_out.at[:, place], sem_o.at[1, step]).start()

    wait_all(downs)
    for step in range(width // 256):
        lanes = slice(step * 256, step * 256 + 256)
        hidden[:, lanes] = hidden[:, lanes] + dot(act[...], weight_down[:, lanes]) + vec[5:6, lanes]
    wait_all(done)

    @pl.loop(0, total // BLOCK)
    def _(step):
        here = pl.ds(pl.multiple_of(step * BLOCK, BLOCK), BLOCK)
        level, scale, y = norm_rows(hidden[here, :], vec[6:7, :], vec[7:8, :])
        unit[here, :] = level.astype(BF16)
        scale2[here, :] = scale
        hidden[here, :] = y
        y_low[here, :] = y.astype(BF16)
        if wide:

            @pl.when(step < short // BLOCK)
            def _():
                pltpu.make_async_copy(hidden.at[here, :], y_short.at[here, :], sem_y.at[step]).start()

    done = [
        copies.start(unit, unit2_out),
        copies.start(y_low.at[:short, :], y_low_short),
        copies.start(y_low.at[short:, :], y_low_long),
    ]
    if wide:
        done.append(copies.start(hidden.at[short:, :], y_long))

        @pl.loop(0, short // BLOCK)
        def _(step):
            here = pl.ds(pl.multiple_of(step * BLOCK, BLOCK), BLOCK)
            pltpu.make_async_copy(hidden.at[here, :], y_short.at[here, :], sem_y.at[step]).wait()

    @pl.loop(0, steps)
    def _(step):
        place = pl.ds(pl.multiple_of(step * tile, tile), tile)
        pltpu.make_async_copy(act.at[:, place], act_out.at[:, place], sem_o.at[0, step]).wait()
        pltpu.make_async_copy(slope.at[:, place], slope_out.at[:, place], sem_o.at[1, step]).wait()

    wait_all(done)


def mlp_forward(wide, rows_short, rows_long, mixed_short, mixed_long, vec, inner, source):
    rows = rows_short.shape[0] + rows_long.shape[0]
    width = rows_short.shape[1]
    return pl.pallas_call(
        functools.partial(mlp_forward_kernel, wide, source.starts),
        out_shape=[
            sds(rows_short.shape if wide else (8, 128), F32),
            sds(rows_long.shape if wide else (8, 128), F32),
            sds(rows_short.shape, BF16),
            sds(rows_long.shape, BF16),
            sds((rows, width), BF16),
            sds((rows, width), BF16),
            sds((rows, 1), F32),
            sds((rows, width), BF16),
            sds((rows, 1), F32),
            sds((rows, inner), BF16),
            sds((rows, inner), BF16),
        ],
        in_specs=[VMEM, VMEM, ANY, ANY, VMEM, ANY],
        out_specs=[ANY] * 6 + [VMEM, ANY, VMEM, ANY, ANY],
        scratch_shapes=[
            pltpu.VMEM((width, width), BF16),
            pltpu.VMEM((width, inner), BF16),
            pltpu.VMEM((inner, width), BF16),
            pltpu.VMEM((rows, width), BF16),
            pltpu.VMEM((rows, width), F32),
            pltpu.VMEM((rows, width), BF16),
            pltpu.VMEM((rows, width), BF16),
            pltpu.VMEM((rows, width), BF16),
            pltpu.VMEM((rows, inner), BF16),
            pltpu.VMEM((rows, inner), BF16),
            pltpu.SemaphoreType.DMA((24,)),
            pltpu.SemaphoreType.DMA((inner // width,)),
            pltpu.SemaphoreType.DMA((2, inner // width)),
            pltpu.SemaphoreType.DMA((rows // BLOCK,)),
        ],
        compiler_params=params(),
        cost_estimate=cost(28),
        name="mlp_forward",
    )(rows_short, rows_long, mixed_short, mixed_long, vec, source.packed)


def norm_back(grad, unit, scale, gain):
    inverse = 1.0 / grad.shape[1]
    pulled = grad * gain
    mean = jnp.sum(pulled, axis=1, keepdims=True) * inverse
    along = jnp.sum(pulled * unit, axis=1, keepdims=True) * inverse
    return scale * (pulled - mean - unit * along)


def ffn_backward_kernel(
    down_start,
    grad_short,
    grad_long,
    unit2,
    scale2,
    vec,
    slope_in,
    packed,
    second_out,
    d_out_out,
    sums,
    sums_up,
    d_up_out,
    weight,
    second,
    d_out,
    slope,
    d_up,
    sems,
    sem_w,
    sem_s,
    sem_o,
):
    copies = Copies(sems)
    total, width = second.shape
    inner = slope.shape[1]
    short = grad_short.shape[0]
    tile = 512
    steps = inner // tile
    loads = []
    for group in range(inner // width):
        start = down_start + group * width
        loads.append(
            copies.start(packed.at[:, start : start + width], weight.at[group * width : (group + 1) * width, :])
        )
    for step in range(steps):
        lanes = slice(step * tile, (step + 1) * tile)
        pltpu.make_async_copy(slope_in.at[:, lanes], slope.at[:, lanes], sem_s.at[step]).start()
    sums[...] = jnp.zeros_like(sums)

    def begin(here, grad):
        dy = grad.astype(F32)
        unit = unit2[here, :].astype(F32)
        dr = norm_back(dy, unit, scale2[here, :], vec[6:7, :])
        second[here, :] = dr
        low = dr.astype(BF16)
        d_out[here, :] = low
        sums[5:6, :] += jnp.sum(low.astype(F32), axis=0, keepdims=True)
        sums[6:7, :] += jnp.sum(dy * unit, axis=0, keepdims=True)
        sums[7:8, :] += jnp.sum(dy, axis=0, keepdims=True)

    @pl.loop(0, short // BLOCK)
    def _(step):
        here = pl.ds(pl.multiple_of(step * BLOCK, BLOCK), BLOCK)
        begin(here, grad_short[here, :])

    begin(slice(short, total), grad_long[...])
    done = [copies.start(second, second_out), copies.start(d_out, d_out_out)]
    wait_all(loads)

    @pl.loop(0, steps)
    def _(step):
        place = pl.ds(pl.multiple_of(step * tile, tile), tile)
        pltpu.make_async_copy(slope_in.at[:, place], slope.at[:, place], sem_s.at[step]).wait()
        low = (dot_rt(d_out[...], weight[place, :]) * slope[:, place].astype(F32)).astype(BF16)
        d_up[:, place] = low
        sums_up[:, place] = jnp.sum(low.astype(F32), axis=0, keepdims=True)
        pltpu.make_async_copy(d_up.at[:, place], d_up_out.at[:, place], sem_o.at[step]).start()

    @pl.loop(0, steps)
    def _(step):
        place = pl.ds(pl.multiple_of(step * tile, tile), tile)
        pltpu.make_async_copy(d_up.at[:, place], d_up_out.at[:, place], sem_o.at[step]).wait()

    wait_all(done)


def ffn_backward(grad, unit2, scale2, vec, slope, source):
    rows, width = unit2.shape
    inner = slope.shape[1]
    return pl.pallas_call(
        functools.partial(ffn_backward_kernel, source.starts[2]),
        out_shape=[
            sds((rows, width), F32),
            sds((rows, width), BF16),
            sds((8, width), F32),
            sds((1, inner), F32),
            sds((rows, inner), BF16),
        ],
        in_specs=[VMEM] * 5 + [ANY, ANY],
        out_specs=[ANY, ANY, VMEM, VMEM, ANY],
        scratch_shapes=[
            pltpu.VMEM((inner, width), BF16),
            pltpu.VMEM((rows, width), F32),
            pltpu.VMEM((rows, width), BF16),
            pltpu.VMEM((rows, inner), BF16),
            pltpu.VMEM((rows, inner), BF16),
            pltpu.SemaphoreType.DMA((inner // width + 2,)),
            pltpu.SemaphoreType.DMA((1,)),
            pltpu.SemaphoreType.DMA((inner // 512,)),
            pltpu.SemaphoreType.DMA((inner // 512,)),
        ],
        compiler_params=params(),
        cost_estimate=cost(14),
        name="ffn_backward",
    )(*grad, unit2, scale2, vec, slope, source.packed)


def mid_backward_kernel(starts, second_in, d_up_in, unit1_in, scale1, vec, packed, *rest):
    (
        d_first_out,
        d_att_out,
        d_mixed_short,
        d_mixed_long,
        sums,
        weight_out,
        weight_up,
        second,
        partial,
        unit1,
        d_up,
        d_att,
        d_mixed,
        sems,
    ) = rest
    out_start, up_start, _ = starts
    copies = Copies(sems)
    total, width = second.shape
    inner = d_up.shape[1]
    short = d_mixed_short.shape[0]
    spans = [slice(0, width), slice(width, inner)]
    loads = []
    for span in spans:
        here = slice(up_start + span.start, up_start + span.stop)
        loads.append(
            [
                copies.start(d_up_in.at[:, span], d_up.at[:, span]),
                copies.start(packed.at[:, here], weight_up.at[:, span]),
            ]
        )
    rest = [
        copies.start(second_in, second),
        copies.start(unit1_in, unit1),
        copies.start(packed.at[:, out_start : out_start + width], weight_out),
    ]
    sums[...] = jnp.zeros_like(sums)
    for part, span in enumerate(spans):
        wait_all(loads[part])
        for step in range(width // 256):
            lanes = slice(step * 256, step * 256 + 256)
            piece = dot_rt(d_up[:, span], weight_up[lanes, span])
            partial[:, lanes] = piece if part == 0 else partial[:, lanes] + piece
    wait_all(rest)

    @pl.loop(0, total // BLOCK)
    def _(step):
        here = pl.ds(pl.multiple_of(step * BLOCK, BLOCK), BLOCK)
        dh = second[here, :] + partial[here, :]
        unit = unit1[here, :].astype(F32)
        dr = norm_back(dh, unit, scale1[here, :], vec[3:4, :])
        second[here, :] = dr
        low = dr.astype(BF16)
        d_att[here, :] = low
        sums[2:3, :] += jnp.sum(low.astype(F32), axis=0, keepdims=True)
        sums[3:4, :] += jnp.sum(dh * unit, axis=0, keepdims=True)
        sums[4:5, :] += jnp.sum(dh, axis=0, keepdims=True)

    done = [copies.start(second, d_first_out), copies.start(d_att, d_att_out)]
    for step in range(width // 256):
        lanes = slice(step * 256, step * 256 + 256)
        d_mixed[:, lanes] = dot_rt(d_att[...], weight_out[lanes, :]).astype(BF16)
        done.append(copies.start(d_mixed.at[:short, lanes], d_mixed_short.at[:, lanes]))
        done.append(copies.start(d_mixed.at[short:, lanes], d_mixed_long.at[:, lanes]))
    wait_all(done)


def mid_backward(second, d_up, unit1, scale1, vec, source, short):
    rows, width = second.shape
    inner = d_up.shape[1]
    return pl.pallas_call(
        functools.partial(mid_backward_kernel, source.starts),
        out_shape=[
            sds((rows, width), F32),
            sds((rows, width), BF16),
            sds((short, width), BF16),
            sds((rows - short, width), BF16),
            sds((8, width), F32),
        ],
        in_specs=[ANY, ANY, ANY, VMEM, VMEM, ANY],
        out_specs=[ANY] * 4 + [VMEM],
        scratch_shapes=[
            pltpu.VMEM((width, width), BF16),
            pltpu.VMEM((width, inner), BF16),
            pltpu.VMEM((rows, width), F32),
            pltpu.VMEM((rows, width), F32),
            pltpu.VMEM((rows, width), BF16),
            pltpu.VMEM((rows, inner), BF16),
            pltpu.VMEM((rows, width), BF16),
            pltpu.VMEM((rows, width), BF16),
            pltpu.SemaphoreType.DMA((24,)),
        ],
        compiler_params=params(),
        cost_estimate=cost(14),
        name="mid_backward",
    )(second, d_up, unit1, scale1, vec, source.packed)


def put_rows(table, result, buffer, part, lanes):
    chips, block = buffer.shape[1:3]
    far = jnp.bitwise_xor(table[2 * chips], part)
    for chip in range(chips):
        slot = table[far * chips + chip]
        buffer[far, slot, :, lanes] = result[chip * block : (chip + 1) * block, :]


def ffn_grads_kernel(
    table, act_in, d_out_in, hid_in, d_up_in, own, other, act, d_out, hid_low, d_up, turned, buffer, sem_i, sem_o
):
    inner = act.shape[1]
    width = d_out.shape[1]
    half_up, half = inner // 2, width // 2
    groups = inner // width
    tile = 768
    loads, ups = Copies(sem_i), []
    begun = [loads.start(d_out_in, d_out)]
    acts = []
    for step in range(groups):
        place = slice(step * width, step * width + width)
        acts.append(loads.start(act_in.at[:, place], act.at[:, place]))
        if step == 0:
            turning = loads.start(hid_in, hid_low)
    for step in range(inner // tile):
        place = slice(step * tile, step * tile + tile)
        ups.append(loads.start(d_up_in.at[:, place], d_up.at[:, place]))
    stores, done = Copies(sem_o), []

    def flush(lanes):
        done.append(stores.start(buffer.at[0, :, :, lanes], own.at[:, :, lanes]))
        done.append(stores.start(buffer.at[1, :, :, lanes], other.at[:, :, lanes]))

    wait_all(begun)
    for step in range(groups):
        acts[step].wait()
        result = dot_lt(act[:, step * width : (step + 1) * width], d_out[...]).astype(BF16)
        lanes = slice(step * half, (step + 1) * half)
        for part in range(2):
            put_rows(table, result[:, part * half : (part + 1) * half], buffer, part, lanes)
        flush(lanes)
    base = groups * half
    turning.wait()
    turned[...] = hid_low[...].T
    for place in range(0, half_up, tile):
        for part in range(2):
            step = (part * half_up + place) // tile
            ups[step].wait()
            result = dot(turned[...], d_up[:, step * tile : (step + 1) * tile]).astype(BF16)
            put_rows(table, result, buffer, part, slice(base + place, base + place + tile))
        flush(slice(base + place, base + place + tile))
    wait_all(done)


def ffn_grads(table, chips, act, d_out, hid_low, d_up):
    rows, inner = act.shape
    width = d_out.shape[1]
    block = width // chips
    groups = inner // width
    cols = groups * width // 2 + inner // 2
    return pl.pallas_call(
        ffn_grads_kernel,
        out_shape=[sds((chips, block, cols), BF16)] * 2,
        in_specs=[SMEM, ANY, ANY, ANY, ANY],
        out_specs=[ANY, ANY],
        scratch_shapes=[
            pltpu.VMEM((rows, inner), BF16),
            pltpu.VMEM((rows, width), BF16),
            pltpu.VMEM((rows, width), BF16),
            pltpu.VMEM((rows, inner), BF16),
            pltpu.VMEM((width, rows), BF16),
            pltpu.VMEM((2, chips, block, cols), BF16),
            pltpu.SemaphoreType.DMA((groups + inner // 768 + 2,)),
            pltpu.SemaphoreType.DMA((2 * groups + 2 * (inner // 1536),)),
        ],
        compiler_params=params(),
        cost_estimate=cost(16),
        name="ffn_grads",
    )(table, act, d_out, hid_low, d_up)


def att_grads_kernel(
    table,
    mixed_short,
    mixed_long,
    d_att_in,
    rows_short,
    rows_long,
    d_short,
    d_query,
    d_own,
    far,
    passed,
    own,
    other,
    columns,
    d_att,
    mixed,
    rows,
    grad,
    turned,
    buffer,
    sem_i,
    sem_o,
    sem_q,
):
    short, width = rows_short.shape
    half = width // 2
    half_qkv = 3 * half
    loads = Copies(sem_i)
    first = [
        loads.start(d_att_in, d_att),
        loads.start(mixed_short, mixed.at[:short, :]),
        loads.start(mixed_long, mixed.at[short:, :]),
    ]
    second = [
        loads.start(rows_short, rows.at[:short, :]),
        loads.start(rows_long, rows.at[short:, :]),
    ]
    third = [
        loads.start(d_query, grad.at[short:, :width]),
        loads.start(d_short, grad.at[:short, :]),
    ]
    total = d_own[...].astype(F32) + far[0].astype(F32) + passed[...].astype(F32)
    grad[short:, width:] = total.astype(BF16)
    stores, done = Copies(sem_o), []

    def flush(lanes):
        done.append(stores.start(buffer.at[0, :, :, lanes], own.at[:, :, lanes]))
        done.append(stores.start(buffer.at[1, :, :, lanes], other.at[:, :, lanes]))

    wait_all(first)
    result = dot_lt(mixed[...], d_att[...]).astype(BF16)
    for part in range(2):
        put_rows(table, result[:, part * half : (part + 1) * half], buffer, part, slice(0, half))
    flush(slice(0, half))
    wait_all(second)
    turned[...] = rows[...].T
    wait_all(third)
    for step in range(3):
        lanes = slice(step * width, (step + 1) * width)
        piece = grad[:, lanes]
        columns[:, lanes] = jnp.sum(piece.astype(F32), axis=0, keepdims=True)
        result = dot(turned[...], piece).astype(BF16)
        for place in range(0, width, half):
            part, start = divmod(step * width + place, half_qkv)
            put_rows(
                table, result[:, place : place + half], buffer, part, slice(half + start, half + start + half)
            )
            far_part = jnp.bitwise_xor(table[2 * buffer.shape[1]], part)
            lanes_out = slice(half + start, half + start + half)
            index = 2 * step + place // half
            for which, target in enumerate((own, other)):

                @pl.when(far_part == which)
                def _(which=which, target=target, lanes_out=lanes_out, index=index):
                    pltpu.make_async_copy(
                        buffer.at[which, :, :, lanes_out], target.at[:, :, lanes_out], sem_q.at[index]
                    ).start()

    for index in range(6):
        part, start = divmod(index * half, half_qkv)
        lanes_out = slice(half + start, half + start + half)
        pltpu.make_async_copy(buffer.at[0, :, :, lanes_out], own.at[:, :, lanes_out], sem_q.at[index]).wait()
    wait_all(done)


def att_grads(
    table, chips, mixed_short, mixed_long, d_att, rows_short, rows_long, d_short, d_query, d_own, far, passed
):
    short, width = rows_short.shape
    rows = short + rows_long.shape[0]
    block = width // chips
    cols = 2 * width
    return pl.pallas_call(
        att_grads_kernel,
        out_shape=[sds((chips, block, cols), BF16)] * 2 + [sds((1, 3 * width), F32)],
        in_specs=[SMEM] + [ANY] * 7 + [VMEM] * 3,
        out_specs=[ANY, ANY, VMEM],
        scratch_shapes=[
            pltpu.VMEM((rows, width), BF16),
            pltpu.VMEM((rows, width), BF16),
            pltpu.VMEM((rows, width), BF16),
            pltpu.VMEM((rows, 3 * width), BF16),
            pltpu.VMEM((width, rows), BF16),
            pltpu.VMEM((2, chips, block, cols), BF16),
            pltpu.SemaphoreType.DMA((7,)),
            pltpu.SemaphoreType.DMA((2,)),
            pltpu.SemaphoreType.DMA((6,)),
        ],
        compiler_params=params(),
        cost_estimate=cost(12),
        name="att_grads",
    )(table, mixed_short, mixed_long, d_att, rows_short, rows_long, d_short, d_query, d_own, far, passed)


def input_grad_kernel(start, table, d_short, d_query, d_own, far, passed, d_first, *rest):
    *weights_in, out_short, out_long, weight, grad, first, out, sems = rest
    copies = Copies(sems)
    short, width = d_short.shape[0], out_short.shape[1]
    loads = []
    if len(weights_in) > 1:
        staged = load_staged(copies, table, weights_in, 0, 3 * width // 2, weight)
    for part in range(3):
        lanes = slice(part * width, (part + 1) * width)
        loads.append([copies.start(d_short.at[:, lanes], grad.at[:short, lanes])])
        if part == 0:
            loads[0].append(copies.start(d_query, grad.at[short:, lanes]))
        if len(weights_in) == 1:
            here = slice(start + part * width, start + (part + 1) * width)
            loads[part].append(copies.start(weights_in[0].at[:, here], weight.at[:, lanes]))
        elif part == 0:
            loads[0] += staged
        if part == 0:
            adding = copies.start(d_first, first)
    total = d_own[...].astype(F32) + far[0].astype(F32) + passed[...].astype(F32)
    grad[short:, width:] = total.astype(BF16)
    done = []
    for part in range(3):
        wait_all(loads[part])
        span = slice(part * width, (part + 1) * width)
        for step in range(width // 256):
            lanes = slice(step * 256, step * 256 + 256)
            total = dot_rt(grad[:, span], weight[lanes, span])
            if part == 0 and step == 0:
                adding.wait()
            if part < 2:
                first[:, lanes] = first[:, lanes] + total
                continue
            out[:, lanes] = (first[:, lanes] + total).astype(out.dtype)
            done.append(copies.start(out.at[:short, lanes], out_short.at[:, lanes]))
            done.append(copies.start(out.at[short:, lanes], out_long.at[:, lanes]))
    wait_all(done)


def input_grad(table, d_short, d_query, d_own, far, passed, d_first, weights, start, dtype):
    rows, width = d_first.shape
    short = d_short.shape[0]
    return pl.pallas_call(
        functools.partial(input_grad_kernel, start),
        out_shape=[sds((short, width), dtype), sds((rows - short, width), dtype)],
        in_specs=[SMEM, ANY, ANY, VMEM, VMEM, VMEM, ANY] + [ANY] * len(weights),
        out_specs=[ANY] * 2,
        scratch_shapes=[
            pltpu.VMEM((width, 3 * width), BF16),
            pltpu.VMEM((rows, 3 * width), BF16),
            pltpu.VMEM((rows, width), F32),
            pltpu.VMEM((rows, width), dtype),
            pltpu.SemaphoreType.DMA((56,)),
        ],
        compiler_params=params(),
        cost_estimate=cost(10),
        name="input_grad",
    )(table, d_short, d_query, d_own, far, passed, d_first, *weights)


def short_backward_kernel(qkv, mixed, d_mixed, raised, inverse, gate, d_qkv, gate_sum):
    low, high = head_masks()
    ones = jnp.concatenate([low, high], axis=0)
    width = mixed.shape[1]
    for pair in range(HEADS // 2):
        lanes = slice(pair * 128, pair * 128 + 128)
        query = qkv[:, lanes] * 0.125
        keys = spread(qkv[:, width + pair * 128 : width + pair * 128 + 128], low, high)
        values = spread(qkv[:, 2 * width + pair * 128 : 2 * width + pair * 128 + 128], low, high)
        grad = d_mixed[:, lanes].astype(F32)
        out = mixed[:, lanes].astype(F32)
        scaled = grad * inverse[:, lanes]
        gate_sum[0, :, lanes] = jnp.sum(grad * out, axis=0, keepdims=True)
        pulled = (scaled * gate[0, :, lanes]).astype(BF16)
        inner = (scaled * out).astype(BF16)
        prob = raised[0, pair]
        bent = dot_rt(jnp.concatenate([pulled, inner], axis=1), jnp.concatenate([values, -ones], axis=1))
        score = (prob.astype(F32) * bent).astype(BF16)
        d_qkv[:, lanes] = (dot(score, keys) * 0.125).astype(BF16)
        turned = dot_lt(query, score)
        turned = jnp.concatenate([turned[:HEAD, :BLOCK], turned[HEAD:, BLOCK:]], axis=0)
        d_qkv[:, width + pair * 128 : width + pair * 128 + 128] = turned.T.astype(BF16)
        turned = dot_lt(pulled, prob)
        turned = jnp.concatenate([turned[:HEAD, :BLOCK], turned[HEAD:, BLOCK:]], axis=0)
        d_qkv[:, 2 * width + pair * 128 : 2 * width + pair * 128 + 128] = turned.T.astype(BF16)


def short_backward(qkv, mixed, d_mixed, raised, inverse, gate):
    rows, width = mixed.shape
    count = rows // BLOCK
    pairs = HEADS // 2
    narrow = pl.BlockSpec((BLOCK, width), lambda i: (i, 0))
    wide = pl.BlockSpec((BLOCK, 3 * width), lambda i: (i, 0))
    vector = pl.BlockSpec((1, 1, width), lambda i: (i, 0, 0))
    return pl.pallas_call(
        short_backward_kernel,
        grid=(count,),
        out_shape=[sds((rows, 3 * width), BF16), sds((count, 1, width), F32)],
        in_specs=[
            wide,
            narrow,
            narrow,
            pl.BlockSpec((1, pairs, BLOCK, 2 * BLOCK), lambda i: (i, 0, 0, 0)),
            narrow,
            vector,
        ],
        out_specs=[wide, vector],
        compiler_params=params(),
        cost_estimate=cost(11.6),
        name="short_backward",
    )(qkv, mixed, d_mixed, raised, inverse, gate)


def long_backward_kernel(blocks, queries, mixed, d_mixed, raised, inverse, parts, gate, *rest):
    sources, (d_query, d_own, d_near, d_core, gate_sum) = rest[:blocks], rest[blocks:]
    low, high = head_masks()
    ones = jnp.concatenate([low, high], axis=0)
    width = mixed.shape[1]
    for pair in range(HEADS // 2):
        lanes = slice(pair * 128, pair * 128 + 128)
        query = queries[:, lanes] * 0.125
        grad = d_mixed[:, lanes].astype(F32)
        out = mixed[:, lanes].astype(F32)
        scaled = grad * inverse[:, lanes]
        inner = (scaled * out).astype(BF16)
        total = 0.0
        for index in range(blocks):
            source = sources[index]
            keys = spread(source[:, lanes], low, high)
            values = spread(source[:, width + pair * 128 : width + pair * 128 + 128], low, high)
            strength = gate[index : index + 1, lanes]
            pulled = (scaled * strength).astype(BF16)
            prob = raised[pair, index]
            bent = dot_rt(jnp.concatenate([pulled, inner], axis=1), jnp.concatenate([values, -ones], axis=1))
            score = (prob.astype(F32) * bent).astype(BF16)
            total = total + dot(score, keys)
            gate_sum[index : index + 1, lanes] = strength * jnp.sum(
                grad * parts[index, :, lanes].astype(F32), axis=0, keepdims=True
            )
            target = (d_own, d_core.at[0], d_near, d_core.at[1])[index]
            turned = dot_lt(query, score)
            turned = jnp.concatenate([turned[:HEAD, :BLOCK], turned[HEAD:, BLOCK:]], axis=0)
            target[:, lanes] = turned.T.astype(BF16)
            turned = dot_lt(pulled, prob)
            turned = jnp.concatenate([turned[:HEAD, :BLOCK], turned[HEAD:, BLOCK:]], axis=0)
            target[:, width + pair * 128 : width + pair * 128 + 128] = turned.T.astype(BF16)
        d_query[:, lanes] = (total * 0.125).astype(BF16)


def long_backward(queries, mixed, d_mixed, raised, inverse, parts, gate, sources):
    rows, width = mixed.shape
    blocks = len(sources)
    return pl.pallas_call(
        functools.partial(long_backward_kernel, blocks),
        out_shape=[
            sds((rows, width), BF16),
            sds((rows, 2 * width), BF16),
            sds((rows, 2 * width), BF16),
            sds((2, rows, 2 * width), BF16),
            sds((blocks, width), F32),
        ],
        in_specs=[VMEM] * (7 + blocks),
        out_specs=[VMEM] * 5,
        compiler_params=params(),
        cost_estimate=cost(8.7),
        name="long_backward",
    )(queries, mixed, d_mixed, raised, inverse, parts, gate, *sources)


class Source:
    def __init__(self, rows, packed, pieces, starts, qkv_start):
        self.rows, self.packed, self.pieces, self.starts, self.qkv_start = rows, packed, pieces, starts, qkv_start

    def qkv(self):
        return self.pieces if self.pieces else (self.packed,)


def on_device(
    plan,
    short_tokens,
    long_tokens,
    short_cotangent,
    long_cotangent,
    qkv_weight,
    out_weight,
    up_weight,
    down_weight,
    vectors,
    up_bias,
    mask_logit,
    short_noise,
    gate_noise,
    block_mask,
    block_order,
):
    shorts, block_rows, width = short_tokens.shape
    blocks = lax.axis_size("seq")
    place = lax.axis_index("seq")
    device = lax.axis_index("dp") * plan.seq + place
    layers = qkv_weight.shape[0]
    inner = up_weight.shape[2]
    own_rows = qkv_weight.shape[1]
    short_rows = shorts * block_rows
    half = width // 2
    half_up = inner // 2
    core = place % 2
    table = plan.tables()
    chips = plan.chips

    per_row = inner // width

    def whole(array):
        return lax.all_gather(array, AXES, axis=0, tiled=True)

    def packed(layer):
        up = up_weight[layer].reshape(own_rows, plan.devices, per_row, own_rows)
        up = up.transpose(0, 2, 1, 3).reshape(own_rows, inner)
        down = down_weight[layer].reshape(per_row, own_rows, width).transpose(1, 0, 2)
        return [out_weight[layer], up, down.reshape(own_rows, inner)]

    def small(layer):
        biases = up_bias[layer].reshape(per_row, own_rows).T
        return jnp.concatenate(
            [vectors[layer], biases, jnp.zeros((own_rows, SMALL - 8 - per_row), BF16)], axis=1
        )

    smalls = [small(layer) for layer in range(layers)]
    sources = []
    for layer in range(layers):
        parts = packed(layer)
        if not plan.staged:
            parts = parts + [qkv_weight[layer]] + (smalls if layer == 0 else [])
        rows = jnp.concatenate(parts, axis=1)
        pieces, qkv_start = (), width + 2 * inner
        if plan.staged:
            qkv_start = None
            sides = [qkv_weight[layer][:, : 3 * half], qkv_weight[layer][:, 3 * half :]]
            if layer == 0:
                sides = [jnp.concatenate([side, extra], axis=1) for side, extra in zip(sides, smalls)]
                earlier = [rows]
            else:
                earlier = [sources[-1].pieces[1], rows]
            pieces = gather(plan, *[after(side, *earlier) for side in sides], core)
        if layer > 0:
            rows = after(rows, sources[-1].packed, *pieces)
        sources.append(Source(rows, whole(rows), pieces, (0, width, width + inner), qkv_start))

    block_ids = jnp.arange(blocks, dtype=jnp.int32)
    near_ids = block_ids ^ place
    placed_ids = block_order[0]
    own_block = jnp.sum(jnp.where(block_ids == place, placed_ids, 0))
    near_int = (near_ids[:, None] == block_ids[None, :]).astype(jnp.int32)
    near_true = jnp.sum(near_int * placed_ids[None, :], axis=1)
    own_hot = (block_ids == own_block).astype(F32)
    near_hot_int = (near_true[:, None] == block_ids[None, :]).astype(jnp.int32)
    near_hot = near_hot_int.astype(F32)
    mask_row = jnp.sum(block_mask[0] * (block_ids == own_block).astype(jnp.int32)[:, None], axis=0)
    opened = jnp.maximum(
        jnp.sum(near_hot_int * mask_row[None, :], axis=1), (block_ids == 0).astype(jnp.int32)
    )
    first_hot = (block_ids == 0).astype(F32)
    corner = first_hot[:, None] * first_hot[None, :]
    highest = lax.Precision.HIGHEST
    logit_near = jnp.einsum(
        "lhij,i,sj->lsh", mask_logit + gate_noise[:, 0], own_hot, near_hot, precision=highest
    )
    gate_long = jax.nn.sigmoid(logit_near)
    gate_short = jax.nn.sigmoid(mask_logit[:, None, :, 0, 0] + short_noise)
    lanes_long = jnp.repeat(gate_long, HEAD, axis=2)
    lanes_short = jnp.repeat(gate_short, HEAD, axis=2)[:, :, None, :]
    head_hot = (jnp.arange(width)[:, None] // HEAD == jnp.arange(HEADS)[None, :]).astype(F32)

    def swap_core(value):
        return lax.ppermute(value, "seq", [(i, i ^ 1) for i in range(blocks)])

    def swap_pair(value):
        return lax.ppermute(value, "seq", [(i, i ^ 2) for i in range(blocks)])

    rows_low = (short_tokens.reshape(short_rows, width), long_tokens[0])
    rows_wide = rows_low
    saved = []
    for layer in range(layers):
        source = sources[layer]
        vec = None if layer == 0 else vecs[layer]
        qkv_short, query_long, kv, *got = project(table, *rows_low, vec, layers, source.qkv(), source.qkv_start)
        if layer == 0:
            vecs = [got[0][which] for which in range(layers)]
            vec = vecs[0]
        kv_core = swap_core(kv)
        kv_pair = swap_pair(kv)
        mixed_short, raised_short, inverse_short = short_forward(qkv_short, lanes_short[layer])
        kv_pair = after(kv_pair, mixed_short)
        key_values = (kv, kv_core, kv_pair, swap_core(kv_pair))
        mixed_long, raised_long, inverse_long, parts = long_forward(
            opened, query_long, lanes_long[layer], key_values
        )
        *y, hid_low, unit1, scale1, unit2, scale2, act, slope = mlp_forward(
            layer + 1 < layers, *rows_wide, mixed_short, mixed_long, vec, inner, source
        )
        saved.append(
            (
                rows_low,
                qkv_short,
                query_long,
                key_values,
                mixed_short,
                raised_short,
                inverse_short,
                mixed_long,
                raised_long,
                inverse_long,
                parts,
                vec,
                hid_low,
                unit1,
                scale1,
                unit2,
                scale2,
                act,
                slope,
            )
        )
        rows_low, rows_wide = y[2:], y[:2]
    outputs = rows_low

    grad = (short_cotangent.reshape(short_rows, width), long_cotangent[0])
    kept = []
    terms = []
    upper = None
    staging = plan.staged
    for layer in reversed(range(layers)):
        last = layer == 0
        source = sources[layer]
        (
            rows_low,
            qkv_short,
            query_long,
            key_values,
            mixed_short,
            raised_short,
            inverse_short,
            mixed_long,
            raised_long,
            inverse_long,
            parts,
            vec,
            hid_low,
            unit1,
            scale1,
            unit2,
            scale2,
            act,
            slope,
        ) = saved[layer]
        second, d_out, sums_ffn, sums_up, d_up = ffn_backward(grad, unit2, scale2, vec, slope, source)
        if upper is not None:
            if staging:
                ffn_upper.wait(d_out)
                ffn_upper.first()
                upper[2] = after(upper[2], ffn_upper.operand, d_out)
            *att, columns = att_grads(table, chips, *upper)
            terms[-1][0] = columns
            if staging:
                att_upper = Reduce(plan, *att)
                ffn_upper.wait(att[0])
                ffn_upper.line()
                d_out = after(d_out, *att, *ffn_upper.operand)
            kept[-1].append(att_upper if staging else att)
        ffn = ffn_grads(table, chips, act, d_out, hid_low, d_up)
        second = after(second, *ffn)
        if staging:
            if upper is not None:
                att_upper.wait(ffn[0])
                att_upper.second()
                second = after(second, att_upper.operand)
            ffn_sum = Reduce(plan, *ffn)
        d_first, d_att, d_mixed_short, d_mixed_long, sums_mid = mid_backward(
            second, d_up, unit1, scale1, vec, source, short_rows
        )
        if staging and upper is not None:
            att_upper.wait(d_att)
            att_upper.first()
            d_mixed_long = after(d_mixed_long, att_upper.operand, *ffn_upper.pending)
        d_query, d_own, d_near, d_core, gate_sum_long = long_backward(
            query_long, mixed_long, d_mixed_long, raised_long, inverse_long, parts, lanes_long[layer], key_values
        )
        far = swap_core(d_core)
        away = (d_near.astype(F32) + far[1].astype(F32)).astype(BF16)
        passed = swap_pair(away)
        if staging:
            ffn_sum.wait(d_query, away)
            ffn_sum.second(passed)
            d_mixed_short = after(d_mixed_short, ffn_sum.operand)
            if upper is not None:
                att_upper.wait(d_query)
                att_upper.line()
                d_mixed_short = after(d_mixed_short, *att_upper.operand)
        d_short, gate_sum_short = short_backward(
            qkv_short, mixed_short, d_mixed_short, raised_short, inverse_short, lanes_short[layer]
        )
        had_upper = upper is not None
        upper = [mixed_short, mixed_long, d_att, *rows_low, d_short, d_query, d_own, far, passed]
        kept.append([ffn_sum if staging else ffn])
        if last:
            *att, columns = att_grads(table, chips, *upper)
            d_first = after(d_first, *att)
            if staging:
                att_sum = Reduce(plan, *att)
                ffn_sum.wait(att[0])
                ffn_sum.first()
                d_first = after(d_first, ffn_sum.operand)
                if had_upper:
                    d_first = after(d_first, *att_upper.pending)
            kept[-1].append(att_sum if staging else att)
        grad = input_grad(
            table,
            d_short,
            d_query,
            d_own,
            far,
            passed,
            d_first,
            source.qkv(),
            source.qkv_start,
            BF16 if last else F32,
        )
        if staging:
            ffn_upper = ffn_sum
            if last:
                ffn_sum.wait(grad[0])
                ffn_sum.line()
                att_sum.wait(grad[0])
                att_sum.second()
        heads = jnp.dot(
            jnp.concatenate([gate_sum_short[:, 0], gate_sum_long]), head_hot, precision=highest
        )
        short_term = jnp.sum(heads[:shorts] * (1.0 - gate_short[layer]), axis=0)
        long_term = heads[shorts:] * (1.0 - gate_long[layer])
        logit_term = (
            jnp.einsum("sh,i,sj->hij", long_term, own_hot, near_hot, precision=highest)
            + short_term[:, None, None] * corner[None]
        )
        terms.append([columns if last else None, sums_mid[2:5], sums_ffn[5:8], sums_up, logit_term])
    kept, terms = kept[::-1], terms[::-1]

    packed_sums = jnp.concatenate(
        [
            jnp.concatenate(
                [
                    rows
                    for columns, mid, ffn, _, _ in terms
                    for rows in (columns[:, :width], columns[:, 2 * width :], mid, ffn)
                ]
            ).reshape(-1, 128),
            jnp.concatenate([term[3] for term in terms]).reshape(-1, 128),
            jnp.stack([term[4] for term in terms]).reshape(-1, 128),
        ]
    )
    count = packed_sums.shape[0]
    packed_sums = jnp.pad(packed_sums, ((0, -count % 8), (0, 0)))
    if staging:
        ffn_sum, att_sum = kept[0]
        sums = Butterfly(plan, packed_sums)
        sums.step()
        sums.step(ffn_sum.operand, att_sum.operand)
        att_sum.first()
        sums.step(att_sum.operand)
        att_sum.wait(*ffn_sum.pending)
        att_sum.line()
        sums.step(*att_sum.operand)
        sums.step(*ffn_sum.pending)
        packed_sums = sums.finish()
    else:
        packed_sums = lax.psum(packed_sums, AXES)
    edge = layers * 8 * width // 128
    more = edge + layers * inner // 128
    vectors_all = packed_sums[:edge].reshape(layers, 8, width)
    vectors_grad = lax.dynamic_slice_in_dim(vectors_all, device * own_rows, own_rows, 2).transpose(0, 2, 1)
    bias_all = packed_sums[edge:more].reshape(layers, per_row, width)
    up_bias_grad = lax.dynamic_slice_in_dim(bias_all, device * own_rows, own_rows, 2).reshape(layers, -1)
    logit_grad = packed_sums[more:count].reshape(mask_logit.shape)

    def scattered(sides):
        rows = jnp.concatenate([side.reshape(width, side.shape[-1]) for side in sides], axis=1)
        rows = lax.psum_scatter(rows, AXES, scatter_dimension=0, tiled=True).astype(F32)
        count = rows.shape[1] // 2
        return rows[:, :count], rows[:, count:]

    def owned(total):
        part = [lax.dynamic_slice_in_dim(total, which * own_rows, own_rows, 0) for which in (core, 1 - core)]
        mine, got = part[0], send(part[1], plan.cores)
        return jnp.where(core == 0, mine, got), jnp.where(core == 0, got, mine)

    qkv_grad, out_grad, up_grad, down_grad = [], [], [], []
    for layer in range(layers):
        ffn, att = kept[layer]
        if staging:
            ffn, att = ffn.finish(), att.finish()
            if layer > 0:
                att = after(att, grad[0], *kept[0][0].operand)
            ffn, att = owned(ffn), owned(att)
            if layer > 0:
                begun = (grad[0], *kept[0][0].operand)
                ffn = after(ffn[0], *begun), after(ffn[1], *begun)
        else:
            ffn, att = scattered(ffn), scattered(att)
        span = per_row * half
        down = [side[:, :span].reshape(own_rows, per_row, half) for side in ffn]
        down = jnp.concatenate(down, axis=2).transpose(1, 0, 2)
        down_grad.append(down.reshape(per_row * own_rows, width))
        up = jnp.concatenate([side[:, span:] for side in ffn], axis=1)
        up = up.reshape(own_rows, per_row, plan.devices, own_rows).transpose(0, 2, 1, 3)
        up_grad.append(up.reshape(own_rows, inner))
        out_grad.append(jnp.concatenate([side[:, :half] for side in att], axis=1))
        qkv_grad.append(jnp.concatenate([side[:, half:] for side in att], axis=1))
    return (
        outputs[0].reshape(shorts, block_rows, width),
        outputs[1][None],
        grad[0].reshape(shorts, block_rows, width),
        grad[1][None],
        jnp.stack(qkv_grad),
        jnp.stack(out_grad),
        jnp.stack(up_grad),
        jnp.stack(down_grad),
        vectors_grad,
        up_bias_grad,
        logit_grad,
    )


def solution(mesh):
    split = ("dp", "seq")
    in_specs = (
        P(split, None, None),
        P("dp", "seq", None),
        P(split, None, None),
        P("dp", "seq", None),
        P(None, split, None),
        P(None, split, None),
        P(None, split, None),
        P(None, split, None),
        P(None, split, None),
        P(None, split),
        P(),
        P(None, split, None),
        P(None, "dp", None, None, None),
        P("dp", None, None),
        P("dp", None),
    )
    out_specs = (
        P(split, None, None),
        P("dp", "seq", None),
        P(split, None, None),
        P("dp", "seq", None),
        P(None, split, None),
        P(None, split, None),
        P(None, split, None),
        P(None, split, None),
        P(None, split, None),
        P(None, split),
        P(),
    )

    def build(*arrays):
        plan = Plan(mesh, arrays[4].shape[1])
        return jax.shard_map(
            functools.partial(on_device, plan),
            mesh=mesh,
            in_specs=in_specs,
            out_specs=out_specs,
            check_vma=False,
        )(*arrays)

    return build
```

```python
import functools

import jax
import jax.numpy as jnp
from jax import lax
from jax.experimental import pallas as pl
from jax.experimental.pallas import tpu as pltpu
from jax.sharding import PartitionSpec as P

HEADS = 12
HEAD = 64
BLOCK = 128
AXES = ("dp", "seq")
BF16 = jnp.bfloat16
F32 = jnp.float32
VMEM = pl.BlockSpec(memory_space=pltpu.VMEM)
SMEM = pl.BlockSpec(memory_space=pltpu.SMEM)
ANY = pl.BlockSpec(memory_space=pl.ANY)
SMALL = 128
ROOT_HALF = 0.7071067811865476
ROOT_TWO_PI_INV = 0.3989422804014327


def sds(shape, dtype):
    return jax.ShapeDtypeStruct(shape, dtype)


def params(mib=60):
    return pltpu.CompilerParams(vmem_limit_bytes=mib * 2**20)


def cost(us):
    return pl.CostEstimate(flops=int(us * 0.5e9), bytes_accessed=int(us * 3.3e6), transcendentals=0)


def dot(left, right):
    return jnp.dot(left, right, preferred_element_type=F32)


def dot_rt(left, right):
    return lax.dot_general(left, right, (((1,), (1,)), ((), ())), preferred_element_type=F32)


def dot_lt(left, right):
    return lax.dot_general(left, right, (((0,), (0,)), ((), ())), preferred_element_type=F32)


class Plan:
    def __init__(self, mesh, width):
        dp, seq = mesh.shape["dp"], mesh.shape["seq"]
        self.dp, self.seq, self.devices = dp, seq, dp * seq
        depth = dp // 2
        chips = depth * 4
        self.staged = (
            seq == 4
            and dp % 2 == 0
            and depth & (depth - 1) == 0
            and width % chips == 0
            and (width // chips) % 16 == 0
        )
        self.depth, self.chips = depth, chips if self.staged else 16
        if self.staged:
            self.z_perms = [self.flip(z=step) for step in range(1, depth)]
            self.first = self.flip_by_core((0, 1), (1, 0))
            self.second = self.flip_by_core((1, 0), (0, 1))
            self.cores = self.flip(core=1)

    def flip(self, z=0, x=0, y=0, core=0):
        pairs = []
        for dev in range(self.devices):
            pairs.append((dev, dev ^ (z * 8 + x * 4 + y * 2 + core)))
        return pairs

    def flip_by_core(self, even, odd):
        pairs = []
        for dev in range(self.devices):
            x, y = even if dev % 2 == 0 else odd
            pairs.append((dev, dev ^ (x * 4 + y * 2)))
        return pairs

    def tables(self):
        slots = jnp.arange(self.chips, dtype=jnp.int32)
        if not self.staged:
            return jnp.concatenate([slots, slots, jnp.zeros((8,), jnp.int32), slots, slots])
        me = lax.axis_index("dp") * 4 + lax.axis_index("seq")
        core, chip = me % 2, me // 2
        away = slots ^ chip
        z, x, y = away // 4, (away // 2) % 2, away % 2
        y_slot = (x * 2 + y) * self.depth + z
        x_slot = (y * 2 + x) * self.depth + z
        steps, a, b = slots % self.depth, (slots // self.depth) % 2, slots // (2 * self.depth)
        y_chip = (steps * 4 + b * 2 + a) ^ chip
        x_chip = (steps * 4 + a * 2 + b) ^ chip
        even = core == 0
        return jnp.concatenate(
            [
                jnp.where(even, y_slot, x_slot),
                jnp.where(even, x_slot, y_slot),
                jnp.full((8,), core, jnp.int32),
                jnp.where(even, y_chip, x_chip),
                jnp.where(even, x_chip, y_chip),
            ]
        ).astype(jnp.int32)


def gather(plan, first, second, core):
    even = core == 0
    got = send(jnp.where(even, second, first), plan.cores)
    mine = jnp.where(even, first, second)
    base = jnp.where(even, jnp.concatenate([mine, got]), jnp.concatenate([got, mine]))
    line = jnp.stack([base] + [send(base, pairs) for pairs in plan.z_perms])
    near = jnp.concatenate([line, send(line, plan.first)])
    far = send(near, plan.second)
    return (near, far, send(near, plan.cores), send(far, plan.cores))


def send(value, pairs):
    return lax.ppermute(value, AXES, pairs)


def after(value, *earlier):
    return lax.optimization_barrier((value, *earlier))[0]


class Reduce:
    def __init__(self, plan, own, other):
        self.plan, self.own = plan, own
        self.part = plan.chips // 2
        self.quarter = self.part // 2
        self.pending = send(other, plan.cores)

    def wait(self, *values):
        if isinstance(self.pending, list):
            self.pending = [after(value, *values) for value in self.pending]
        else:
            self.pending = after(self.pending, *values)

    def second(self, *earlier):
        part = self.part
        self.got = self.pending
        away = self.own[part:].astype(F32) + self.got[part:].astype(F32)
        self.operand = after(away.astype(BF16), *earlier) if earlier else away.astype(BF16)
        self.pending = send(self.operand, self.plan.second)

    def first(self):
        part, quarter = self.part, self.quarter
        self.got_b = self.pending
        near = self.own[quarter:part].astype(F32) + self.got[quarter:part].astype(F32)
        near = near + self.got_b[quarter:].astype(F32)
        self.operand = near.astype(BF16)
        self.pending = send(self.operand, self.plan.first)

    def line(self):
        quarter = self.quarter
        line = self.own[:quarter].astype(F32) + self.got[:quarter].astype(F32)
        line = line + self.got_b[:quarter].astype(F32) + self.pending.astype(F32)
        low = line.astype(BF16)
        self.total = line[0]
        self.operand = lax.optimization_barrier(tuple(low[step] for step in range(1, self.plan.depth)))
        self.pending = [send(part, pairs) for part, pairs in zip(self.operand, self.plan.z_perms)]

    def finish(self):
        total = self.total
        for value in self.pending:
            total = total + value.astype(F32)
        return total


class Butterfly:
    def __init__(self, plan, value):
        self.plan, self.value, self.bit, self.pending = plan, value, 1, None

    def step(self, *earlier):
        if self.pending is not None:
            self.value = self.value + after(self.pending, *earlier)
        self.pending = None
        if self.bit < self.plan.devices:
            pairs = [(dev, dev ^ self.bit) for dev in range(self.plan.devices)]
            self.pending = send(self.value, pairs)
            self.bit *= 2

    def finish(self):
        while self.pending is not None:
            self.step()
        return self.value


class Copies:
    def __init__(self, sems):
        self.sems, self.count = sems, 0

    def start(self, source, target):
        copy = pltpu.make_async_copy(source, target, self.sems.at[self.count])
        self.count += 1
        copy.start()
        return copy


def wait_all(copies):
    for copy in copies:
        copy.wait()


def load_staged(copies, table, pieces, low, high, target):
    begun = []
    slots, rows, _ = pieces[0].shape
    count = 2 * slots
    core = table[2 * count]
    for place, piece in enumerate(pieces):
        half = core if place < 2 else 1 - core
        lanes = pl.ds(pl.multiple_of(half * (high - low), 128), high - low)
        for slot in range(slots):
            chip = table[2 * count + 8 + place * slots + slot]
            here = pl.ds(pl.multiple_of(chip * rows, 16), rows)
            begun.append(copies.start(piece.at[slot, :, low:high], target.at[here, lanes]))
    return begun


def project_kernel(start, given, table, rows_short, rows_long, *rest):
    if given:
        vec, *weights_in, out_short, out_query, out_kv, rows, weight, out, small, sems = rest
    else:
        *weights_in, out_short, out_query, out_kv, vec, rows, weight, out, small, sems = rest
    copies = Copies(sems)
    short, width = rows_short.shape
    begun = [
        copies.start(rows_short, rows.at[:short, :]),
        copies.start(rows_long, rows.at[short:, :]),
    ]
    loads = []
    half = 3 * width // 2
    if len(weights_in) > 1:
        begun += load_staged(copies, table, weights_in, 0, half, weight)
        if not given:
            begun += load_staged(copies, table, weights_in, half, half + SMALL, small)
    else:
        if not given:
            here = slice(start + 3 * width, start + 3 * width + small.shape[1])
            begun.append(copies.start(weights_in[0].at[:, here], small))
        for part in range(3):
            here = slice(start + part * width, start + (part + 1) * width)
            loads.append(
                copies.start(weights_in[0].at[:, here], weight.at[:, part * width : (part + 1) * width])
            )
    wait_all(begun)
    if not given:
        turned = small[...].T
        for layer in range(small.shape[1] // SMALL):
            vec[layer] = turned[layer * SMALL : layer * SMALL + 16, :].astype(F32)
        first = vec.at[0]
    else:
        first = vec
    done = []
    for part in range(3):
        lanes = slice(part * width, (part + 1) * width)
        wait_all(loads[part : part + 1])
        result = dot(rows[...], weight[:, lanes])
        if part != 1:
            result = result + first[part // 2 : part // 2 + 1, :]
        out[:, lanes] = result.astype(BF16)
        if part == 0:
            target = out_query
        else:
            target = out_kv.at[:, (part - 1) * width : part * width]
        done.append(copies.start(out.at[short:, lanes], target))
        done.append(copies.start(out.at[:short, lanes], out_short.at[:, lanes]))
    wait_all(done)


def project(table, rows_short, rows_long, vec, layers, weights, start):
    short, width = rows_short.shape
    count = short + rows_long.shape[0]
    given = vec is not None
    return pl.pallas_call(
        functools.partial(project_kernel, start, given),
        out_shape=[
            sds((short, 3 * width), BF16),
            sds((count - short, width), BF16),
            sds((count - short, 2 * width), BF16),
        ]
        + ([] if given else [sds((layers, 16, width), F32)]),
        in_specs=[SMEM, ANY, ANY] + [VMEM] * given + [ANY] * len(weights),
        out_specs=[ANY] * 3 + [VMEM] * (not given),
        scratch_shapes=[
            pltpu.VMEM((count, width), BF16),
            pltpu.VMEM((width, 3 * width), BF16),
            pltpu.VMEM((count, 3 * width), BF16),
            pltpu.VMEM((width, layers * SMALL), BF16),
            pltpu.SemaphoreType.DMA((80,)),
        ],
        compiler_params=params(),
        cost_estimate=cost(10),
        name="project",
    )(table, rows_short, rows_long, *([vec] if given else []), *weights)


def head_masks():
    lane = lax.broadcasted_iota(jnp.int32, (BLOCK, BLOCK), 1)
    low = jnp.where(lane < HEAD, 1.0, 0.0).astype(BF16)
    high = jnp.where(lane < HEAD, 0.0, 1.0).astype(BF16)
    return low, high


def spread(pair, low, high):
    return jnp.concatenate([pair * low, pair * high], axis=0)


def short_forward_kernel(qkv, gate, mixed, raised, inverse):
    low, high = head_masks()
    ones = jnp.concatenate([low, high], axis=0)
    width = mixed.shape[1]
    for pair in range(HEADS // 2):
        lanes = slice(pair * 128, pair * 128 + 128)
        query = qkv[:, lanes] * 0.125
        keys = spread(qkv[:, width + pair * 128 : width + pair * 128 + 128], low, high)
        values = spread(qkv[:, 2 * width + pair * 128 : 2 * width + pair * 128 + 128], low, high)
        scores = dot_rt(query, keys)
        left, right = scores[:, :BLOCK], scores[:, BLOCK:]
        left = jnp.exp(left - jnp.max(left, axis=1, keepdims=True))
        right = jnp.exp(right - jnp.max(right, axis=1, keepdims=True))
        prob = jnp.concatenate([left, right], axis=1).astype(BF16)
        both = dot(prob, jnp.concatenate([values, ones], axis=1))
        inv = 1.0 / both[:, BLOCK:]
        raised[0, pair] = prob
        inverse[:, lanes] = inv
        mixed[:, lanes] = (both[:, :BLOCK] * inv * gate[0, :, lanes]).astype(BF16)


def short_forward(qkv, gate):
    rows = qkv.shape[0]
    width = qkv.shape[1] // 3
    count = rows // BLOCK
    pairs = HEADS // 2
    return pl.pallas_call(
        short_forward_kernel,
        grid=(count,),
        out_shape=[
            sds((rows, width), BF16),
            sds((count, pairs, BLOCK, 2 * BLOCK), BF16),
            sds((rows, width), F32),
        ],
        in_specs=[
            pl.BlockSpec((BLOCK, 3 * width), lambda i: (i, 0)),
            pl.BlockSpec((1, 1, width), lambda i: (i, 0, 0)),
        ],
        out_specs=[
            pl.BlockSpec((BLOCK, width), lambda i: (i, 0)),
            pl.BlockSpec((1, pairs, BLOCK, 2 * BLOCK), lambda i: (i, 0, 0, 0)),
            pl.BlockSpec((BLOCK, width), lambda i: (i, 0)),
        ],
        compiler_params=params(),
        cost_estimate=cost(7),
        name="short_forward",
    )(qkv, gate)


def long_forward_kernel(blocks, opened, queries, gate, *rest):
    sources, (mixed, raised, inverse, parts) = rest[:blocks], rest[blocks:]
    low, high = head_masks()
    ones = jnp.concatenate([low, high], axis=0)
    width = mixed.shape[1]
    for pair in range(HEADS // 2):
        lanes = slice(pair * 128, pair * 128 + 128)
        query = queries[:, lanes] * 0.125
        scores, values = [], []
        for index in range(blocks):
            source = sources[index]
            keys = spread(source[:, lanes], low, high)
            values.append(spread(source[:, width + pair * 128 : width + pair * 128 + 128], low, high))
            score = dot_rt(query, keys)
            scores.append(jnp.where(opened[index] > 0, score, -1e30))
        top = functools.reduce(jnp.maximum, scores)
        top_left = jnp.max(top[:, :BLOCK], axis=1, keepdims=True)
        top_right = jnp.max(top[:, BLOCK:], axis=1, keepdims=True)
        both = []
        for index in range(blocks):
            left = jnp.exp(scores[index][:, :BLOCK] - top_left)
            right = jnp.exp(scores[index][:, BLOCK:] - top_right)
            prob = jnp.concatenate([left, right], axis=1).astype(BF16)
            raised[pair, index] = prob
            both.append(dot(prob, jnp.concatenate([values[index], ones], axis=1)))
        inv = 1.0 / sum(value[:, BLOCK:] for value in both)
        inverse[:, lanes] = inv
        total = 0.0
        for index in range(blocks):
            part = both[index][:, :BLOCK] * inv
            parts[index, :, lanes] = part.astype(BF16)
            total = total + part * gate[index : index + 1, lanes]
        mixed[:, lanes] = total.astype(BF16)


def long_forward(opened, queries, gate, sources):
    rows, width = queries.shape
    blocks = len(sources)
    return pl.pallas_call(
        functools.partial(long_forward_kernel, blocks),
        out_shape=[
            sds((rows, width), BF16),
            sds((HEADS // 2, blocks, BLOCK, 2 * BLOCK), BF16),
            sds((rows, width), F32),
            sds((blocks, rows, width), BF16),
        ],
        in_specs=[SMEM, VMEM, VMEM] + [VMEM] * blocks,
        out_specs=[VMEM] * 4,
        compiler_params=params(),
        cost_estimate=cost(5.3),
        name="long_forward",
    )(opened, queries, gate, *sources)


def norm_rows(rows, gain, shift):
    inverse = 1.0 / rows.shape[1]
    center = rows - jnp.sum(rows, axis=1, keepdims=True) * inverse
    spread_ = jnp.sum(center * center, axis=1, keepdims=True) * inverse
    scale = lax.rsqrt(spread_ + 1e-05)
    unit = center * scale
    return unit, scale, unit * gain + shift


def mlp_forward_kernel(
    wide,
    starts,
    rows_short,
    rows_long,
    mixed_short,
    mixed_long,
    vec,
    packed,
    *rest,
):
    (
        y_short,
        y_long,
        y_low_short,
        y_low_long,
        hid_low_out,
        unit1_out,
        scale1,
        unit2_out,
        scale2,
        act_out,
        slope_out,
        weight_out,
        weight_up,
        weight_down,
        mixed,
        hidden,
        hid_low,
        unit,
        y_low,
        act,
        slope,
        sems,
        sem_w,
        sem_o,
        sem_y,
    ) = rest
    out_start, up_start, down_start = starts
    copies = Copies(sems)
    total, width = hidden.shape
    inner = act.shape[1]
    short = rows_short.shape[0]
    tile = width
    steps = inner // tile
    begun = [
        copies.start(mixed_short, mixed.at[:short, :]),
        copies.start(mixed_long, mixed.at[short:, :]),
        copies.start(packed.at[:, out_start : out_start + width], weight_out),
    ]
    downs = []
    for step in range(steps):
        lanes = slice(step * tile, (step + 1) * tile)
        here = slice(up_start + step * tile, up_start + (step + 1) * tile)
        pltpu.make_async_copy(packed.at[:, here], weight_up.at[:, lanes], sem_w.at[step]).start()
    for group in range(inner // width):
        start = down_start + group * width
        downs.append(
            copies.start(packed.at[:, start : start + width], weight_down.at[group * width : (group + 1) * width, :])
        )
    wait_all(begun)
    for step in range(width // 256):
        lanes = slice(step * 256, step * 256 + 256)
        summed = dot(mixed[...], weight_out[:, lanes]) + vec[2:3, lanes]
        hidden[:short, lanes] = summed[:short] + rows_short[:, lanes].astype(F32)
        hidden[short:, lanes] = summed[short:] + rows_long[:, lanes].astype(F32)

    @pl.loop(0, total // BLOCK)
    def _(step):
        here = pl.ds(pl.multiple_of(step * BLOCK, BLOCK), BLOCK)
        level, scale, hid = norm_rows(hidden[here, :], vec[3:4, :], vec[4:5, :])
        unit[here, :] = level.astype(BF16)
        scale1[here, :] = scale
        hidden[here, :] = hid
        hid_low[here, :] = hid.astype(BF16)

    done = [copies.start(unit, unit1_out), copies.start(hid_low, hid_low_out)]

    @pl.loop(0, steps)
    def _(step):
        place = pl.ds(pl.multiple_of(step * tile, tile), tile)
        pltpu.make_async_copy(weight_up.at[:, place], weight_up.at[:, place], sem_w.at[step]).wait()
        upper = dot(hid_low[...], weight_up[:, place]) + vec[pl.ds(8 + step, 1), :]
        below = 0.5 + 0.5 * lax.erf(upper * ROOT_HALF)
        act[:, place] = (upper * below).astype(BF16)
        bell = ROOT_TWO_PI_INV * jnp.exp(-0.5 * upper * upper)
        slope[:, place] = (below + upper * bell).astype(BF16)
        pltpu.make_async_copy(act.at[:, place], act_out.at[:, place], sem_o.at[0, step]).start()
        pltpu.make_async_copy(slope.at[:, place], slope_out.at[:, place], sem_o.at[1, step]).start()

    wait_all(downs)
    for step in range(width // 256):
        lanes = slice(step * 256, step * 256 + 256)
        hidden[:, lanes] = hidden[:, lanes] + dot(act[...], weight_down[:, lanes]) + vec[5:6, lanes]
    wait_all(done)

    @pl.loop(0, total // BLOCK)
    def _(step):
        here = pl.ds(pl.multiple_of(step * BLOCK, BLOCK), BLOCK)
        level, scale, y = norm_rows(hidden[here, :], vec[6:7, :], vec[7:8, :])
        unit[here, :] = level.astype(BF16)
        scale2[here, :] = scale
        hidden[here, :] = y
        y_low[here, :] = y.astype(BF16)
        if wide:

            @pl.when(step < short // BLOCK)
            def _():
                pltpu.make_async_copy(hidden.at[here, :], y_short.at[here, :], sem_y.at[step]).start()

    done = [
        copies.start(unit, unit2_out),
        copies.start(y_low.at[:short, :], y_low_short),
        copies.start(y_low.at[short:, :], y_low_long),
    ]
    if wide:
        done.append(copies.start(hidden.at[short:, :], y_long))

        @pl.loop(0, short // BLOCK)
        def _(step):
            here = pl.ds(pl.multiple_of(step * BLOCK, BLOCK), BLOCK)
            pltpu.make_async_copy(hidden.at[here, :], y_short.at[here, :], sem_y.at[step]).wait()

    @pl.loop(0, steps)
    def _(step):
        place = pl.ds(pl.multiple_of(step * tile, tile), tile)
        pltpu.make_async_copy(act.at[:, place], act_out.at[:, place], sem_o.at[0, step]).wait()
        pltpu.make_async_copy(slope.at[:, place], slope_out.at[:, place], sem_o.at[1, step]).wait()

    wait_all(done)


def mlp_forward(wide, rows_short, rows_long, mixed_short, mixed_long, vec, inner, source):
    rows = rows_short.shape[0] + rows_long.shape[0]
    width = rows_short.shape[1]
    return pl.pallas_call(
        functools.partial(mlp_forward_kernel, wide, source.starts),
        out_shape=[
            sds(rows_short.shape if wide else (8, 128), F32),
            sds(rows_long.shape if wide else (8, 128), F32),
            sds(rows_short.shape, BF16),
            sds(rows_long.shape, BF16),
            sds((rows, width), BF16),
            sds((rows, width), BF16),
            sds((rows, 1), F32),
            sds((rows, width), BF16),
            sds((rows, 1), F32),
            sds((rows, inner), BF16),
            sds((rows, inner), BF16),
        ],
        in_specs=[VMEM, VMEM, ANY, ANY, VMEM, ANY],
        out_specs=[ANY] * 6 + [VMEM, ANY, VMEM, ANY, ANY],
        scratch_shapes=[
            pltpu.VMEM((width, width), BF16),
            pltpu.VMEM((width, inner), BF16),
            pltpu.VMEM((inner, width), BF16),
            pltpu.VMEM((rows, width), BF16),
            pltpu.VMEM((rows, width), F32),
            pltpu.VMEM((rows, width), BF16),
            pltpu.VMEM((rows, width), BF16),
            pltpu.VMEM((rows, width), BF16),
            pltpu.VMEM((rows, inner), BF16),
            pltpu.VMEM((rows, inner), BF16),
            pltpu.SemaphoreType.DMA((24,)),
            pltpu.SemaphoreType.DMA((inner // width,)),
            pltpu.SemaphoreType.DMA((2, inner // width)),
            pltpu.SemaphoreType.DMA((rows // BLOCK,)),
        ],
        compiler_params=params(),
        cost_estimate=cost(28),
        name="mlp_forward",
    )(rows_short, rows_long, mixed_short, mixed_long, vec, source.packed)


def norm_back(grad, unit, scale, gain):
    inverse = 1.0 / grad.shape[1]
    pulled = grad * gain
    mean = jnp.sum(pulled, axis=1, keepdims=True) * inverse
    along = jnp.sum(pulled * unit, axis=1, keepdims=True) * inverse
    return scale * (pulled - mean - unit * along)


def ffn_backward_kernel(
    down_start,
    grad_short,
    grad_long,
    unit2,
    scale2,
    vec,
    slope_in,
    packed,
    second_out,
    d_out_out,
    sums,
    sums_up,
    d_up_out,
    weight,
    second,
    d_out,
    slope,
    d_up,
    sems,
    sem_w,
    sem_s,
    sem_o,
):
    copies = Copies(sems)
    total, width = second.shape
    inner = slope.shape[1]
    short = grad_short.shape[0]
    tile = 512
    steps = inner // tile
    loads = []
    for group in range(inner // width):
        start = down_start + group * width
        loads.append(
            copies.start(packed.at[:, start : start + width], weight.at[group * width : (group + 1) * width, :])
        )
    for step in range(steps):
        lanes = slice(step * tile, (step + 1) * tile)
        pltpu.make_async_copy(slope_in.at[:, lanes], slope.at[:, lanes], sem_s.at[step]).start()
    sums[...] = jnp.zeros_like(sums)

    def begin(here, grad):
        dy = grad.astype(F32)
        unit = unit2[here, :].astype(F32)
        dr = norm_back(dy, unit, scale2[here, :], vec[6:7, :])
        second[here, :] = dr
        low = dr.astype(BF16)
        d_out[here, :] = low
        sums[5:6, :] += jnp.sum(low.astype(F32), axis=0, keepdims=True)
        sums[6:7, :] += jnp.sum(dy * unit, axis=0, keepdims=True)
        sums[7:8, :] += jnp.sum(dy, axis=0, keepdims=True)

    @pl.loop(0, short // BLOCK)
    def _(step):
        here = pl.ds(pl.multiple_of(step * BLOCK, BLOCK), BLOCK)
        begin(here, grad_short[here, :])

    begin(slice(short, total), grad_long[...])
    done = [copies.start(second, second_out), copies.start(d_out, d_out_out)]
    wait_all(loads)

    @pl.loop(0, steps)
    def _(step):
        place = pl.ds(pl.multiple_of(step * tile, tile), tile)
        pltpu.make_async_copy(slope_in.at[:, place], slope.at[:, place], sem_s.at[step]).wait()
        low = (dot_rt(d_out[...], weight[place, :]) * slope[:, place].astype(F32)).astype(BF16)
        d_up[:, place] = low
        sums_up[:, place] = jnp.sum(low.astype(F32), axis=0, keepdims=True)
        pltpu.make_async_copy(d_up.at[:, place], d_up_out.at[:, place], sem_o.at[step]).start()

    @pl.loop(0, steps)
    def _(step):
        place = pl.ds(pl.multiple_of(step * tile, tile), tile)
        pltpu.make_async_copy(d_up.at[:, place], d_up_out.at[:, place], sem_o.at[step]).wait()

    wait_all(done)


def ffn_backward(grad, unit2, scale2, vec, slope, source):
    rows, width = unit2.shape
    inner = slope.shape[1]
    return pl.pallas_call(
        functools.partial(ffn_backward_kernel, source.starts[2]),
        out_shape=[
            sds((rows, width), F32),
            sds((rows, width), BF16),
            sds((8, width), F32),
            sds((1, inner), F32),
            sds((rows, inner), BF16),
        ],
        in_specs=[VMEM] * 5 + [ANY, ANY],
        out_specs=[ANY, ANY, VMEM, VMEM, ANY],
        scratch_shapes=[
            pltpu.VMEM((inner, width), BF16),
            pltpu.VMEM((rows, width), F32),
            pltpu.VMEM((rows, width), BF16),
            pltpu.VMEM((rows, inner), BF16),
            pltpu.VMEM((rows, inner), BF16),
            pltpu.SemaphoreType.DMA((inner // width + 2,)),
            pltpu.SemaphoreType.DMA((1,)),
            pltpu.SemaphoreType.DMA((inner // 512,)),
            pltpu.SemaphoreType.DMA((inner // 512,)),
        ],
        compiler_params=params(),
        cost_estimate=cost(14),
        name="ffn_backward",
    )(*grad, unit2, scale2, vec, slope, source.packed)


def mid_backward_kernel(starts, second_in, d_up_in, unit1_in, scale1, vec, packed, *rest):
    (
        d_first_out,
        d_att_out,
        d_mixed_short,
        d_mixed_long,
        sums,
        weight_out,
        weight_up,
        second,
        partial,
        unit1,
        d_up,
        d_att,
        d_mixed,
        sems,
    ) = rest
    out_start, up_start, _ = starts
    copies = Copies(sems)
    total, width = second.shape
    inner = d_up.shape[1]
    short = d_mixed_short.shape[0]
    spans = [slice(0, width), slice(width, inner)]
    loads = []
    for span in spans:
        here = slice(up_start + span.start, up_start + span.stop)
        loads.append(
            [
                copies.start(d_up_in.at[:, span], d_up.at[:, span]),
                copies.start(packed.at[:, here], weight_up.at[:, span]),
            ]
        )
    rest = [
        copies.start(second_in, second),
        copies.start(unit1_in, unit1),
        copies.start(packed.at[:, out_start : out_start + width], weight_out),
    ]
    sums[...] = jnp.zeros_like(sums)
    for part, span in enumerate(spans):
        wait_all(loads[part])
        for step in range(width // 256):
            lanes = slice(step * 256, step * 256 + 256)
            piece = dot_rt(d_up[:, span], weight_up[lanes, span])
            partial[:, lanes] = piece if part == 0 else partial[:, lanes] + piece
    wait_all(rest)

    @pl.loop(0, total // BLOCK)
    def _(step):
        here = pl.ds(pl.multiple_of(step * BLOCK, BLOCK), BLOCK)
        dh = second[here, :] + partial[here, :]
        unit = unit1[here, :].astype(F32)
        dr = norm_back(dh, unit, scale1[here, :], vec[3:4, :])
        second[here, :] = dr
        low = dr.astype(BF16)
        d_att[here, :] = low
        sums[2:3, :] += jnp.sum(low.astype(F32), axis=0, keepdims=True)
        sums[3:4, :] += jnp.sum(dh * unit, axis=0, keepdims=True)
        sums[4:5, :] += jnp.sum(dh, axis=0, keepdims=True)

    done = [copies.start(second, d_first_out), copies.start(d_att, d_att_out)]
    for step in range(width // 256):
        lanes = slice(step * 256, step * 256 + 256)
        d_mixed[:, lanes] = dot_rt(d_att[...], weight_out[lanes, :]).astype(BF16)
        done.append(copies.start(d_mixed.at[:short, lanes], d_mixed_short.at[:, lanes]))
        done.append(copies.start(d_mixed.at[short:, lanes], d_mixed_long.at[:, lanes]))
    wait_all(done)


def mid_backward(second, d_up, unit1, scale1, vec, source, short):
    rows, width = second.shape
    inner = d_up.shape[1]
    return pl.pallas_call(
        functools.partial(mid_backward_kernel, source.starts),
        out_shape=[
            sds((rows, width), F32),
            sds((rows, width), BF16),
            sds((short, width), BF16),
            sds((rows - short, width), BF16),
            sds((8, width), F32),
        ],
        in_specs=[ANY, ANY, ANY, VMEM, VMEM, ANY],
        out_specs=[ANY] * 4 + [VMEM],
        scratch_shapes=[
            pltpu.VMEM((width, width), BF16),
            pltpu.VMEM((width, inner), BF16),
            pltpu.VMEM((rows, width), F32),
            pltpu.VMEM((rows, width), F32),
            pltpu.VMEM((rows, width), BF16),
            pltpu.VMEM((rows, inner), BF16),
            pltpu.VMEM((rows, width), BF16),
            pltpu.VMEM((rows, width), BF16),
            pltpu.SemaphoreType.DMA((24,)),
        ],
        compiler_params=params(),
        cost_estimate=cost(14),
        name="mid_backward",
    )(second, d_up, unit1, scale1, vec, source.packed)


def put_rows(table, result, buffer, part, lanes):
    chips, block = buffer.shape[1:3]
    far = jnp.bitwise_xor(table[2 * chips], part)
    for chip in range(chips):
        slot = table[far * chips + chip]
        buffer[far, slot, :, lanes] = result[chip * block : (chip + 1) * block, :]


def ffn_grads_kernel(
    table, act_in, d_out_in, hid_in, d_up_in, own, other, act, d_out, hid_low, d_up, turned, buffer, sem_i, sem_o
):
    inner = act.shape[1]
    width = d_out.shape[1]
    half_up, half = inner // 2, width // 2
    groups = inner // width
    tile = 768
    loads, ups = Copies(sem_i), []
    begun = [loads.start(d_out_in, d_out)]
    acts = []
    for step in range(groups):
        place = slice(step * width, step * width + width)
        acts.append(loads.start(act_in.at[:, place], act.at[:, place]))
        if step == 0:
            turning = loads.start(hid_in, hid_low)
    for step in range(inner // tile):
        place = slice(step * tile, step * tile + tile)
        ups.append(loads.start(d_up_in.at[:, place], d_up.at[:, place]))
    stores, done = Copies(sem_o), []

    def flush(lanes):
        done.append(stores.start(buffer.at[0, :, :, lanes], own.at[:, :, lanes]))
        done.append(stores.start(buffer.at[1, :, :, lanes], other.at[:, :, lanes]))

    wait_all(begun)
    for step in range(groups):
        acts[step].wait()
        result = dot_lt(act[:, step * width : (step + 1) * width], d_out[...]).astype(BF16)
        lanes = slice(step * half, (step + 1) * half)
        for part in range(2):
            put_rows(table, result[:, part * half : (part + 1) * half], buffer, part, lanes)
        flush(lanes)
    base = groups * half
    turning.wait()
    turned[...] = hid_low[...].T
    for place in range(0, half_up, tile):
        for part in range(2):
            step = (part * half_up + place) // tile
            ups[step].wait()
            result = dot(turned[...], d_up[:, step * tile : (step + 1) * tile]).astype(BF16)
            put_rows(table, result, buffer, part, slice(base + place, base + place + tile))
        flush(slice(base + place, base + place + tile))
    wait_all(done)


def ffn_grads(table, chips, act, d_out, hid_low, d_up):
    rows, inner = act.shape
    width = d_out.shape[1]
    block = width // chips
    groups = inner // width
    cols = groups * width // 2 + inner // 2
    return pl.pallas_call(
        ffn_grads_kernel,
        out_shape=[sds((chips, block, cols), BF16)] * 2,
        in_specs=[SMEM, ANY, ANY, ANY, ANY],
        out_specs=[ANY, ANY],
        scratch_shapes=[
            pltpu.VMEM((rows, inner), BF16),
            pltpu.VMEM((rows, width), BF16),
            pltpu.VMEM((rows, width), BF16),
            pltpu.VMEM((rows, inner), BF16),
            pltpu.VMEM((width, rows), BF16),
            pltpu.VMEM((2, chips, block, cols), BF16),
            pltpu.SemaphoreType.DMA((groups + inner // 768 + 2,)),
            pltpu.SemaphoreType.DMA((2 * groups + 2 * (inner // 1536),)),
        ],
        compiler_params=params(),
        cost_estimate=cost(16),
        name="ffn_grads",
    )(table, act, d_out, hid_low, d_up)


def att_grads_kernel(
    table,
    mixed_short,
    mixed_long,
    d_att_in,
    rows_short,
    rows_long,
    d_short,
    d_query,
    d_own,
    far,
    passed,
    own,
    other,
    columns,
    d_att,
    mixed,
    rows,
    grad,
    turned,
    buffer,
    sem_i,
    sem_o,
    sem_q,
):
    short, width = rows_short.shape
    half = width // 2
    half_qkv = 3 * half
    loads = Copies(sem_i)
    first = [
        loads.start(d_att_in, d_att),
        loads.start(mixed_short, mixed.at[:short, :]),
        loads.start(mixed_long, mixed.at[short:, :]),
    ]
    second = [
        loads.start(rows_short, rows.at[:short, :]),
        loads.start(rows_long, rows.at[short:, :]),
    ]
    third = [
        loads.start(d_query, grad.at[short:, :width]),
        loads.start(d_short, grad.at[:short, :]),
    ]
    total = d_own[...].astype(F32) + far[0].astype(F32) + passed[...].astype(F32)
    grad[short:, width:] = total.astype(BF16)
    stores, done = Copies(sem_o), []

    def flush(lanes):
        done.append(stores.start(buffer.at[0, :, :, lanes], own.at[:, :, lanes]))
        done.append(stores.start(buffer.at[1, :, :, lanes], other.at[:, :, lanes]))

    wait_all(first)
    result = dot_lt(mixed[...], d_att[...]).astype(BF16)
    for part in range(2):
        put_rows(table, result[:, part * half : (part + 1) * half], buffer, part, slice(0, half))
    flush(slice(0, half))
    wait_all(second)
    turned[...] = rows[...].T
    wait_all(third)
    for step in range(3):
        lanes = slice(step * width, (step + 1) * width)
        piece = grad[:, lanes]
        columns[:, lanes] = jnp.sum(piece.astype(F32), axis=0, keepdims=True)
        result = dot(turned[...], piece).astype(BF16)
        for place in range(0, width, half):
            part, start = divmod(step * width + place, half_qkv)
            put_rows(
                table, result[:, place : place + half], buffer, part, slice(half + start, half + start + half)
            )
            far_part = jnp.bitwise_xor(table[2 * buffer.shape[1]], part)
            lanes_out = slice(half + start, half + start + half)
            index = 2 * step + place // half
            for which, target in enumerate((own, other)):

                @pl.when(far_part == which)
                def _(which=which, target=target, lanes_out=lanes_out, index=index):
                    pltpu.make_async_copy(
                        buffer.at[which, :, :, lanes_out], target.at[:, :, lanes_out], sem_q.at[index]
                    ).start()

    for index in range(6):
        part, start = divmod(index * half, half_qkv)
        lanes_out = slice(half + start, half + start + half)
        pltpu.make_async_copy(buffer.at[0, :, :, lanes_out], own.at[:, :, lanes_out], sem_q.at[index]).wait()
    wait_all(done)


def att_grads(
    table, chips, mixed_short, mixed_long, d_att, rows_short, rows_long, d_short, d_query, d_own, far, passed
):
    short, width = rows_short.shape
    rows = short + rows_long.shape[0]
    block = width // chips
    cols = 2 * width
    return pl.pallas_call(
        att_grads_kernel,
        out_shape=[sds((chips, block, cols), BF16)] * 2 + [sds((1, 3 * width), F32)],
        in_specs=[SMEM] + [ANY] * 7 + [VMEM] * 3,
        out_specs=[ANY, ANY, VMEM],
        scratch_shapes=[
            pltpu.VMEM((rows, width), BF16),
            pltpu.VMEM((rows, width), BF16),
            pltpu.VMEM((rows, width), BF16),
            pltpu.VMEM((rows, 3 * width), BF16),
            pltpu.VMEM((width, rows), BF16),
            pltpu.VMEM((2, chips, block, cols), BF16),
            pltpu.SemaphoreType.DMA((7,)),
            pltpu.SemaphoreType.DMA((2,)),
            pltpu.SemaphoreType.DMA((6,)),
        ],
        compiler_params=params(),
        cost_estimate=cost(12),
        name="att_grads",
    )(table, mixed_short, mixed_long, d_att, rows_short, rows_long, d_short, d_query, d_own, far, passed)


def input_grad_kernel(start, table, d_short, d_query, d_own, far, passed, d_first, *rest):
    *weights_in, out_short, out_long, weight, grad, first, out, sems = rest
    copies = Copies(sems)
    short, width = d_short.shape[0], out_short.shape[1]
    loads = []
    if len(weights_in) > 1:
        staged = load_staged(copies, table, weights_in, 0, 3 * width // 2, weight)
    for part in range(3):
        lanes = slice(part * width, (part + 1) * width)
        loads.append([copies.start(d_short.at[:, lanes], grad.at[:short, lanes])])
        if part == 0:
            loads[0].append(copies.start(d_query, grad.at[short:, lanes]))
        if len(weights_in) == 1:
            here = slice(start + part * width, start + (part + 1) * width)
            loads[part].append(copies.start(weights_in[0].at[:, here], weight.at[:, lanes]))
        elif part == 0:
            loads[0] += staged
        if part == 0:
            adding = copies.start(d_first, first)
    total = d_own[...].astype(F32) + far[0].astype(F32) + passed[...].astype(F32)
    grad[short:, width:] = total.astype(BF16)
    done = []
    for part in range(3):
        wait_all(loads[part])
        span = slice(part * width, (part + 1) * width)
        for step in range(width // 256):
            lanes = slice(step * 256, step * 256 + 256)
            total = dot_rt(grad[:, span], weight[lanes, span])
            if part == 0 and step == 0:
                adding.wait()
            if part < 2:
                first[:, lanes] = first[:, lanes] + total
                continue
            out[:, lanes] = (first[:, lanes] + total).astype(out.dtype)
            done.append(copies.start(out.at[:short, lanes], out_short.at[:, lanes]))
            done.append(copies.start(out.at[short:, lanes], out_long.at[:, lanes]))
    wait_all(done)


def input_grad(table, d_short, d_query, d_own, far, passed, d_first, weights, start, dtype):
    rows, width = d_first.shape
    short = d_short.shape[0]
    return pl.pallas_call(
        functools.partial(input_grad_kernel, start),
        out_shape=[sds((short, width), dtype), sds((rows - short, width), dtype)],
        in_specs=[SMEM, ANY, ANY, VMEM, VMEM, VMEM, ANY] + [ANY] * len(weights),
        out_specs=[ANY] * 2,
        scratch_shapes=[
            pltpu.VMEM((width, 3 * width), BF16),
            pltpu.VMEM((rows, 3 * width), BF16),
            pltpu.VMEM((rows, width), F32),
            pltpu.VMEM((rows, width), dtype),
            pltpu.SemaphoreType.DMA((56,)),
        ],
        compiler_params=params(),
        cost_estimate=cost(10),
        name="input_grad",
    )(table, d_short, d_query, d_own, far, passed, d_first, *weights)


def short_backward_kernel(qkv, mixed, d_mixed, raised, inverse, gate, d_qkv, gate_sum):
    low, high = head_masks()
    ones = jnp.concatenate([low, high], axis=0)
    width = mixed.shape[1]
    for pair in range(HEADS // 2):
        lanes = slice(pair * 128, pair * 128 + 128)
        query = qkv[:, lanes] * 0.125
        keys = spread(qkv[:, width + pair * 128 : width + pair * 128 + 128], low, high)
        values = spread(qkv[:, 2 * width + pair * 128 : 2 * width + pair * 128 + 128], low, high)
        grad = d_mixed[:, lanes].astype(F32)
        out = mixed[:, lanes].astype(F32)
        scaled = grad * inverse[:, lanes]
        gate_sum[0, :, lanes] = jnp.sum(grad * out, axis=0, keepdims=True)
        pulled = (scaled * gate[0, :, lanes]).astype(BF16)
        inner = (scaled * out).astype(BF16)
        prob = raised[0, pair]
        bent = dot_rt(jnp.concatenate([pulled, inner], axis=1), jnp.concatenate([values, -ones], axis=1))
        score = (prob.astype(F32) * bent).astype(BF16)
        d_qkv[:, lanes] = (dot(score, keys) * 0.125).astype(BF16)
        turned = dot_lt(query, score)
        turned = jnp.concatenate([turned[:HEAD, :BLOCK], turned[HEAD:, BLOCK:]], axis=0)
        d_qkv[:, width + pair * 128 : width + pair * 128 + 128] = turned.T.astype(BF16)
        turned = dot_lt(pulled, prob)
        turned = jnp.concatenate([turned[:HEAD, :BLOCK], turned[HEAD:, BLOCK:]], axis=0)
        d_qkv[:, 2 * width + pair * 128 : 2 * width + pair * 128 + 128] = turned.T.astype(BF16)


def short_backward(qkv, mixed, d_mixed, raised, inverse, gate):
    rows, width = mixed.shape
    count = rows // BLOCK
    pairs = HEADS // 2
    narrow = pl.BlockSpec((BLOCK, width), lambda i: (i, 0))
    wide = pl.BlockSpec((BLOCK, 3 * width), lambda i: (i, 0))
    vector = pl.BlockSpec((1, 1, width), lambda i: (i, 0, 0))
    return pl.pallas_call(
        short_backward_kernel,
        grid=(count,),
        out_shape=[sds((rows, 3 * width), BF16), sds((count, 1, width), F32)],
        in_specs=[
            wide,
            narrow,
            narrow,
            pl.BlockSpec((1, pairs, BLOCK, 2 * BLOCK), lambda i: (i, 0, 0, 0)),
            narrow,
            vector,
        ],
        out_specs=[wide, vector],
        compiler_params=params(),
        cost_estimate=cost(11.6),
        name="short_backward",
    )(qkv, mixed, d_mixed, raised, inverse, gate)


def long_backward_kernel(blocks, queries, mixed, d_mixed, raised, inverse, parts, gate, *rest):
    sources, (d_query, d_own, d_near, d_core, gate_sum) = rest[:blocks], rest[blocks:]
    low, high = head_masks()
    ones = jnp.concatenate([low, high], axis=0)
    width = mixed.shape[1]
    for pair in range(HEADS // 2):
        lanes = slice(pair * 128, pair * 128 + 128)
        query = queries[:, lanes] * 0.125
        grad = d_mixed[:, lanes].astype(F32)
        out = mixed[:, lanes].astype(F32)
        scaled = grad * inverse[:, lanes]
        inner = (scaled * out).astype(BF16)
        total = 0.0
        for index in range(blocks):
            source = sources[index]
            keys = spread(source[:, lanes], low, high)
            values = spread(source[:, width + pair * 128 : width + pair * 128 + 128], low, high)
            strength = gate[index : index + 1, lanes]
            pulled = (scaled * strength).astype(BF16)
            prob = raised[pair, index]
            bent = dot_rt(jnp.concatenate([pulled, inner], axis=1), jnp.concatenate([values, -ones], axis=1))
            score = (prob.astype(F32) * bent).astype(BF16)
            total = total + dot(score, keys)
            gate_sum[index : index + 1, lanes] = strength * jnp.sum(
                grad * parts[index, :, lanes].astype(F32), axis=0, keepdims=True
            )
            target = (d_own, d_core.at[0], d_near, d_core.at[1])[index]
            turned = dot_lt(query, score)
            turned = jnp.concatenate([turned[:HEAD, :BLOCK], turned[HEAD:, BLOCK:]], axis=0)
            target[:, lanes] = turned.T.astype(BF16)
            turned = dot_lt(pulled, prob)
            turned = jnp.concatenate([turned[:HEAD, :BLOCK], turned[HEAD:, BLOCK:]], axis=0)
            target[:, width + pair * 128 : width + pair * 128 + 128] = turned.T.astype(BF16)
        d_query[:, lanes] = (total * 0.125).astype(BF16)


def long_backward(queries, mixed, d_mixed, raised, inverse, parts, gate, sources):
    rows, width = mixed.shape
    blocks = len(sources)
    return pl.pallas_call(
        functools.partial(long_backward_kernel, blocks),
        out_shape=[
            sds((rows, width), BF16),
            sds((rows, 2 * width), BF16),
            sds((rows, 2 * width), BF16),
            sds((2, rows, 2 * width), BF16),
            sds((blocks, width), F32),
        ],
        in_specs=[VMEM] * (7 + blocks),
        out_specs=[VMEM] * 5,
        compiler_params=params(),
        cost_estimate=cost(8.7),
        name="long_backward",
    )(queries, mixed, d_mixed, raised, inverse, parts, gate, *sources)


class Source:
    def __init__(self, rows, packed, pieces, starts, qkv_start):
        self.rows, self.packed, self.pieces, self.starts, self.qkv_start = rows, packed, pieces, starts, qkv_start

    def qkv(self):
        return self.pieces if self.pieces else (self.packed,)


def on_device(
    plan,
    short_tokens,
    long_tokens,
    short_cotangent,
    long_cotangent,
    qkv_weight,
    out_weight,
    up_weight,
    down_weight,
    vectors,
    up_bias,
    mask_logit,
    short_noise,
    gate_noise,
    block_mask,
    block_order,
):
    shorts, block_rows, width = short_tokens.shape
    blocks = lax.axis_size("seq")
    place = lax.axis_index("seq")
    device = lax.axis_index("dp") * plan.seq + place
    layers = qkv_weight.shape[0]
    inner = up_weight.shape[2]
    own_rows = qkv_weight.shape[1]
    short_rows = shorts * block_rows
    half = width // 2
    half_up = inner // 2
    core = place % 2
    table = plan.tables()
    chips = plan.chips

    per_row = inner // width

    def whole(array):
        return lax.all_gather(array, AXES, axis=0, tiled=True)

    def packed(layer):
        up = up_weight[layer].reshape(own_rows, plan.devices, per_row, own_rows)
        up = up.transpose(0, 2, 1, 3).reshape(own_rows, inner)
        down = down_weight[layer].reshape(per_row, own_rows, width).transpose(1, 0, 2)
        return [out_weight[layer], up, down.reshape(own_rows, inner)]

    def small(layer):
        biases = up_bias[layer].reshape(per_row, own_rows).T
        return jnp.concatenate(
            [vectors[layer], biases, jnp.zeros((own_rows, SMALL - 8 - per_row), BF16)], axis=1
        )

    smalls = [small(layer) for layer in range(layers)]
    sources = []
    for layer in range(layers):
        parts = packed(layer)
        if not plan.staged:
            parts = parts + [qkv_weight[layer]] + (smalls if layer == 0 else [])
        rows = jnp.concatenate(parts, axis=1)
        pieces, qkv_start = (), width + 2 * inner
        if plan.staged:
            qkv_start = None
            sides = [qkv_weight[layer][:, : 3 * half], qkv_weight[layer][:, 3 * half :]]
            if layer == 0:
                sides = [jnp.concatenate([side, extra], axis=1) for side, extra in zip(sides, smalls)]
                earlier = [rows]
            else:
                earlier = [sources[-1].pieces[1], rows]
            pieces = gather(plan, *[after(side, *earlier) for side in sides], core)
        if layer > 0:
            rows = after(rows, sources[-1].packed, *pieces[:1])
        sources.append(Source(rows, whole(rows), pieces, (0, width, width + inner), qkv_start))

    block_ids = jnp.arange(blocks, dtype=jnp.int32)
    near_ids = block_ids ^ place
    placed_ids = block_order[0]
    own_block = jnp.sum(jnp.where(block_ids == place, placed_ids, 0))
    near_int = (near_ids[:, None] == block_ids[None, :]).astype(jnp.int32)
    near_true = jnp.sum(near_int * placed_ids[None, :], axis=1)
    own_hot = (block_ids == own_block).astype(F32)
    near_hot_int = (near_true[:, None] == block_ids[None, :]).astype(jnp.int32)
    near_hot = near_hot_int.astype(F32)
    mask_row = jnp.sum(block_mask[0] * (block_ids == own_block).astype(jnp.int32)[:, None], axis=0)
    opened = jnp.maximum(
        jnp.sum(near_hot_int * mask_row[None, :], axis=1), (block_ids == 0).astype(jnp.int32)
    )
    first_hot = (block_ids == 0).astype(F32)
    corner = first_hot[:, None] * first_hot[None, :]
    highest = lax.Precision.HIGHEST
    logit_near = jnp.einsum(
        "lhij,i,sj->lsh", mask_logit + gate_noise[:, 0], own_hot, near_hot, precision=highest
    )
    gate_long = jax.nn.sigmoid(logit_near)
    gate_short = jax.nn.sigmoid(mask_logit[:, None, :, 0, 0] + short_noise)
    lanes_long = jnp.repeat(gate_long, HEAD, axis=2)
    lanes_short = jnp.repeat(gate_short, HEAD, axis=2)[:, :, None, :]
    head_hot = (jnp.arange(width)[:, None] // HEAD == jnp.arange(HEADS)[None, :]).astype(F32)

    def swap_core(value):
        return lax.ppermute(value, "seq", [(i, i ^ 1) for i in range(blocks)])

    def swap_pair(value):
        return lax.ppermute(value, "seq", [(i, i ^ 2) for i in range(blocks)])

    rows_low = (short_tokens.reshape(short_rows, width), long_tokens[0])
    rows_wide = rows_low
    saved = []
    for layer in range(layers):
        source = sources[layer]
        vec = None if layer == 0 else vecs[layer]
        qkv_short, query_long, kv, *got = project(table, *rows_low, vec, layers, source.qkv(), source.qkv_start)
        if layer == 0:
            vecs = [got[0][which] for which in range(layers)]
            vec = vecs[0]
        kv_core = swap_core(kv)
        kv_pair = swap_pair(kv)
        mixed_short, raised_short, inverse_short = short_forward(qkv_short, lanes_short[layer])
        kv_pair = after(kv_pair, mixed_short)
        key_values = (kv, kv_core, kv_pair, swap_core(kv_pair))
        mixed_long, raised_long, inverse_long, parts = long_forward(
            opened, query_long, lanes_long[layer], key_values
        )
        *y, hid_low, unit1, scale1, unit2, scale2, act, slope = mlp_forward(
            layer + 1 < layers, *rows_wide, mixed_short, mixed_long, vec, inner, source
        )
        saved.append(
            (
                rows_low,
                qkv_short,
                query_long,
                key_values,
                mixed_short,
                raised_short,
                inverse_short,
                mixed_long,
                raised_long,
                inverse_long,
                parts,
                vec,
                hid_low,
                unit1,
                scale1,
                unit2,
                scale2,
                act,
                slope,
            )
        )
        rows_low, rows_wide = y[2:], y[:2]
    outputs = rows_low

    grad = (short_cotangent.reshape(short_rows, width), long_cotangent[0])
    kept = []
    terms = []
    upper = None
    staging = plan.staged
    for layer in reversed(range(layers)):
        last = layer == 0
        source = sources[layer]
        (
            rows_low,
            qkv_short,
            query_long,
            key_values,
            mixed_short,
            raised_short,
            inverse_short,
            mixed_long,
            raised_long,
            inverse_long,
            parts,
            vec,
            hid_low,
            unit1,
            scale1,
            unit2,
            scale2,
            act,
            slope,
        ) = saved[layer]
        second, d_out, sums_ffn, sums_up, d_up = ffn_backward(grad, unit2, scale2, vec, slope, source)
        if upper is not None:
            if staging:
                ffn_upper.wait(d_out)
                ffn_upper.first()
                upper[2] = after(upper[2], ffn_upper.operand, d_out)
            *att, columns = att_grads(table, chips, *upper)
            terms[-1][0] = columns
            if staging:
                att_upper = Reduce(plan, *att)
                ffn_upper.wait(att[0])
                ffn_upper.line()
                d_out = after(d_out, *att, *ffn_upper.operand)
            kept[-1].append(att_upper if staging else att)
        ffn = ffn_grads(table, chips, act, d_out, hid_low, d_up)
        second = after(second, *ffn)
        if staging:
            if upper is not None:
                att_upper.wait(ffn[0])
                att_upper.second()
                second = after(second, att_upper.operand)
            ffn_sum = Reduce(plan, *ffn)
        d_first, d_att, d_mixed_short, d_mixed_long, sums_mid = mid_backward(
            second, d_up, unit1, scale1, vec, source, short_rows
        )
        if staging and upper is not None:
            att_upper.wait(d_att)
            att_upper.first()
            d_mixed_long = after(d_mixed_long, att_upper.operand, *ffn_upper.pending)
        d_query, d_own, d_near, d_core, gate_sum_long = long_backward(
            query_long, mixed_long, d_mixed_long, raised_long, inverse_long, parts, lanes_long[layer], key_values
        )
        far = swap_core(d_core)
        away = (d_near.astype(F32) + far[1].astype(F32)).astype(BF16)
        passed = swap_pair(away)
        if staging:
            ffn_sum.wait(d_query, away)
            ffn_sum.second(passed)
            d_mixed_short = after(d_mixed_short, ffn_sum.operand)
            if upper is not None:
                att_upper.wait(d_query)
                att_upper.line()
                d_mixed_short = after(d_mixed_short, *att_upper.operand)
        d_short, gate_sum_short = short_backward(
            qkv_short, mixed_short, d_mixed_short, raised_short, inverse_short, lanes_short[layer]
        )
        had_upper = upper is not None
        upper = [mixed_short, mixed_long, d_att, *rows_low, d_short, d_query, d_own, far, passed]
        kept.append([ffn_sum if staging else ffn])
        if last:
            *att, columns = att_grads(table, chips, *upper)
            d_first = after(d_first, *att)
            if staging:
                att_sum = Reduce(plan, *att)
                ffn_sum.wait(att[0])
                ffn_sum.first()
                d_first = after(d_first, ffn_sum.operand)
                if had_upper:
                    d_first = after(d_first, *att_upper.pending)
            kept[-1].append(att_sum if staging else att)
        grad = input_grad(
            table,
            d_short,
            d_query,
            d_own,
            far,
            passed,
            d_first,
            source.qkv(),
            source.qkv_start,
            BF16 if last else F32,
        )
        if staging:
            ffn_upper = ffn_sum
            if last:
                ffn_sum.wait(grad[0])
                ffn_sum.line()
                att_sum.wait(grad[0])
                att_sum.second()
        heads = jnp.dot(
            jnp.concatenate([gate_sum_short[:, 0], gate_sum_long]), head_hot, precision=highest
        )
        short_term = jnp.sum(heads[:shorts] * (1.0 - gate_short[layer]), axis=0)
        long_term = heads[shorts:] * (1.0 - gate_long[layer])
        logit_term = (
            jnp.einsum("sh,i,sj->hij", long_term, own_hot, near_hot, precision=highest)
            + short_term[:, None, None] * corner[None]
        )
        terms.append([columns if last else None, sums_mid[2:5], sums_ffn[5:8], sums_up, logit_term])
    kept, terms = kept[::-1], terms[::-1]

    packed_sums = jnp.concatenate(
        [
            jnp.concatenate(
                [
                    rows
                    for columns, mid, ffn, _, _ in terms
                    for rows in (columns[:, :width], columns[:, 2 * width :], mid, ffn)
                ]
            ).reshape(-1, 128),
            jnp.concatenate([term[3] for term in terms]).reshape(-1, 128),
            jnp.stack([term[4] for term in terms]).reshape(-1, 128),
        ]
    )
    count = packed_sums.shape[0]
    packed_sums = jnp.pad(packed_sums, ((0, -count % 8), (0, 0)))
    if staging:
        ffn_sum, att_sum = kept[0]
        sums = Butterfly(plan, packed_sums)
        sums.step()
        sums.step(ffn_sum.operand, att_sum.operand)
        att_sum.first()
        sums.step(att_sum.operand)
        att_sum.wait(*ffn_sum.pending)
        att_sum.line()
        sums.step(*att_sum.operand)
        sums.step(*ffn_sum.pending)
        packed_sums = sums.finish()
    else:
        packed_sums = lax.psum(packed_sums, AXES)
    edge = layers * 8 * width // 128
    more = edge + layers * inner // 128
    vectors_all = packed_sums[:edge].reshape(layers, 8, width)
    vectors_grad = lax.dynamic_slice_in_dim(vectors_all, device * own_rows, own_rows, 2).transpose(0, 2, 1)
    bias_all = packed_sums[edge:more].reshape(layers, per_row, width)
    up_bias_grad = lax.dynamic_slice_in_dim(bias_all, device * own_rows, own_rows, 2).reshape(layers, -1)
    logit_grad = packed_sums[more:count].reshape(mask_logit.shape)

    def scattered(sides):
        rows = jnp.concatenate([side.reshape(width, side.shape[-1]) for side in sides], axis=1)
        rows = lax.psum_scatter(rows, AXES, scatter_dimension=0, tiled=True).astype(F32)
        count = rows.shape[1] // 2
        return rows[:, :count], rows[:, count:]

    def owned(total):
        part = [lax.dynamic_slice_in_dim(total, which * own_rows, own_rows, 0) for which in (core, 1 - core)]
        mine, got = part[0], send(part[1], plan.cores)
        return jnp.where(core == 0, mine, got), jnp.where(core == 0, got, mine)

    qkv_grad, out_grad, up_grad, down_grad = [], [], [], []
    for layer in range(layers):
        ffn, att = kept[layer]
        if staging:
            ffn, att = ffn.finish(), att.finish()
            if layer > 0:
                att = after(att, grad[0], *kept[0][0].operand)
            ffn, att = owned(ffn), owned(att)
            if layer > 0:
                begun = (grad[0], *kept[0][0].operand)
                ffn = after(ffn[0], *begun), after(ffn[1], *begun)
        else:
            ffn, att = scattered(ffn), scattered(att)
        span = per_row * half
        down = [side[:, :span].reshape(own_rows, per_row, half) for side in ffn]
        down = jnp.concatenate(down, axis=2).transpose(1, 0, 2)
        down_grad.append(down.reshape(per_row * own_rows, width))
        up = jnp.concatenate([side[:, span:] for side in ffn], axis=1)
        up = up.reshape(own_rows, per_row, plan.devices, own_rows).transpose(0, 2, 1, 3)
        up_grad.append(up.reshape(own_rows, inner))
        out_grad.append(jnp.concatenate([side[:, :half] for side in att], axis=1))
        qkv_grad.append(jnp.concatenate([side[:, half:] for side in att], axis=1))
    return (
        outputs[0].reshape(shorts, block_rows, width),
        outputs[1][None],
        grad[0].reshape(shorts, block_rows, width),
        grad[1][None],
        jnp.stack(qkv_grad),
        jnp.stack(out_grad),
        jnp.stack(up_grad),
        jnp.stack(down_grad),
        vectors_grad,
        up_bias_grad,
        logit_grad,
    )


def solution(mesh):
    split = ("dp", "seq")
    in_specs = (
        P(split, None, None),
        P("dp", "seq", None),
        P(split, None, None),
        P("dp", "seq", None),
        P(None, split, None),
        P(None, split, None),
        P(None, split, None),
        P(None, split, None),
        P(None, split, None),
        P(None, split),
        P(),
        P(None, split, None),
        P(None, "dp", None, None, None),
        P("dp", None, None),
        P("dp", None),
    )
    out_specs = (
        P(split, None, None),
        P("dp", "seq", None),
        P(split, None, None),
        P("dp", "seq", None),
        P(None, split, None),
        P(None, split, None),
        P(None, split, None),
        P(None, split, None),
        P(None, split, None),
        P(None, split),
        P(),
    )

    def build(*arrays):
        plan = Plan(mesh, arrays[4].shape[1])
        return jax.shard_map(
            functools.partial(on_device, plan),
            mesh=mesh,
            in_specs=in_specs,
            out_specs=out_specs,
            check_vma=False,
        )(*arrays)

    return build
```

```python
import functools

import jax
import jax.numpy as jnp
from jax import lax
from jax.experimental import pallas as pl
from jax.experimental.pallas import tpu as pltpu
from jax.sharding import PartitionSpec as P

HEADS = 12
HEAD = 64
BLOCK = 128
AXES = ("dp", "seq")
BF16 = jnp.bfloat16
F32 = jnp.float32
VMEM = pl.BlockSpec(memory_space=pltpu.VMEM)
SMEM = pl.BlockSpec(memory_space=pltpu.SMEM)
ANY = pl.BlockSpec(memory_space=pl.ANY)
SMALL = 128
ROOT_HALF = 0.7071067811865476
ROOT_TWO_PI_INV = 0.3989422804014327


def sds(shape, dtype):
    return jax.ShapeDtypeStruct(shape, dtype)


def params(mib=60):
    return pltpu.CompilerParams(vmem_limit_bytes=mib * 2**20)


def cost(us):
    return pl.CostEstimate(flops=int(us * 0.5e9), bytes_accessed=int(us * 3.3e6), transcendentals=0)


def dot(left, right):
    return jnp.dot(left, right, preferred_element_type=F32)


def dot_rt(left, right):
    return lax.dot_general(left, right, (((1,), (1,)), ((), ())), preferred_element_type=F32)


def dot_lt(left, right):
    return lax.dot_general(left, right, (((0,), (0,)), ((), ())), preferred_element_type=F32)


class Plan:
    def __init__(self, mesh, width):
        dp, seq = mesh.shape["dp"], mesh.shape["seq"]
        self.dp, self.seq, self.devices = dp, seq, dp * seq
        depth = dp // 2
        chips = depth * 4
        self.staged = (
            seq == 4
            and dp % 2 == 0
            and depth & (depth - 1) == 0
            and width % chips == 0
            and (width // chips) % 16 == 0
        )
        self.depth, self.chips = depth, chips if self.staged else 16
        if self.staged:
            self.z_perms = [self.flip(z=step) for step in range(1, depth)]
            self.first = self.flip_by_core((0, 1), (1, 0))
            self.second = self.flip_by_core((1, 0), (0, 1))
            self.cores = self.flip(core=1)

    def flip(self, z=0, x=0, y=0, core=0):
        pairs = []
        for dev in range(self.devices):
            pairs.append((dev, dev ^ (z * 8 + x * 4 + y * 2 + core)))
        return pairs

    def flip_by_core(self, even, odd):
        pairs = []
        for dev in range(self.devices):
            x, y = even if dev % 2 == 0 else odd
            pairs.append((dev, dev ^ (x * 4 + y * 2)))
        return pairs

    def tables(self):
        slots = jnp.arange(self.chips, dtype=jnp.int32)
        if not self.staged:
            return jnp.concatenate([slots, slots, jnp.zeros((8,), jnp.int32), slots, slots])
        me = lax.axis_index("dp") * 4 + lax.axis_index("seq")
        core, chip = me % 2, me // 2
        away = slots ^ chip
        z, x, y = away // 4, (away // 2) % 2, away % 2
        y_slot = (x * 2 + y) * self.depth + z
        x_slot = (y * 2 + x) * self.depth + z
        steps, a, b = slots % self.depth, (slots // self.depth) % 2, slots // (2 * self.depth)
        y_chip = (steps * 4 + b * 2 + a) ^ chip
        x_chip = (steps * 4 + a * 2 + b) ^ chip
        even = core == 0
        return jnp.concatenate(
            [
                jnp.where(even, y_slot, x_slot),
                jnp.where(even, x_slot, y_slot),
                jnp.full((8,), core, jnp.int32),
                jnp.where(even, y_chip, x_chip),
                jnp.where(even, x_chip, y_chip),
            ]
        ).astype(jnp.int32)


def gather(plan, first, second, core):
    even = core == 0
    got = send(jnp.where(even, second, first), plan.cores)
    mine = jnp.where(even, first, second)
    base = jnp.where(even, jnp.concatenate([mine, got]), jnp.concatenate([got, mine]))
    line = jnp.stack([base] + [send(base, pairs) for pairs in plan.z_perms])
    near = jnp.concatenate([line, send(line, plan.first)])
    far = send(near, plan.second)
    return (near, far, send(near, plan.cores), send(far, plan.cores))


def send(value, pairs):
    return lax.ppermute(value, AXES, pairs)


def after(value, *earlier):
    return lax.optimization_barrier((value, *earlier))[0]


class Reduce:
    def __init__(self, plan, own, other):
        self.plan, self.own = plan, own
        self.part = plan.chips // 2
        self.quarter = self.part // 2
        self.pending = send(other, plan.cores)

    def wait(self, *values):
        if isinstance(self.pending, list):
            self.pending = [after(value, *values) for value in self.pending]
        else:
            self.pending = after(self.pending, *values)

    def second(self, *earlier):
        part = self.part
        self.got = self.pending
        away = self.own[part:].astype(F32) + self.got[part:].astype(F32)
        self.operand = after(away.astype(BF16), *earlier) if earlier else away.astype(BF16)
        self.pending = send(self.operand, self.plan.second)

    def first(self):
        part, quarter = self.part, self.quarter
        self.got_b = self.pending
        near = self.own[quarter:part].astype(F32) + self.got[quarter:part].astype(F32)
        near = near + self.got_b[quarter:].astype(F32)
        self.operand = near.astype(BF16)
        self.pending = send(self.operand, self.plan.first)

    def line(self):
        quarter = self.quarter
        line = self.own[:quarter].astype(F32) + self.got[:quarter].astype(F32)
        line = line + self.got_b[:quarter].astype(F32) + self.pending.astype(F32)
        low = line.astype(BF16)
        self.total = line[0]
        self.operand = lax.optimization_barrier(tuple(low[step] for step in range(1, self.plan.depth)))
        self.pending = [send(part, pairs) for part, pairs in zip(self.operand, self.plan.z_perms)]

    def finish(self):
        total = self.total
        for value in self.pending:
            total = total + value.astype(F32)
        return total


class Butterfly:
    def __init__(self, plan, value):
        self.plan, self.value, self.bit, self.pending = plan, value, 1, None

    def step(self, *earlier):
        if self.pending is not None:
            self.value = self.value + after(self.pending, *earlier)
        self.pending = None
        if self.bit < self.plan.devices:
            pairs = [(dev, dev ^ self.bit) for dev in range(self.plan.devices)]
            self.pending = send(self.value, pairs)
            self.bit *= 2

    def finish(self):
        while self.pending is not None:
            self.step()
        return self.value


class Copies:
    def __init__(self, sems):
        self.sems, self.count = sems, 0

    def start(self, source, target):
        copy = pltpu.make_async_copy(source, target, self.sems.at[self.count])
        self.count += 1
        copy.start()
        return copy


def wait_all(copies):
    for copy in copies:
        copy.wait()


def load_staged(copies, table, pieces, low, high, target):
    begun = []
    slots, rows, _ = pieces[0].shape
    count = 2 * slots
    core = table[2 * count]
    for place, piece in enumerate(pieces):
        half = core if place < 2 else 1 - core
        lanes = pl.ds(pl.multiple_of(half * (high - low), 128), high - low)
        for slot in range(slots):
            chip = table[2 * count + 8 + place * slots + slot]
            here = pl.ds(pl.multiple_of(chip * rows, 16), rows)
            begun.append(copies.start(piece.at[slot, :, low:high], target.at[here, lanes]))
    return begun


def project_kernel(start, given, table, rows_short, rows_long, *rest):
    if given:
        vec, *weights_in, out_short, out_query, out_kv, rows, weight, out, small, sems = rest
    else:
        *weights_in, out_short, out_query, out_kv, vec, rows, weight, out, small, sems = rest
    copies = Copies(sems)
    short, width = rows_short.shape
    begun = [
        copies.start(rows_short, rows.at[:short, :]),
        copies.start(rows_long, rows.at[short:, :]),
    ]
    loads = []
    half = 3 * width // 2
    if len(weights_in) > 1:
        begun += load_staged(copies, table, weights_in, 0, half, weight)
        if not given:
            begun += load_staged(copies, table, weights_in, half, half + SMALL, small)
    else:
        if not given:
            here = slice(start + 3 * width, start + 3 * width + small.shape[1])
            begun.append(copies.start(weights_in[0].at[:, here], small))
        for part in range(3):
            here = slice(start + part * width, start + (part + 1) * width)
            loads.append(
                copies.start(weights_in[0].at[:, here], weight.at[:, part * width : (part + 1) * width])
            )
    wait_all(begun)
    if not given:
        turned = small[...].T
        for layer in range(small.shape[1] // SMALL):
            vec[layer] = turned[layer * SMALL : layer * SMALL + 16, :].astype(F32)
        first = vec.at[0]
    else:
        first = vec
    done = []
    for part in range(3):
        lanes = slice(part * width, (part + 1) * width)
        wait_all(loads[part : part + 1])
        result = dot(rows[...], weight[:, lanes])
        if part != 1:
            result = result + first[part // 2 : part // 2 + 1, :]
        out[:, lanes] = result.astype(BF16)
        if part == 0:
            target = out_query
        else:
            target = out_kv.at[:, (part - 1) * width : part * width]
        done.append(copies.start(out.at[short:, lanes], target))
        done.append(copies.start(out.at[:short, lanes], out_short.at[:, lanes]))
    wait_all(done)


def project(table, rows_short, rows_long, vec, layers, weights, start):
    short, width = rows_short.shape
    count = short + rows_long.shape[0]
    given = vec is not None
    return pl.pallas_call(
        functools.partial(project_kernel, start, given),
        out_shape=[
            sds((short, 3 * width), BF16),
            sds((count - short, width), BF16),
            sds((count - short, 2 * width), BF16),
        ]
        + ([] if given else [sds((layers, 16, width), F32)]),
        in_specs=[SMEM, ANY, ANY] + [VMEM] * given + [ANY] * len(weights),
        out_specs=[ANY] * 3 + [VMEM] * (not given),
        scratch_shapes=[
            pltpu.VMEM((count, width), BF16),
            pltpu.VMEM((width, 3 * width), BF16),
            pltpu.VMEM((count, 3 * width), BF16),
            pltpu.VMEM((width, layers * SMALL), BF16),
            pltpu.SemaphoreType.DMA((80,)),
        ],
        compiler_params=params(),
        cost_estimate=cost(10),
        name="project",
    )(table, rows_short, rows_long, *([vec] if given else []), *weights)


def head_masks():
    lane = lax.broadcasted_iota(jnp.int32, (BLOCK, BLOCK), 1)
    low = jnp.where(lane < HEAD, 1.0, 0.0).astype(BF16)
    high = jnp.where(lane < HEAD, 0.0, 1.0).astype(BF16)
    return low, high


def spread(pair, low, high):
    return jnp.concatenate([pair * low, pair * high], axis=0)


def short_forward_kernel(qkv, gate, mixed, raised, inverse):
    low, high = head_masks()
    ones = jnp.concatenate([low, high], axis=0)
    width = mixed.shape[1]
    for pair in range(HEADS // 2):
        lanes = slice(pair * 128, pair * 128 + 128)
        query = qkv[:, lanes] * 0.125
        keys = spread(qkv[:, width + pair * 128 : width + pair * 128 + 128], low, high)
        values = spread(qkv[:, 2 * width + pair * 128 : 2 * width + pair * 128 + 128], low, high)
        scores = dot_rt(query, keys)
        left, right = scores[:, :BLOCK], scores[:, BLOCK:]
        left = jnp.exp(left - jnp.max(left, axis=1, keepdims=True))
        right = jnp.exp(right - jnp.max(right, axis=1, keepdims=True))
        prob = jnp.concatenate([left, right], axis=1).astype(BF16)
        both = dot(prob, jnp.concatenate([values, ones], axis=1))
        inv = 1.0 / both[:, BLOCK:]
        raised[0, pair] = prob
        inverse[:, lanes] = inv
        mixed[:, lanes] = (both[:, :BLOCK] * inv * gate[0, :, lanes]).astype(BF16)


def short_forward(qkv, gate):
    rows = qkv.shape[0]
    width = qkv.shape[1] // 3
    count = rows // BLOCK
    pairs = HEADS // 2
    return pl.pallas_call(
        short_forward_kernel,
        grid=(count,),
        out_shape=[
            sds((rows, width), BF16),
            sds((count, pairs, BLOCK, 2 * BLOCK), BF16),
            sds((rows, width), F32),
        ],
        in_specs=[
            pl.BlockSpec((BLOCK, 3 * width), lambda i: (i, 0)),
            pl.BlockSpec((1, 1, width), lambda i: (i, 0, 0)),
        ],
        out_specs=[
            pl.BlockSpec((BLOCK, width), lambda i: (i, 0)),
            pl.BlockSpec((1, pairs, BLOCK, 2 * BLOCK), lambda i: (i, 0, 0, 0)),
            pl.BlockSpec((BLOCK, width), lambda i: (i, 0)),
        ],
        compiler_params=params(),
        cost_estimate=cost(7),
        name="short_forward",
    )(qkv, gate)


def long_forward_kernel(blocks, opened, queries, gate, *rest):
    sources, (mixed, raised, inverse, parts) = rest[:blocks], rest[blocks:]
    low, high = head_masks()
    ones = jnp.concatenate([low, high], axis=0)
    width = mixed.shape[1]
    for pair in range(HEADS // 2):
        lanes = slice(pair * 128, pair * 128 + 128)
        query = queries[:, lanes] * 0.125
        scores, values = [], []
        for index in range(blocks):
            source = sources[index]
            keys = spread(source[:, lanes], low, high)
            values.append(spread(source[:, width + pair * 128 : width + pair * 128 + 128], low, high))
            score = dot_rt(query, keys)
            scores.append(jnp.where(opened[index] > 0, score, -1e30))
        top = functools.reduce(jnp.maximum, scores)
        top_left = jnp.max(top[:, :BLOCK], axis=1, keepdims=True)
        top_right = jnp.max(top[:, BLOCK:], axis=1, keepdims=True)
        both = []
        for index in range(blocks):
            left = jnp.exp(scores[index][:, :BLOCK] - top_left)
            right = jnp.exp(scores[index][:, BLOCK:] - top_right)
            prob = jnp.concatenate([left, right], axis=1).astype(BF16)
            raised[pair, index] = prob
            both.append(dot(prob, jnp.concatenate([values[index], ones], axis=1)))
        inv = 1.0 / sum(value[:, BLOCK:] for value in both)
        inverse[:, lanes] = inv
        total = 0.0
        for index in range(blocks):
            part = both[index][:, :BLOCK] * inv
            parts[index, :, lanes] = part.astype(BF16)
            total = total + part * gate[index : index + 1, lanes]
        mixed[:, lanes] = total.astype(BF16)


def long_forward(opened, queries, gate, sources):
    rows, width = queries.shape
    blocks = len(sources)
    return pl.pallas_call(
        functools.partial(long_forward_kernel, blocks),
        out_shape=[
            sds((rows, width), BF16),
            sds((HEADS // 2, blocks, BLOCK, 2 * BLOCK), BF16),
            sds((rows, width), F32),
            sds((blocks, rows, width), BF16),
        ],
        in_specs=[SMEM, VMEM, VMEM] + [VMEM] * blocks,
        out_specs=[VMEM] * 4,
        compiler_params=params(),
        cost_estimate=cost(5.3),
        name="long_forward",
    )(opened, queries, gate, *sources)


def norm_rows(rows, gain, shift):
    inverse = 1.0 / rows.shape[1]
    center = rows - jnp.sum(rows, axis=1, keepdims=True) * inverse
    spread_ = jnp.sum(center * center, axis=1, keepdims=True) * inverse
    scale = lax.rsqrt(spread_ + 1e-05)
    unit = center * scale
    return unit, scale, unit * gain + shift


def mlp_forward_kernel(
    wide,
    starts,
    rows_short,
    rows_long,
    mixed_short,
    mixed_long,
    vec,
    packed,
    *rest,
):
    (
        y_short,
        y_long,
        y_low_short,
        y_low_long,
        hid_low_out,
        unit1_out,
        scale1,
        unit2_out,
        scale2,
        act_out,
        slope_out,
        weight_out,
        weight_up,
        weight_down,
        mixed,
        hidden,
        hid_low,
        unit,
        y_low,
        act,
        slope,
        sems,
        sem_w,
        sem_o,
        sem_y,
    ) = rest
    out_start, up_start, down_start = starts
    copies = Copies(sems)
    total, width = hidden.shape
    inner = act.shape[1]
    short = rows_short.shape[0]
    tile = width
    steps = inner // tile
    begun = [
        copies.start(mixed_short, mixed.at[:short, :]),
        copies.start(mixed_long, mixed.at[short:, :]),
        copies.start(packed.at[:, out_start : out_start + width], weight_out),
    ]
    downs = []
    for step in range(steps):
        lanes = slice(step * tile, (step + 1) * tile)
        here = slice(up_start + step * tile, up_start + (step + 1) * tile)
        pltpu.make_async_copy(packed.at[:, here], weight_up.at[:, lanes], sem_w.at[step]).start()
    for group in range(inner // width):
        start = down_start + group * width
        downs.append(
            copies.start(packed.at[:, start : start + width], weight_down.at[group * width : (group + 1) * width, :])
        )
    wait_all(begun)
    for step in range(width // 256):
        lanes = slice(step * 256, step * 256 + 256)
        summed = dot(mixed[...], weight_out[:, lanes]) + vec[2:3, lanes]
        hidden[:short, lanes] = summed[:short] + rows_short[:, lanes].astype(F32)
        hidden[short:, lanes] = summed[short:] + rows_long[:, lanes].astype(F32)

    @pl.loop(0, total // BLOCK)
    def _(step):
        here = pl.ds(pl.multiple_of(step * BLOCK, BLOCK), BLOCK)
        level, scale, hid = norm_rows(hidden[here, :], vec[3:4, :], vec[4:5, :])
        unit[here, :] = level.astype(BF16)
        scale1[here, :] = scale
        hidden[here, :] = hid
        hid_low[here, :] = hid.astype(BF16)

    done = [copies.start(unit, unit1_out), copies.start(hid_low, hid_low_out)]

    @pl.loop(0, steps, unroll=True)
    def _(step):
        place = pl.ds(pl.multiple_of(step * tile, tile), tile)
        pltpu.make_async_copy(weight_up.at[:, place], weight_up.at[:, place], sem_w.at[step]).wait()
        upper = dot(hid_low[...], weight_up[:, place]) + vec[pl.ds(8 + step, 1), :]
        below = 0.5 + 0.5 * lax.erf(upper * ROOT_HALF)
        act[:, place] = (upper * below).astype(BF16)
        bell = ROOT_TWO_PI_INV * jnp.exp(-0.5 * upper * upper)
        slope[:, place] = (below + upper * bell).astype(BF16)
        pltpu.make_async_copy(act.at[:, place], act_out.at[:, place], sem_o.at[0, step]).start()
        pltpu.make_async_copy(slope.at[:, place], slope_out.at[:, place], sem_o.at[1, step]).start()

    wait_all(downs)
    for step in range(width // 256):
        lanes = slice(step * 256, step * 256 + 256)
        hidden[:, lanes] = hidden[:, lanes] + dot(act[...], weight_down[:, lanes]) + vec[5:6, lanes]
    wait_all(done)

    @pl.loop(0, total // BLOCK)
    def _(step):
        here = pl.ds(pl.multiple_of(step * BLOCK, BLOCK), BLOCK)
        level, scale, y = norm_rows(hidden[here, :], vec[6:7, :], vec[7:8, :])
        unit[here, :] = level.astype(BF16)
        scale2[here, :] = scale
        hidden[here, :] = y
        y_low[here, :] = y.astype(BF16)
        if wide:

            @pl.when(step < short // BLOCK)
            def _():
                pltpu.make_async_copy(hidden.at[here, :], y_short.at[here, :], sem_y.at[step]).start()

    done = [
        copies.start(unit, unit2_out),
        copies.start(y_low.at[:short, :], y_low_short),
        copies.start(y_low.at[short:, :], y_low_long),
    ]
    if wide:
        done.append(copies.start(hidden.at[short:, :], y_long))

        @pl.loop(0, short // BLOCK)
        def _(step):
            here = pl.ds(pl.multiple_of(step * BLOCK, BLOCK), BLOCK)
            pltpu.make_async_copy(hidden.at[here, :], y_short.at[here, :], sem_y.at[step]).wait()

    @pl.loop(0, steps)
    def _(step):
        place = pl.ds(pl.multiple_of(step * tile, tile), tile)
        pltpu.make_async_copy(act.at[:, place], act_out.at[:, place], sem_o.at[0, step]).wait()
        pltpu.make_async_copy(slope.at[:, place], slope_out.at[:, place], sem_o.at[1, step]).wait()

    wait_all(done)


def mlp_forward(wide, rows_short, rows_long, mixed_short, mixed_long, vec, inner, source):
    rows = rows_short.shape[0] + rows_long.shape[0]
    width = rows_short.shape[1]
    return pl.pallas_call(
        functools.partial(mlp_forward_kernel, wide, source.starts),
        out_shape=[
            sds(rows_short.shape if wide else (8, 128), F32),
            sds(rows_long.shape if wide else (8, 128), F32),
            sds(rows_short.shape, BF16),
            sds(rows_long.shape, BF16),
            sds((rows, width), BF16),
            sds((rows, width), BF16),
            sds((rows, 1), F32),
            sds((rows, width), BF16),
            sds((rows, 1), F32),
            sds((rows, inner), BF16),
            sds((rows, inner), BF16),
        ],
        in_specs=[VMEM, VMEM, ANY, ANY, VMEM, ANY],
        out_specs=[ANY] * 6 + [VMEM, ANY, VMEM, ANY, ANY],
        scratch_shapes=[
            pltpu.VMEM((width, width), BF16),
            pltpu.VMEM((width, inner), BF16),
            pltpu.VMEM((inner, width), BF16),
            pltpu.VMEM((rows, width), BF16),
            pltpu.VMEM((rows, width), F32),
            pltpu.VMEM((rows, width), BF16),
            pltpu.VMEM((rows, width), BF16),
            pltpu.VMEM((rows, width), BF16),
            pltpu.VMEM((rows, inner), BF16),
            pltpu.VMEM((rows, inner), BF16),
            pltpu.SemaphoreType.DMA((24,)),
            pltpu.SemaphoreType.DMA((inner // width,)),
            pltpu.SemaphoreType.DMA((2, inner // width)),
            pltpu.SemaphoreType.DMA((rows // BLOCK,)),
        ],
        compiler_params=params(),
        cost_estimate=cost(28),
        name="mlp_forward",
    )(rows_short, rows_long, mixed_short, mixed_long, vec, source.packed)


def norm_back(grad, unit, scale, gain):
    inverse = 1.0 / grad.shape[1]
    pulled = grad * gain
    mean = jnp.sum(pulled, axis=1, keepdims=True) * inverse
    along = jnp.sum(pulled * unit, axis=1, keepdims=True) * inverse
    return scale * (pulled - mean - unit * along)


def ffn_backward_kernel(
    down_start,
    grad_short,
    grad_long,
    unit2,
    scale2,
    vec,
    slope_in,
    packed,
    second_out,
    d_out_out,
    sums,
    sums_up,
    d_up_out,
    weight,
    second,
    d_out,
    slope,
    d_up,
    sems,
    sem_w,
    sem_s,
    sem_o,
):
    copies = Copies(sems)
    total, width = second.shape
    inner = slope.shape[1]
    short = grad_short.shape[0]
    tile = 512
    steps = inner // tile
    loads = []
    for group in range(inner // width):
        start = down_start + group * width
        loads.append(
            copies.start(packed.at[:, start : start + width], weight.at[group * width : (group + 1) * width, :])
        )
    for step in range(steps):
        lanes = slice(step * tile, (step + 1) * tile)
        pltpu.make_async_copy(slope_in.at[:, lanes], slope.at[:, lanes], sem_s.at[step]).start()
    sums[...] = jnp.zeros_like(sums)

    def begin(here, grad):
        dy = grad.astype(F32)
        unit = unit2[here, :].astype(F32)
        dr = norm_back(dy, unit, scale2[here, :], vec[6:7, :])
        second[here, :] = dr
        low = dr.astype(BF16)
        d_out[here, :] = low
        sums[5:6, :] += jnp.sum(low.astype(F32), axis=0, keepdims=True)
        sums[6:7, :] += jnp.sum(dy * unit, axis=0, keepdims=True)
        sums[7:8, :] += jnp.sum(dy, axis=0, keepdims=True)

    @pl.loop(0, short // BLOCK)
    def _(step):
        here = pl.ds(pl.multiple_of(step * BLOCK, BLOCK), BLOCK)
        begin(here, grad_short[here, :])

    begin(slice(short, total), grad_long[...])
    done = [copies.start(second, second_out), copies.start(d_out, d_out_out)]
    wait_all(loads)

    @pl.loop(0, steps, unroll=True)
    def _(step):
        place = pl.ds(pl.multiple_of(step * tile, tile), tile)
        pltpu.make_async_copy(slope_in.at[:, place], slope.at[:, place], sem_s.at[step]).wait()
        low = (dot_rt(d_out[...], weight[place, :]) * slope[:, place].astype(F32)).astype(BF16)
        d_up[:, place] = low
        sums_up[:, place] = jnp.sum(low.astype(F32), axis=0, keepdims=True)
        pltpu.make_async_copy(d_up.at[:, place], d_up_out.at[:, place], sem_o.at[step]).start()

    @pl.loop(0, steps)
    def _(step):
        place = pl.ds(pl.multiple_of(step * tile, tile), tile)
        pltpu.make_async_copy(d_up.at[:, place], d_up_out.at[:, place], sem_o.at[step]).wait()

    wait_all(done)


def ffn_backward(grad, unit2, scale2, vec, slope, source):
    rows, width = unit2.shape
    inner = slope.shape[1]
    return pl.pallas_call(
        functools.partial(ffn_backward_kernel, source.starts[2]),
        out_shape=[
            sds((rows, width), F32),
            sds((rows, width), BF16),
            sds((8, width), F32),
            sds((1, inner), F32),
            sds((rows, inner), BF16),
        ],
        in_specs=[VMEM] * 5 + [ANY, ANY],
        out_specs=[ANY, ANY, VMEM, VMEM, ANY],
        scratch_shapes=[
            pltpu.VMEM((inner, width), BF16),
            pltpu.VMEM((rows, width), F32),
            pltpu.VMEM((rows, width), BF16),
            pltpu.VMEM((rows, inner), BF16),
            pltpu.VMEM((rows, inner), BF16),
            pltpu.SemaphoreType.DMA((inner // width + 2,)),
            pltpu.SemaphoreType.DMA((1,)),
            pltpu.SemaphoreType.DMA((inner // 512,)),
            pltpu.SemaphoreType.DMA((inner // 512,)),
        ],
        compiler_params=params(),
        cost_estimate=cost(14),
        name="ffn_backward",
    )(*grad, unit2, scale2, vec, slope, source.packed)


def mid_backward_kernel(starts, second_in, d_up_in, unit1_in, scale1, vec, packed, *rest):
    (
        d_first_out,
        d_att_out,
        d_mixed_short,
        d_mixed_long,
        sums,
        weight_out,
        weight_up,
        second,
        partial,
        unit1,
        d_up,
        d_att,
        d_mixed,
        sems,
    ) = rest
    out_start, up_start, _ = starts
    copies = Copies(sems)
    total, width = second.shape
    inner = d_up.shape[1]
    short = d_mixed_short.shape[0]
    spans = [slice(0, width), slice(width, inner)]
    loads = []
    for span in spans:
        here = slice(up_start + span.start, up_start + span.stop)
        loads.append(
            [
                copies.start(d_up_in.at[:, span], d_up.at[:, span]),
                copies.start(packed.at[:, here], weight_up.at[:, span]),
            ]
        )
    rest = [
        copies.start(second_in, second),
        copies.start(unit1_in, unit1),
        copies.start(packed.at[:, out_start : out_start + width], weight_out),
    ]
    sums[...] = jnp.zeros_like(sums)
    for part, span in enumerate(spans):
        wait_all(loads[part])
        for step in range(width // 256):
            lanes = slice(step * 256, step * 256 + 256)
            piece = dot_rt(d_up[:, span], weight_up[lanes, span])
            partial[:, lanes] = piece if part == 0 else partial[:, lanes] + piece
    wait_all(rest)

    @pl.loop(0, total // BLOCK)
    def _(step):
        here = pl.ds(pl.multiple_of(step * BLOCK, BLOCK), BLOCK)
        dh = second[here, :] + partial[here, :]
        unit = unit1[here, :].astype(F32)
        dr = norm_back(dh, unit, scale1[here, :], vec[3:4, :])
        second[here, :] = dr
        low = dr.astype(BF16)
        d_att[here, :] = low
        sums[2:3, :] += jnp.sum(low.astype(F32), axis=0, keepdims=True)
        sums[3:4, :] += jnp.sum(dh * unit, axis=0, keepdims=True)
        sums[4:5, :] += jnp.sum(dh, axis=0, keepdims=True)

    done = [copies.start(second, d_first_out), copies.start(d_att, d_att_out)]
    for step in range(width // 256):
        lanes = slice(step * 256, step * 256 + 256)
        d_mixed[:, lanes] = dot_rt(d_att[...], weight_out[lanes, :]).astype(BF16)
        done.append(copies.start(d_mixed.at[:short, lanes], d_mixed_short.at[:, lanes]))
        done.append(copies.start(d_mixed.at[short:, lanes], d_mixed_long.at[:, lanes]))
    wait_all(done)


def mid_backward(second, d_up, unit1, scale1, vec, source, short):
    rows, width = second.shape
    inner = d_up.shape[1]
    return pl.pallas_call(
        functools.partial(mid_backward_kernel, source.starts),
        out_shape=[
            sds((rows, width), F32),
            sds((rows, width), BF16),
            sds((short, width), BF16),
            sds((rows - short, width), BF16),
            sds((8, width), F32),
        ],
        in_specs=[ANY, ANY, ANY, VMEM, VMEM, ANY],
        out_specs=[ANY] * 4 + [VMEM],
        scratch_shapes=[
            pltpu.VMEM((width, width), BF16),
            pltpu.VMEM((width, inner), BF16),
            pltpu.VMEM((rows, width), F32),
            pltpu.VMEM((rows, width), F32),
            pltpu.VMEM((rows, width), BF16),
            pltpu.VMEM((rows, inner), BF16),
            pltpu.VMEM((rows, width), BF16),
            pltpu.VMEM((rows, width), BF16),
            pltpu.SemaphoreType.DMA((24,)),
        ],
        compiler_params=params(),
        cost_estimate=cost(14),
        name="mid_backward",
    )(second, d_up, unit1, scale1, vec, source.packed)


def put_rows(table, result, buffer, part, lanes):
    chips, block = buffer.shape[1:3]
    far = jnp.bitwise_xor(table[2 * chips], part)
    for chip in range(chips):
        slot = table[far * chips + chip]
        buffer[far, slot, :, lanes] = result[chip * block : (chip + 1) * block, :]


def ffn_grads_kernel(
    table, act_in, d_out_in, hid_in, d_up_in, own, other, act, d_out, hid_low, d_up, turned, buffer, sem_i, sem_o
):
    inner = act.shape[1]
    width = d_out.shape[1]
    half_up, half = inner // 2, width // 2
    groups = inner // width
    tile = 768
    loads, ups = Copies(sem_i), []
    begun = [loads.start(d_out_in, d_out)]
    acts = []
    for step in range(groups):
        place = slice(step * width, step * width + width)
        acts.append(loads.start(act_in.at[:, place], act.at[:, place]))
        if step == 0:
            turning = loads.start(hid_in, hid_low)
    for step in range(inner // tile):
        place = slice(step * tile, step * tile + tile)
        ups.append(loads.start(d_up_in.at[:, place], d_up.at[:, place]))
    stores, done = Copies(sem_o), []

    def flush(lanes):
        done.append(stores.start(buffer.at[0, :, :, lanes], own.at[:, :, lanes]))
        done.append(stores.start(buffer.at[1, :, :, lanes], other.at[:, :, lanes]))

    wait_all(begun)
    for step in range(groups):
        acts[step].wait()
        result = dot_lt(act[:, step * width : (step + 1) * width], d_out[...]).astype(BF16)
        lanes = slice(step * half, (step + 1) * half)
        for part in range(2):
            put_rows(table, result[:, part * half : (part + 1) * half], buffer, part, lanes)
        flush(lanes)
    base = groups * half
    turning.wait()
    turned[...] = hid_low[...].T
    for place in range(0, half_up, tile):
        for part in range(2):
            step = (part * half_up + place) // tile
            ups[step].wait()
            result = dot(turned[...], d_up[:, step * tile : (step + 1) * tile]).astype(BF16)
            put_rows(table, result, buffer, part, slice(base + place, base + place + tile))
        flush(slice(base + place, base + place + tile))
    wait_all(done)


def ffn_grads(table, chips, act, d_out, hid_low, d_up):
    rows, inner = act.shape
    width = d_out.shape[1]
    block = width // chips
    groups = inner // width
    cols = groups * width // 2 + inner // 2
    return pl.pallas_call(
        ffn_grads_kernel,
        out_shape=[sds((chips, block, cols), BF16)] * 2,
        in_specs=[SMEM, ANY, ANY, ANY, ANY],
        out_specs=[ANY, ANY],
        scratch_shapes=[
            pltpu.VMEM((rows, inner), BF16),
            pltpu.VMEM((rows, width), BF16),
            pltpu.VMEM((rows, width), BF16),
            pltpu.VMEM((rows, inner), BF16),
            pltpu.VMEM((width, rows), BF16),
            pltpu.VMEM((2, chips, block, cols), BF16),
            pltpu.SemaphoreType.DMA((groups + inner // 768 + 2,)),
            pltpu.SemaphoreType.DMA((2 * groups + 2 * (inner // 1536),)),
        ],
        compiler_params=params(),
        cost_estimate=cost(16),
        name="ffn_grads",
    )(table, act, d_out, hid_low, d_up)


def att_grads_kernel(
    table,
    mixed_short,
    mixed_long,
    d_att_in,
    rows_short,
    rows_long,
    d_short,
    d_query,
    d_own,
    far,
    passed,
    own,
    other,
    columns,
    d_att,
    mixed,
    rows,
    grad,
    turned,
    buffer,
    sem_i,
    sem_o,
    sem_q,
):
    short, width = rows_short.shape
    half = width // 2
    half_qkv = 3 * half
    loads = Copies(sem_i)
    first = [
        loads.start(d_att_in, d_att),
        loads.start(mixed_short, mixed.at[:short, :]),
        loads.start(mixed_long, mixed.at[short:, :]),
    ]
    second = [
        loads.start(rows_short, rows.at[:short, :]),
        loads.start(rows_long, rows.at[short:, :]),
    ]
    third = [
        loads.start(d_query, grad.at[short:, :width]),
        loads.start(d_short, grad.at[:short, :]),
    ]
    total = d_own[...].astype(F32) + far[0].astype(F32) + passed[...].astype(F32)
    grad[short:, width:] = total.astype(BF16)
    stores, done = Copies(sem_o), []

    def flush(lanes):
        done.append(stores.start(buffer.at[0, :, :, lanes], own.at[:, :, lanes]))
        done.append(stores.start(buffer.at[1, :, :, lanes], other.at[:, :, lanes]))

    wait_all(first)
    result = dot_lt(mixed[...], d_att[...]).astype(BF16)
    for part in range(2):
        put_rows(table, result[:, part * half : (part + 1) * half], buffer, part, slice(0, half))
    flush(slice(0, half))
    wait_all(second)
    turned[...] = rows[...].T
    wait_all(third)
    for step in range(3):
        lanes = slice(step * width, (step + 1) * width)
        piece = grad[:, lanes]
        columns[:, lanes] = jnp.sum(piece.astype(F32), axis=0, keepdims=True)
        result = dot(turned[...], piece).astype(BF16)
        for place in range(0, width, half):
            part, start = divmod(step * width + place, half_qkv)
            put_rows(
                table, result[:, place : place + half], buffer, part, slice(half + start, half + start + half)
            )
            far_part = jnp.bitwise_xor(table[2 * buffer.shape[1]], part)
            lanes_out = slice(half + start, half + start + half)
            index = 2 * step + place // half
            for which, target in enumerate((own, other)):

                @pl.when(far_part == which)
                def _(which=which, target=target, lanes_out=lanes_out, index=index):
                    pltpu.make_async_copy(
                        buffer.at[which, :, :, lanes_out], target.at[:, :, lanes_out], sem_q.at[index]
                    ).start()

    for index in range(6):
        part, start = divmod(index * half, half_qkv)
        lanes_out = slice(half + start, half + start + half)
        pltpu.make_async_copy(buffer.at[0, :, :, lanes_out], own.at[:, :, lanes_out], sem_q.at[index]).wait()
    wait_all(done)


def att_grads(
    table, chips, mixed_short, mixed_long, d_att, rows_short, rows_long, d_short, d_query, d_own, far, passed
):
    short, width = rows_short.shape
    rows = short + rows_long.shape[0]
    block = width // chips
    cols = 2 * width
    return pl.pallas_call(
        att_grads_kernel,
        out_shape=[sds((chips, block, cols), BF16)] * 2 + [sds((1, 3 * width), F32)],
        in_specs=[SMEM] + [ANY] * 7 + [VMEM] * 3,
        out_specs=[ANY, ANY, VMEM],
        scratch_shapes=[
            pltpu.VMEM((rows, width), BF16),
            pltpu.VMEM((rows, width), BF16),
            pltpu.VMEM((rows, width), BF16),
            pltpu.VMEM((rows, 3 * width), BF16),
            pltpu.VMEM((width, rows), BF16),
            pltpu.VMEM((2, chips, block, cols), BF16),
            pltpu.SemaphoreType.DMA((7,)),
            pltpu.SemaphoreType.DMA((2,)),
            pltpu.SemaphoreType.DMA((6,)),
        ],
        compiler_params=params(),
        cost_estimate=cost(12),
        name="att_grads",
    )(table, mixed_short, mixed_long, d_att, rows_short, rows_long, d_short, d_query, d_own, far, passed)


def input_grad_kernel(start, table, d_short, d_query, d_own, far, passed, d_first, *rest):
    *weights_in, out_short, out_long, weight, grad, first, out, sems = rest
    copies = Copies(sems)
    short, width = d_short.shape[0], out_short.shape[1]
    loads = []
    if len(weights_in) > 1:
        staged = load_staged(copies, table, weights_in, 0, 3 * width // 2, weight)
    for part in range(3):
        lanes = slice(part * width, (part + 1) * width)
        loads.append([copies.start(d_short.at[:, lanes], grad.at[:short, lanes])])
        if part == 0:
            loads[0].append(copies.start(d_query, grad.at[short:, lanes]))
        if len(weights_in) == 1:
            here = slice(start + part * width, start + (part + 1) * width)
            loads[part].append(copies.start(weights_in[0].at[:, here], weight.at[:, lanes]))
        elif part == 0:
            loads[0] += staged
        if part == 0:
            adding = copies.start(d_first, first)
    total = d_own[...].astype(F32) + far[0].astype(F32) + passed[...].astype(F32)
    grad[short:, width:] = total.astype(BF16)
    done = []
    for part in range(3):
        wait_all(loads[part])
        span = slice(part * width, (part + 1) * width)
        for step in range(width // 256):
            lanes = slice(step * 256, step * 256 + 256)
            total = dot_rt(grad[:, span], weight[lanes, span])
            if part == 0 and step == 0:
                adding.wait()
            if part < 2:
                first[:, lanes] = first[:, lanes] + total
                continue
            out[:, lanes] = (first[:, lanes] + total).astype(out.dtype)
            done.append(copies.start(out.at[:short, lanes], out_short.at[:, lanes]))
            done.append(copies.start(out.at[short:, lanes], out_long.at[:, lanes]))
    wait_all(done)


def input_grad(table, d_short, d_query, d_own, far, passed, d_first, weights, start, dtype):
    rows, width = d_first.shape
    short = d_short.shape[0]
    return pl.pallas_call(
        functools.partial(input_grad_kernel, start),
        out_shape=[sds((short, width), dtype), sds((rows - short, width), dtype)],
        in_specs=[SMEM, ANY, ANY, VMEM, VMEM, VMEM, ANY] + [ANY] * len(weights),
        out_specs=[ANY] * 2,
        scratch_shapes=[
            pltpu.VMEM((width, 3 * width), BF16),
            pltpu.VMEM((rows, 3 * width), BF16),
            pltpu.VMEM((rows, width), F32),
            pltpu.VMEM((rows, width), dtype),
            pltpu.SemaphoreType.DMA((56,)),
        ],
        compiler_params=params(),
        cost_estimate=cost(10),
        name="input_grad",
    )(table, d_short, d_query, d_own, far, passed, d_first, *weights)


def short_backward_kernel(qkv, mixed, d_mixed, raised, inverse, gate, d_qkv, gate_sum):
    low, high = head_masks()
    ones = jnp.concatenate([low, high], axis=0)
    width = mixed.shape[1]
    for pair in range(HEADS // 2):
        lanes = slice(pair * 128, pair * 128 + 128)
        query = qkv[:, lanes] * 0.125
        keys = spread(qkv[:, width + pair * 128 : width + pair * 128 + 128], low, high)
        values = spread(qkv[:, 2 * width + pair * 128 : 2 * width + pair * 128 + 128], low, high)
        grad = d_mixed[:, lanes].astype(F32)
        out = mixed[:, lanes].astype(F32)
        scaled = grad * inverse[:, lanes]
        gate_sum[0, :, lanes] = jnp.sum(grad * out, axis=0, keepdims=True)
        pulled = (scaled * gate[0, :, lanes]).astype(BF16)
        inner = (scaled * out).astype(BF16)
        prob = raised[0, pair]
        bent = dot_rt(jnp.concatenate([pulled, inner], axis=1), jnp.concatenate([values, -ones], axis=1))
        score = (prob.astype(F32) * bent).astype(BF16)
        d_qkv[:, lanes] = (dot(score, keys) * 0.125).astype(BF16)
        turned = dot_lt(query, score)
        turned = jnp.concatenate([turned[:HEAD, :BLOCK], turned[HEAD:, BLOCK:]], axis=0)
        d_qkv[:, width + pair * 128 : width + pair * 128 + 128] = turned.T.astype(BF16)
        turned = dot_lt(pulled, prob)
        turned = jnp.concatenate([turned[:HEAD, :BLOCK], turned[HEAD:, BLOCK:]], axis=0)
        d_qkv[:, 2 * width + pair * 128 : 2 * width + pair * 128 + 128] = turned.T.astype(BF16)


def short_backward(qkv, mixed, d_mixed, raised, inverse, gate):
    rows, width = mixed.shape
    count = rows // BLOCK
    pairs = HEADS // 2
    narrow = pl.BlockSpec((BLOCK, width), lambda i: (i, 0))
    wide = pl.BlockSpec((BLOCK, 3 * width), lambda i: (i, 0))
    vector = pl.BlockSpec((1, 1, width), lambda i: (i, 0, 0))
    return pl.pallas_call(
        short_backward_kernel,
        grid=(count,),
        out_shape=[sds((rows, 3 * width), BF16), sds((count, 1, width), F32)],
        in_specs=[
            wide,
            narrow,
            narrow,
            pl.BlockSpec((1, pairs, BLOCK, 2 * BLOCK), lambda i: (i, 0, 0, 0)),
            narrow,
            vector,
        ],
        out_specs=[wide, vector],
        compiler_params=params(),
        cost_estimate=cost(11.6),
        name="short_backward",
    )(qkv, mixed, d_mixed, raised, inverse, gate)


def long_backward_kernel(blocks, queries, mixed, d_mixed, raised, inverse, parts, gate, *rest):
    sources, (d_query, d_own, d_near, d_core, gate_sum) = rest[:blocks], rest[blocks:]
    low, high = head_masks()
    ones = jnp.concatenate([low, high], axis=0)
    width = mixed.shape[1]
    for pair in range(HEADS // 2):
        lanes = slice(pair * 128, pair * 128 + 128)
        query = queries[:, lanes] * 0.125
        grad = d_mixed[:, lanes].astype(F32)
        out = mixed[:, lanes].astype(F32)
        scaled = grad * inverse[:, lanes]
        inner = (scaled * out).astype(BF16)
        total = 0.0
        for index in range(blocks):
            source = sources[index]
            keys = spread(source[:, lanes], low, high)
            values = spread(source[:, width + pair * 128 : width + pair * 128 + 128], low, high)
            strength = gate[index : index + 1, lanes]
            pulled = (scaled * strength).astype(BF16)
            prob = raised[pair, index]
            bent = dot_rt(jnp.concatenate([pulled, inner], axis=1), jnp.concatenate([values, -ones], axis=1))
            score = (prob.astype(F32) * bent).astype(BF16)
            total = total + dot(score, keys)
            gate_sum[index : index + 1, lanes] = strength * jnp.sum(
                grad * parts[index, :, lanes].astype(F32), axis=0, keepdims=True
            )
            target = (d_own, d_core.at[0], d_near, d_core.at[1])[index]
            turned = dot_lt(query, score)
            turned = jnp.concatenate([turned[:HEAD, :BLOCK], turned[HEAD:, BLOCK:]], axis=0)
            target[:, lanes] = turned.T.astype(BF16)
            turned = dot_lt(pulled, prob)
            turned = jnp.concatenate([turned[:HEAD, :BLOCK], turned[HEAD:, BLOCK:]], axis=0)
            target[:, width + pair * 128 : width + pair * 128 + 128] = turned.T.astype(BF16)
        d_query[:, lanes] = (total * 0.125).astype(BF16)


def long_backward(queries, mixed, d_mixed, raised, inverse, parts, gate, sources):
    rows, width = mixed.shape
    blocks = len(sources)
    return pl.pallas_call(
        functools.partial(long_backward_kernel, blocks),
        out_shape=[
            sds((rows, width), BF16),
            sds((rows, 2 * width), BF16),
            sds((rows, 2 * width), BF16),
            sds((2, rows, 2 * width), BF16),
            sds((blocks, width), F32),
        ],
        in_specs=[VMEM] * (7 + blocks),
        out_specs=[VMEM] * 5,
        compiler_params=params(),
        cost_estimate=cost(8.7),
        name="long_backward",
    )(queries, mixed, d_mixed, raised, inverse, parts, gate, *sources)


class Source:
    def __init__(self, rows, packed, pieces, starts, qkv_start):
        self.rows, self.packed, self.pieces, self.starts, self.qkv_start = rows, packed, pieces, starts, qkv_start

    def qkv(self):
        return self.pieces if self.pieces else (self.packed,)


def on_device(
    plan,
    short_tokens,
    long_tokens,
    short_cotangent,
    long_cotangent,
    qkv_weight,
    out_weight,
    up_weight,
    down_weight,
    vectors,
    up_bias,
    mask_logit,
    short_noise,
    gate_noise,
    block_mask,
    block_order,
):
    shorts, block_rows, width = short_tokens.shape
    blocks = lax.axis_size("seq")
    place = lax.axis_index("seq")
    device = lax.axis_index("dp") * plan.seq + place
    layers = qkv_weight.shape[0]
    inner = up_weight.shape[2]
    own_rows = qkv_weight.shape[1]
    short_rows = shorts * block_rows
    half = width // 2
    half_up = inner // 2
    core = place % 2
    table = plan.tables()
    chips = plan.chips

    per_row = inner // width

    def whole(array):
        return lax.all_gather(array, AXES, axis=0, tiled=True)

    def packed(layer):
        up = up_weight[layer].reshape(own_rows, plan.devices, per_row, own_rows)
        up = up.transpose(0, 2, 1, 3).reshape(own_rows, inner)
        down = down_weight[layer].reshape(per_row, own_rows, width).transpose(1, 0, 2)
        return [out_weight[layer], up, down.reshape(own_rows, inner)]

    def small(layer):
        biases = up_bias[layer].reshape(per_row, own_rows).T
        return jnp.concatenate(
            [vectors[layer], biases, jnp.zeros((own_rows, SMALL - 8 - per_row), BF16)], axis=1
        )

    smalls = [small(layer) for layer in range(layers)]
    sources = []
    for layer in range(layers):
        parts = packed(layer)
        if not plan.staged:
            parts = parts + [qkv_weight[layer]] + (smalls if layer == 0 else [])
        rows = jnp.concatenate(parts, axis=1)
        pieces, qkv_start = (), width + 2 * inner
        if plan.staged:
            qkv_start = None
            sides = [qkv_weight[layer][:, : 3 * half], qkv_weight[layer][:, 3 * half :]]
            if layer == 0:
                sides = [jnp.concatenate([side, extra], axis=1) for side, extra in zip(sides, smalls)]
                earlier = [rows]
            else:
                earlier = [sources[-1].pieces[1], rows]
            pieces = gather(plan, *[after(side, *earlier) for side in sides], core)
        if layer > 0:
            rows = after(rows, sources[-1].packed, *pieces[:1])
        sources.append(Source(rows, whole(rows), pieces, (0, width, width + inner), qkv_start))

    block_ids = jnp.arange(blocks, dtype=jnp.int32)
    near_ids = block_ids ^ place
    placed_ids = block_order[0]
    own_block = jnp.sum(jnp.where(block_ids == place, placed_ids, 0))
    near_int = (near_ids[:, None] == block_ids[None, :]).astype(jnp.int32)
    near_true = jnp.sum(near_int * placed_ids[None, :], axis=1)
    own_hot = (block_ids == own_block).astype(F32)
    near_hot_int = (near_true[:, None] == block_ids[None, :]).astype(jnp.int32)
    near_hot = near_hot_int.astype(F32)
    mask_row = jnp.sum(block_mask[0] * (block_ids == own_block).astype(jnp.int32)[:, None], axis=0)
    opened = jnp.maximum(
        jnp.sum(near_hot_int * mask_row[None, :], axis=1), (block_ids == 0).astype(jnp.int32)
    )
    first_hot = (block_ids == 0).astype(F32)
    corner = first_hot[:, None] * first_hot[None, :]
    highest = lax.Precision.HIGHEST
    logit_near = jnp.einsum(
        "lhij,i,sj->lsh", mask_logit + gate_noise[:, 0], own_hot, near_hot, precision=highest
    )
    gate_long = jax.nn.sigmoid(logit_near)
    gate_short = jax.nn.sigmoid(mask_logit[:, None, :, 0, 0] + short_noise)
    lanes_long = jnp.repeat(gate_long, HEAD, axis=2)
    lanes_short = jnp.repeat(gate_short, HEAD, axis=2)[:, :, None, :]
    head_hot = (jnp.arange(width)[:, None] // HEAD == jnp.arange(HEADS)[None, :]).astype(F32)

    def swap_core(value):
        return lax.ppermute(value, "seq", [(i, i ^ 1) for i in range(blocks)])

    def swap_pair(value):
        return lax.ppermute(value, "seq", [(i, i ^ 2) for i in range(blocks)])

    rows_low = (short_tokens.reshape(short_rows, width), long_tokens[0])
    rows_wide = rows_low
    saved = []
    for layer in range(layers):
        source = sources[layer]
        vec = None if layer == 0 else vecs[layer]
        qkv_short, query_long, kv, *got = project(table, *rows_low, vec, layers, source.qkv(), source.qkv_start)
        if layer == 0:
            vecs = [got[0][which] for which in range(layers)]
            vec = vecs[0]
        kv_core = swap_core(kv)
        kv_pair = swap_pair(kv)
        mixed_short, raised_short, inverse_short = short_forward(qkv_short, lanes_short[layer])
        kv_pair = after(kv_pair, mixed_short)
        key_values = (kv, kv_core, kv_pair, swap_core(kv_pair))
        mixed_long, raised_long, inverse_long, parts = long_forward(
            opened, query_long, lanes_long[layer], key_values
        )
        *y, hid_low, unit1, scale1, unit2, scale2, act, slope = mlp_forward(
            layer + 1 < layers, *rows_wide, mixed_short, mixed_long, vec, inner, source
        )
        saved.append(
            (
                rows_low,
                qkv_short,
                query_long,
                key_values,
                mixed_short,
                raised_short,
                inverse_short,
                mixed_long,
                raised_long,
                inverse_long,
                parts,
                vec,
                hid_low,
                unit1,
                scale1,
                unit2,
                scale2,
                act,
                slope,
            )
        )
        rows_low, rows_wide = y[2:], y[:2]
    outputs = rows_low

    grad = (short_cotangent.reshape(short_rows, width), long_cotangent[0])
    kept = []
    terms = []
    upper = None
    staging = plan.staged
    for layer in reversed(range(layers)):
        last = layer == 0
        source = sources[layer]
        (
            rows_low,
            qkv_short,
            query_long,
            key_values,
            mixed_short,
            raised_short,
            inverse_short,
            mixed_long,
            raised_long,
            inverse_long,
            parts,
            vec,
            hid_low,
            unit1,
            scale1,
            unit2,
            scale2,
            act,
            slope,
        ) = saved[layer]
        second, d_out, sums_ffn, sums_up, d_up = ffn_backward(grad, unit2, scale2, vec, slope, source)
        if upper is not None:
            if staging:
                ffn_upper.wait(d_out)
                ffn_upper.first()
                upper[2] = after(upper[2], ffn_upper.operand, d_out)
            *att, columns = att_grads(table, chips, *upper)
            terms[-1][0] = columns
            if staging:
                att_upper = Reduce(plan, *att)
                ffn_upper.wait(att[0])
                ffn_upper.line()
                d_out = after(d_out, *att, *ffn_upper.operand)
            kept[-1].append(att_upper if staging else att)
        ffn = ffn_grads(table, chips, act, d_out, hid_low, d_up)
        second = after(second, *ffn)
        if staging:
            if upper is not None:
                att_upper.wait(ffn[0])
                att_upper.second()
                second = after(second, att_upper.operand)
            ffn_sum = Reduce(plan, *ffn)
        d_first, d_att, d_mixed_short, d_mixed_long, sums_mid = mid_backward(
            second, d_up, unit1, scale1, vec, source, short_rows
        )
        if staging and upper is not None:
            att_upper.wait(d_att)
            att_upper.first()
            d_mixed_long = after(d_mixed_long, att_upper.operand, *ffn_upper.pending)
        d_query, d_own, d_near, d_core, gate_sum_long = long_backward(
            query_long, mixed_long, d_mixed_long, raised_long, inverse_long, parts, lanes_long[layer], key_values
        )
        far = swap_core(d_core)
        away = (d_near.astype(F32) + far[1].astype(F32)).astype(BF16)
        passed = swap_pair(away)
        if staging:
            ffn_sum.wait(d_query, away)
            ffn_sum.second(passed)
            d_mixed_short = after(d_mixed_short, ffn_sum.operand)
            if upper is not None:
                att_upper.wait(d_query)
                att_upper.line()
                d_mixed_short = after(d_mixed_short, *att_upper.operand)
        d_short, gate_sum_short = short_backward(
            qkv_short, mixed_short, d_mixed_short, raised_short, inverse_short, lanes_short[layer]
        )
        had_upper = upper is not None
        upper = [mixed_short, mixed_long, d_att, *rows_low, d_short, d_query, d_own, far, passed]
        kept.append([ffn_sum if staging else ffn])
        if last:
            *att, columns = att_grads(table, chips, *upper)
            d_first = after(d_first, *att)
            if staging:
                att_sum = Reduce(plan, *att)
                ffn_sum.wait(att[0])
                ffn_sum.first()
                d_first = after(d_first, ffn_sum.operand)
                if had_upper:
                    d_first = after(d_first, *att_upper.pending)
            kept[-1].append(att_sum if staging else att)
        grad = input_grad(
            table,
            d_short,
            d_query,
            d_own,
            far,
            passed,
            d_first,
            source.qkv(),
            source.qkv_start,
            BF16 if last else F32,
        )
        if staging:
            ffn_upper = ffn_sum
            if last:
                ffn_sum.wait(grad[0])
                ffn_sum.line()
                att_sum.wait(grad[0])
                att_sum.second()
        heads = jnp.dot(
            jnp.concatenate([gate_sum_short[:, 0], gate_sum_long]), head_hot, precision=highest
        )
        short_term = jnp.sum(heads[:shorts] * (1.0 - gate_short[layer]), axis=0)
        long_term = heads[shorts:] * (1.0 - gate_long[layer])
        logit_term = (
            jnp.einsum("sh,i,sj->hij", long_term, own_hot, near_hot, precision=highest)
            + short_term[:, None, None] * corner[None]
        )
        terms.append([columns if last else None, sums_mid[2:5], sums_ffn[5:8], sums_up, logit_term])
    kept, terms = kept[::-1], terms[::-1]

    packed_sums = jnp.concatenate(
        [
            jnp.concatenate(
                [
                    rows
                    for columns, mid, ffn, _, _ in terms
                    for rows in (columns[:, :width], columns[:, 2 * width :], mid, ffn)
                ]
            ).reshape(-1, 128),
            jnp.concatenate([term[3] for term in terms]).reshape(-1, 128),
            jnp.stack([term[4] for term in terms]).reshape(-1, 128),
        ]
    )
    count = packed_sums.shape[0]
    packed_sums = jnp.pad(packed_sums, ((0, -count % 8), (0, 0)))
    if staging:
        ffn_sum, att_sum = kept[0]
        sums = Butterfly(plan, packed_sums)
        sums.step()
        sums.step(ffn_sum.operand, att_sum.operand)
        att_sum.first()
        sums.step(att_sum.operand)
        att_sum.wait(*ffn_sum.pending)
        att_sum.line()
        sums.step(*att_sum.operand)
        sums.step(*ffn_sum.pending)
        packed_sums = sums.finish()
    else:
        packed_sums = lax.psum(packed_sums, AXES)
    edge = layers * 8 * width // 128
    more = edge + layers * inner // 128
    vectors_all = packed_sums[:edge].reshape(layers, 8, width)
    vectors_grad = lax.dynamic_slice_in_dim(vectors_all, device * own_rows, own_rows, 2).transpose(0, 2, 1)
    bias_all = packed_sums[edge:more].reshape(layers, per_row, width)
    up_bias_grad = lax.dynamic_slice_in_dim(bias_all, device * own_rows, own_rows, 2).reshape(layers, -1)
    logit_grad = packed_sums[more:count].reshape(mask_logit.shape)

    def scattered(sides):
        rows = jnp.concatenate([side.reshape(width, side.shape[-1]) for side in sides], axis=1)
        rows = lax.psum_scatter(rows, AXES, scatter_dimension=0, tiled=True).astype(F32)
        count = rows.shape[1] // 2
        return rows[:, :count], rows[:, count:]

    def owned(total):
        part = [lax.dynamic_slice_in_dim(total, which * own_rows, own_rows, 0) for which in (core, 1 - core)]
        mine, got = part[0], send(part[1], plan.cores)
        return jnp.where(core == 0, mine, got), jnp.where(core == 0, got, mine)

    qkv_grad, out_grad, up_grad, down_grad = [], [], [], []
    for layer in range(layers):
        ffn, att = kept[layer]
        if staging:
            ffn, att = ffn.finish(), att.finish()
            if layer > 0:
                att = after(att, grad[0], *kept[0][0].operand)
            ffn, att = owned(ffn), owned(att)
            if layer > 0:
                begun = (grad[0], *kept[0][0].operand)
                ffn = after(ffn[0], *begun), after(ffn[1], *begun)
        else:
            ffn, att = scattered(ffn), scattered(att)
        span = per_row * half
        down = [side[:, :span].reshape(own_rows, per_row, half) for side in ffn]
        down = jnp.concatenate(down, axis=2).transpose(1, 0, 2)
        down_grad.append(down.reshape(per_row * own_rows, width))
        up = jnp.concatenate([side[:, span:] for side in ffn], axis=1)
        up = up.reshape(own_rows, per_row, plan.devices, own_rows).transpose(0, 2, 1, 3)
        up_grad.append(up.reshape(own_rows, inner))
        out_grad.append(jnp.concatenate([side[:, :half] for side in att], axis=1))
        qkv_grad.append(jnp.concatenate([side[:, half:] for side in att], axis=1))
    return (
        outputs[0].reshape(shorts, block_rows, width),
        outputs[1][None],
        grad[0].reshape(shorts, block_rows, width),
        grad[1][None],
        jnp.stack(qkv_grad),
        jnp.stack(out_grad),
        jnp.stack(up_grad),
        jnp.stack(down_grad),
        vectors_grad,
        up_bias_grad,
        logit_grad,
    )


def solution(mesh):
    split = ("dp", "seq")
    in_specs = (
        P(split, None, None),
        P("dp", "seq", None),
        P(split, None, None),
        P("dp", "seq", None),
        P(None, split, None),
        P(None, split, None),
        P(None, split, None),
        P(None, split, None),
        P(None, split, None),
        P(None, split),
        P(),
        P(None, split, None),
        P(None, "dp", None, None, None),
        P("dp", None, None),
        P("dp", None),
    )
    out_specs = (
        P(split, None, None),
        P("dp", "seq", None),
        P(split, None, None),
        P("dp", "seq", None),
        P(None, split, None),
        P(None, split, None),
        P(None, split, None),
        P(None, split, None),
        P(None, split, None),
        P(None, split),
        P(),
    )

    def build(*arrays):
        plan = Plan(mesh, arrays[4].shape[1])
        return jax.shard_map(
            functools.partial(on_device, plan),
            mesh=mesh,
            in_specs=in_specs,
            out_specs=out_specs,
            check_vma=False,
        )(*arrays)

    return build
```
